32 devices in a mesh: dp: 4 (over y, x), fsdp: 8 (over z, core).
Axes of the slice: x: 2, y: 2, z: 4, core: 2. Of those that a mesh axis runs over, the one named last changes fastest.
Arguments:
- tokens: bfloat16 [32768, 768], P(('dp', 'fsdp')), may hold values from -6 to 6
- doc_ids: int32 [32, 1024], P(('dp', 'fsdp')), may hold values from 0 to 5, never falling along the last dimension, each value on 1 to 512 neighbouring positions
- cotangent: bfloat16 [32768, 768], P(('dp', 'fsdp')), may hold values from -6 to 6
- first_gain: bfloat16 [768], P(('dp', 'fsdp')), may hold values from 0.099609375 to 1.8984375
- first_offset: bfloat16 [768], P(('dp', 'fsdp')), may hold values from -1.75 to 1.75
- qkv_weight: bfloat16 [768, 2304], P(('dp', 'fsdp')), may hold values from -0.21875 to 0.21875
- query_bias: bfloat16 [768], P(('dp', 'fsdp')), may hold values from -3 to 3
- value_bias: bfloat16 [768], P(('dp', 'fsdp')), may hold values from -3 to 3
- out_weight: bfloat16 [768, 768], P(('dp', 'fsdp')), may hold values from -5 to 5
- out_bias: bfloat16 [768], P(('dp', 'fsdp')), may hold values from -6 to 6
- second_gain: bfloat16 [768], P(('dp', 'fsdp')), may hold values from 0.099609375 to 1.8984375
- second_offset: bfloat16 [768], P(('dp', 'fsdp')), may hold values from -1.75 to 1.75
- up_weight: bfloat16 [768, 3072], P(('dp', 'fsdp')), may hold values from -0.21875 to 0.21875
- up_bias: bfloat16 [3072], P(('dp', 'fsdp')), may hold values from -3 to 3
- down_weight: bfloat16 [3072, 768], P(('dp', 'fsdp')), may hold values from -0.625 to 0.625
- down_bias: bfloat16 [768], P(('dp', 'fsdp')), may hold values from -6 to 6
Outputs:
- layer_out: bfloat16 [32768, 768], P(('dp', 'fsdp'))
- grad_tokens: float32 [32768, 768], P(('dp', 'fsdp'))
- grad_first_gain: float32 [768], P(('dp', 'fsdp'))
- grad_first_offset: float32 [768], P(('dp', 'fsdp'))
- grad_qkv_weight: float32 [768, 2304], P(('dp', 'fsdp'))
- grad_query_bias: float32 [768], P(('dp', 'fsdp'))
- grad_value_bias: float32 [768], P(('dp', 'fsdp'))
- grad_out_weight: float32 [768, 768], P(('dp', 'fsdp'))
- grad_out_bias: float32 [768], P(('dp', 'fsdp'))
- grad_second_gain: float32 [768], P(('dp', 'fsdp'))
- grad_second_offset: float32 [768], P(('dp', 'fsdp'))
- grad_up_weight: float32 [768, 3072], P(('dp', 'fsdp'))
- grad_up_bias: float32 [3072], P(('dp', 'fsdp'))
- grad_down_weight: float32 [3072, 768], P(('dp', 'fsdp'))
- grad_down_bias: float32 [768], P(('dp', 'fsdp'))
The draws below stay inside these ranges and needn't reach their ends.
Inputs may be any that keep to these rules, and one draw needn't show every extreme that they name: `doc_ids`: in each packed row document numbers never fall, every document 0 to 5 has 1 to 512 tokens and one has exactly 512.
All inputs are finite; a program needn't handle non-finite values.
Results may differ from the reference program's by a relative error of at most 0.013.
Values may be sent and summed in bfloat16 or wider, within the bound.
A program may use at most 256 MiB of HBM per device.

```python
import math
import jax
import jax.numpy as jnp
import numpy as np
from jax import lax

D = 768
HEADS = 12
HEAD_DIM = 64
FF = 3072
SEQ = 1024
DOCS = 6
MOST_DOC = 512
ROWS = 32
TOKENS = 32768


def strengthened(drawn, stream_key, source, target, shards_of, factor):
    def block_of(dim):
        return (jnp.arange(drawn.shape[dim]) // (drawn.shape[dim] // shards_of)).reshape((-1,) + (1,) * (drawn.ndim - 1 - dim))

    near = jax.random.permutation(stream_key, shards_of)[block_of(target)]
    far = (block_of(target) + shards_of // 2) % shards_of
    return jnp.where((block_of(source) == near) | (block_of(source) == far), factor * drawn, drawn)


def levels(own_key, shape, cuts, low, largest):
    def one(dim, parts):
        draws = jax.random.uniform(jax.random.fold_in(jax.random.fold_in(own_key, 6), dim), (parts,), jnp.float32, low / len(cuts), largest / len(cuts))
        return jnp.repeat(jnp.exp(draws), shape[dim] // parts).reshape((-1,) + (1,) * (len(shape) - dim - 1))

    gain = one(*cuts[0])
    for cut in cuts[1:]:
        gain = gain * one(*cut)
    return gain


def profile(number_of, total, reach, lean):
    loads = [(1 << 20) // math.isqrt(grade ** lean) + 1 for grade in range(2, number_of + 1)]
    surplus, counts = total - reach - (number_of - 1), [1] * (number_of - 1)
    while surplus > 0:
        movable = [i for i in range(number_of - 1) if counts[i] < reach]
        mass, remaining = sum([loads[i] for i in movable]), surplus
        for i in movable:
            more = min(reach - counts[i], max(1, remaining * loads[i] // mass), surplus)
            counts[i] = counts[i] + more
            surplus = surplus - more
    return np.array([reach] + counts)


def ragged_sizes(own_key, amount, total, bound, slope):
    if amount == 2:
        one = jax.random.randint(own_key, (), max(1, total - bound), min(bound, total - 1) + 1)
        return jnp.stack([one, total - one])
    tallies = jnp.asarray(profile(amount, total, bound, slope), jnp.int32)
    pairs = (amount - 1) // 2
    donor, taker = tallies[1:1 + 2 * pairs:2], tallies[2:2 + 2 * pairs:2]
    room = jnp.minimum(donor - 1, bound - taker)
    moved = jax.random.randint(jax.random.fold_in(own_key, 1), (pairs,), 0, 1 << 20) % (room + 1)
    tallies = tallies.at[1:1 + 2 * pairs:2].set(donor - moved).at[2:2 + 2 * pairs:2].set(taker + moved)
    return tallies[jax.random.permutation(jax.random.fold_in(own_key, 2), amount)]


def noise(stream_key, shape, width, bound, pieces=(), kind=jnp.bfloat16):
    array = jax.random.normal(stream_key, shape, jnp.float32) * width
    if len(pieces) > 0:
        array = levels(stream_key, shape, pieces, -0.22, 0.18) * array
    return jnp.clip(array, min=-bound, max=bound).astype(kind)


def heavy_noise(rng, extent, deviation, most, pieces, heavy, kind=jnp.bfloat16):
    array = deviation * jax.random.normal(rng, extent, jnp.float32)
    if pieces:
        array = array * levels(rng, extent, pieces, -0.22, 0.18)
    return jnp.clip(strengthened(array, jax.random.fold_in(rng, 3), *heavy), -most, most).astype(kind)


def setup_inputs(seed: int = 0) -> dict:
    key_of = jax.random.split(jax.random.key(seed), 17)
    return {
        "tokens": noise(key_of[0], (TOKENS, D), 1.0, 6.0, ((0, 32),)),
        "doc_ids": jax.vmap(lambda own: jnp.searchsorted(jnp.cumsum(ragged_sizes(own, DOCS, SEQ, MOST_DOC, 1)), jnp.arange(SEQ), side="right"))(jax.random.split(key_of[1], ROWS)).reshape((ROWS, SEQ)).astype(jnp.int32),
        "cotangent": heavy_noise(key_of[2], (TOKENS, D), 1.0, 6.0, ((0, 32),), (0, 1, 32, 2.75)),
        "first_gain": jnp.clip(1.0 + 0.18 * jax.random.normal(key_of[3], (D,), jnp.float32), 0.099609375, 1.8984375).astype(jnp.bfloat16),
        "first_offset": noise(key_of[4], (D,), 0.3, 1.75, ((0, 32),)),
        "qkv_weight": noise(key_of[5], (D, 3 * D), D ** -0.5, 0.21875, ((0, 32),)),
        "query_bias": noise(key_of[6], (D,), 0.5, 3.0, ((0, 32),)),
        "value_bias": noise(key_of[7], (D,), 0.5, 3.0, ((0, 32),)),
        "out_weight": noise(key_of[8], (D, D), (24 * D ** -0.5), 5.0, ((0, 32),)),
        "out_bias": noise(key_of[9], (D,), 1.0, 6.0, ((0, 32),)),
        "second_gain": jnp.clip(1.0 + 0.18 * jax.random.normal(key_of[10], (D,), jnp.float32), 0.099609375, 1.8984375).astype(jnp.bfloat16),
        "second_offset": noise(key_of[11], (D,), 0.3, 1.75, ((0, 32),)),
        "up_weight": noise(key_of[12], (D, FF), D ** -0.5, 0.21875, ((0, 32),)),
        "up_bias": noise(key_of[13], (FF,), 0.5, 3.0, ((0, 32),)),
        "down_weight": noise(key_of[14], (FF, D), (6 * FF ** -0.5), 0.625, ((0, 32),)),
        "down_bias": noise(key_of[15], (D,), 1.0, 6.0, ((0, 32),)),
    }


@jax.custom_vjp
def low(v):
    return lax.optimization_barrier(v.astype(jnp.bfloat16)).astype(jnp.float32)

@jax.custom_vjp
def low_back(v):
    return v

def low_keep(v):
    return (low(v), None)

def low_pass(kept, grad):
    return (grad,)

def back_keep(v):
    return (v, None)

def back_low(kept, grad):
    return (low(grad),)
low.defvjp(low_keep, low_pass)
low_back.defvjp(back_keep, back_low)
norm_eps = 1e-05
branch_scale = 48.0 ** (-0.5)
highest = lax.Precision.HIGHEST

def layer_norm(values, gains, offsets):
    average = lax.optimization_barrier(jnp.mean(values, axis=-1, keepdims=True))
    centred = values - average
    variance = lax.optimization_barrier(jnp.mean(centred * centred, axis=-1, keepdims=True))
    return centred * lax.rsqrt(variance + norm_eps) * gains + offsets

def matmul(former, latter):
    return jnp.dot(former, latter, precision=highest)

def row_attention(queries, keys, values, documents):
    positions = jnp.arange(queries.shape[0])
    allowed = (documents[:, None] == documents[None, :]) & (positions[None, :] <= positions[:, None])
    scores = jnp.einsum('qhd,khd->hqk', queries, keys, precision=highest) * HEAD_DIM ** (-0.5)
    scores = low_back(scores)
    scores = jnp.where(allowed[None], scores, -1e+30)
    weights = low(jax.nn.softmax(scores, axis=-1))
    return jnp.einsum('hqk,khd->qhd', weights, values, precision=highest)

def forward(tokens, first_gain, first_offset, qkv_weight, query_bias, value_bias, out_weight, out_bias, second_gain, second_offset, up_weight, up_bias, down_weight, down_bias, documents):
    normed_one = low(layer_norm(tokens, first_gain, first_offset))
    projected = matmul(normed_one, qkv_weight)
    queries = low(low_back(projected[:, :D] + query_bias))
    keys = low(low_back(projected[:, D:2 * D]))
    values = low(low_back(projected[:, 2 * D:] + value_bias))
    row_shape = (-1, SEQ, HEADS, HEAD_DIM)

    def scan_step(carried, row_item):
        return (carried, jax.checkpoint(row_attention)(*row_item))
    _, attended = lax.scan(scan_step, 0, (queries.reshape(row_shape), keys.reshape(row_shape), values.reshape(row_shape), documents))
    attended = low(low_back(attended.reshape(-1, D)))
    branch = low_back(matmul(attended, out_weight) + out_bias)
    middle = tokens + branch_scale * branch
    normed_two = low(layer_norm(middle, second_gain, second_offset))
    hidden = low_back(matmul(normed_two, up_weight) + up_bias)
    active = low(jax.nn.gelu(hidden, approximate=True))
    outer = low_back(matmul(active, down_weight) + down_bias)
    return middle + branch_scale * outer

def reference(tokens, doc_ids, cotangent, first_gain, first_offset, qkv_weight, query_bias, value_bias, out_weight, out_bias, second_gain, second_offset, up_weight, up_bias, down_weight, down_bias):
    params = [p.astype(jnp.float32) for p in (first_gain, first_offset, qkv_weight, query_bias, value_bias, out_weight, out_bias, second_gain, second_offset, up_weight, up_bias, down_weight, down_bias)]
    documents = doc_ids.astype(jnp.int32)

    def whole_layer(inputs, *weights):
        return forward(inputs, *weights, documents)
    layer_out, pullback = jax.vjp(whole_layer, tokens.astype(jnp.float32), *params)
    gradients = pullback(cotangent.astype(jnp.float32))
    return (layer_out.astype(jnp.bfloat16), gradients[0], gradients[1], gradients[2], gradients[3], gradients[4], gradients[5], gradients[6], gradients[7], gradients[8], gradients[9], gradients[10], gradients[11], gradients[12], gradients[13])
```

```python
import jax
import jax.numpy as jnp
from jax import lax
from jax.experimental import pallas as pl
from jax.experimental.pallas import tpu as pltpu
from jax.sharding import PartitionSpec as P

HEADS = 12
HEAD_DIM = 64


norm_eps = 1e-05
branch_scale = 48.0 ** (-0.5)


def layer_norm(values, gains, offsets):
    average = jnp.mean(values, axis=-1, keepdims=True)
    centred = values - average
    variance = jnp.mean(centred * centred, axis=-1, keepdims=True)
    return centred * lax.rsqrt(variance + norm_eps) * gains + offsets


def scaled_norm(values, gains):
    return layer_norm(values, gains, 0.0)


def dense(former, latter):
    return jnp.dot(former, latter, preferred_element_type=jnp.float32)


def contract_rows(former, latter):
    return lax.dot_general(
        former, latter, (((0,), (0,)), ((), ())), preferred_element_type=jnp.float32
    )


def contract_cols(former, latter):
    return lax.dot_general(
        former, latter, (((1,), (1,)), ((), ())), preferred_element_type=jnp.float32
    )


def block_scores(queries, keys, documents, row_start, row_stop):
    score_scale = queries.shape[2] ** (-0.5)
    scores = (
        jnp.einsum(
            "qhd,khd->hqk",
            queries[row_start:row_stop],
            keys[:row_stop],
            preferred_element_type=jnp.float32,
        )
        * score_scale
    )
    positions = jnp.arange(row_stop)
    allowed = (documents[row_start:row_stop, None] == documents[None, :row_stop]) & (
        positions[None, :] <= positions[row_start:row_stop, None]
    )
    return jnp.where(allowed[None], scores, -1e30)


def attend_row(queries, keys, values, documents):
    seq_len = queries.shape[0]
    block_rows = min(512, seq_len)
    outputs = []
    logsums = []
    for row_start in range(0, seq_len, block_rows):
        row_stop = row_start + block_rows
        scores = block_scores(queries, keys, documents, row_start, row_stop)
        highest = jnp.max(scores, axis=-1, keepdims=True)
        raised = jnp.exp(scores - highest)
        summed = jnp.sum(raised, axis=-1, keepdims=True)
        weights = (raised / summed).astype(jnp.bfloat16)
        outputs.append(
            jnp.einsum(
                "hqk,khd->qhd", weights, values[:row_stop], preferred_element_type=jnp.float32
            )
        )
        logsums.append((highest + jnp.log(summed))[..., 0])
    return (jnp.concatenate(outputs, axis=0).astype(jnp.bfloat16), jnp.concatenate(logsums, axis=1))


def attend_row_back(queries, keys, values, documents, logsums, grad_out):
    seq_len = queries.shape[0]
    block_rows = min(512, seq_len)
    score_scale = queries.shape[2] ** (-0.5)
    query_parts = []
    grad_keys = jnp.zeros(keys.shape, jnp.float32)
    grad_values = jnp.zeros(values.shape, jnp.float32)
    for row_start in range(0, seq_len, block_rows):
        row_stop = row_start + block_rows
        scores = block_scores(queries, keys, documents, row_start, row_stop)
        probs = jnp.exp(scores - logsums[:, row_start:row_stop, None])
        incoming = grad_out[row_start:row_stop]
        grad_probs = jnp.einsum(
            "qhd,khd->hqk", incoming, values[:row_stop], preferred_element_type=jnp.float32
        )
        inner_sum = jnp.sum(probs * grad_probs, axis=-1, keepdims=True)
        grad_scores = (probs * (grad_probs - inner_sum)).astype(jnp.bfloat16)
        query_parts.append(
            jnp.einsum(
                "hqk,khd->qhd", grad_scores, keys[:row_stop], preferred_element_type=jnp.float32
            )
            * score_scale
        )
        key_term = (
            jnp.einsum(
                "hqk,qhd->khd",
                grad_scores,
                queries[row_start:row_stop],
                preferred_element_type=jnp.float32,
            )
            * score_scale
        )
        value_term = jnp.einsum(
            "hqk,qhd->khd", probs.astype(jnp.bfloat16), incoming, preferred_element_type=jnp.float32
        )
        padding = ((0, seq_len - row_stop), (0, 0), (0, 0))
        grad_keys = grad_keys + jnp.pad(key_term, padding)
        grad_values = grad_values + jnp.pad(value_term, padding)
    return (jnp.concatenate(query_parts, axis=0), grad_keys, grad_values)


MESH = pl.DeviceIdType.MESH
WIDTH = 768
HIDDEN = 3072
CHIPS = 16
CORES = 2
VMEM_LIMIT = 60 * 2**20

UNITS = (
    ("qkv", 0, 384, 384),
    ("qkv", 768, 384, 384),
    ("qkv", 1536, 384, 384),
    ("out", 0, 384, 384),
    ("up", 0, 384, 384),
    ("up", 768, 384, 384),
    ("up", 1536, 384, 384),
    ("up", 2304, 384, 384),
    ("down", 0, 384, 128),
    ("down", 128, 384, 128),
    ("down", 256, 384, 128),
)
SHARD_ROWS = {"qkv": 24, "out": 24, "up": 24, "down": 96}
COLUMNS = {"qkv": 2304, "out": 768, "up": 3072, "down": 768}
NAMES = ("qkv", "out", "up", "down")


def fits(mesh):
    return mesh.shape["dp"] == 4 and mesh.shape["fsdp"] == 8


def padded(rows):
    return -(-rows // 16) * 16


class Place:
    def __init__(self):
        self.dp = lax.axis_index("dp")
        self.fsdp = lax.axis_index("fsdp")
        self.core = lax.rem(self.fsdp, 2)
        self.z = lax.div(self.fsdp, 2)
        x = lax.rem(self.dp, 2)
        y = lax.div(self.dp, 2)
        self.dp_x = y * 2 + (1 - x)
        self.dp_y = (1 - y) * 2 + x
        self.dp_far = 3 - self.dp
        core = self.core
        self.near = self.dp_x * (1 - core) + self.dp_y * core
        self.next = self.dp_y * (1 - core) + self.dp_x * core
        self.chip = self.dp * 4 + self.z
        self.partner = (self.dp, self.z * 2 + (1 - core))
        self.at_near = (self.near, self.fsdp)
        self.at_next = (self.next, self.fsdp)

    def along_z(self, step):
        z = lax.rem(self.z + step, 4)
        return (self.dp, z * 2 + self.core)

    def greet(self):
        barrier = pltpu.get_barrier_semaphore()
        others = [self.partner, (self.dp_x, self.fsdp), (self.dp_y, self.fsdp), (self.dp_far, self.fsdp)]
        others += [self.along_z(step) for step in (1, 2, 3)]
        for other in others:
            pl.semaphore_signal(barrier, inc=1, device_id=other, device_id_type=MESH)
        pl.semaphore_wait(barrier, len(others))


def send(source, target, sems, index, device):
    copy = pltpu.make_async_remote_copy(
        src_ref=source,
        dst_ref=target,
        send_sem=sems[0].at[index],
        recv_sem=sems[1].at[index],
        device_id=device,
        device_id_type=MESH,
    )
    copy.start()
    return copy


def aligned(value, step):
    return pl.multiple_of(value, step)


class SmallSum:
    STAGES = 3

    def __init__(self, place, buffers, landed, sems):
        self.place, self.buffers, self.landed, self.sems = place, buffers, landed, sems

    @staticmethod
    def scratch():
        return [
            pltpu.VMEM((3, 16, WIDTH), jnp.float32),
            pltpu.VMEM((7, 16, WIDTH), jnp.float32),
            pltpu.SemaphoreType.DMA((7,)),
            pltpu.SemaphoreType.DMA((7,)),
        ]

    def begin(self, value):
        self.buffers[0] = value
        p = self.place
        self.copies = [send(self.buffers.at[0], self.landed.at[0], self.sems, 0, p.partner)]

    def middle(self):
        p = self.place
        self.copies[0].wait()
        self.buffers[1] = self.buffers[0] + self.landed[0]
        self.copies = [
            send(self.buffers.at[1], self.landed.at[1 + i], self.sems, 1 + i, (dp, p.fsdp))
            for i, dp in enumerate((p.dp_x, p.dp_y, p.dp_far))
        ]

    def last(self):
        p = self.place
        for copy in self.copies:
            copy.wait()
        self.buffers[2] = (self.buffers[1] + self.landed[1]) + (self.landed[2] + self.landed[3])
        self.copies = [
            send(self.buffers.at[2], self.landed.at[4 + i], self.sems, 4 + i, p.along_z(1 + i)) for i in range(3)
        ]

    def end(self):
        for copy in self.copies:
            copy.wait()
        return (self.buffers[2] + self.landed[4]) + (self.landed[5] + self.landed[6])


class GatherUnit:
    SEMS = 11

    def __init__(self, place, unit, shard, full, pair_out, pair_in, send_sems, recv_sems):
        self.place = place
        name, first, step, self.width = unit
        self.rows = SHARD_ROWS[name]
        self.shard, self.full = shard, full
        self.mine = aligned(first + step * place.core, 128)
        self.other = aligned(first + step * (1 - place.core), 128)
        self.pair_out, self.pair_in = pair_out, pair_in
        self.sems = (send_sems, recv_sems)
        self.sent = []

    def group(self, dp):
        rows = 8 * self.rows
        return self.full.at[pl.ds(aligned(dp * rows, 16), rows), pl.ds(self.mine, self.width)]

    def push(self, view, index, device):
        copy = send(view, view, self.sems, index, device)
        self.sent.append(copy)
        return copy

    def pair(self):
        self.pair_out[0 : self.rows] = self.shard[:, pl.ds(self.other, self.width)]
        if self.rows % 16:
            rest = padded(self.rows) - self.rows
            self.pair_out[self.rows :] = jnp.zeros((rest, self.width), jnp.bfloat16)
        self.pair_copy = send(self.pair_out, self.pair_in, self.sems, 0, self.place.partner)

    def along_z(self):
        p = self.place
        self.pair_copy.wait()
        own = self.shard[:, pl.ds(self.mine, self.width)].astype(jnp.float32)
        came = self.pair_in[0 : self.rows].astype(jnp.float32)
        first = p.core == 0
        block = jnp.concatenate([jnp.where(first, own, came), jnp.where(first, came, own)], axis=0)
        row = aligned(p.chip * (2 * self.rows), 16)
        view = self.full.at[pl.ds(row, 2 * self.rows), pl.ds(self.mine, self.width)]
        view[...] = block.astype(jnp.bfloat16)
        self.z_copies = [self.push(view, step, p.along_z(step)) for step in (1, 2, 3)]

    def to_near(self):
        p = self.place
        for copy in self.z_copies:
            copy.wait_recv()
        own = self.group(p.dp)
        self.near_copy = self.push(own, 4, p.at_near)
        self.next_copies = [self.push(own, 5, p.at_next)]
        self.core_copies = [self.push(own, 7, p.partner)]

    def to_next(self):
        p = self.place
        self.near_copy.wait_recv()
        came = self.group(p.near)
        self.next_copies.append(self.push(came, 6, p.at_next))
        self.core_copies.append(self.push(came, 8, p.partner))

    def to_core(self):
        p = self.place
        for copy, dp, index in zip(self.next_copies, (p.next, p.dp_far), (9, 10)):
            copy.wait_recv()
            self.core_copies.append(self.push(self.group(dp), index, p.partner))

    def arrived(self):
        for copy in self.core_copies:
            copy.wait_recv()

    def finish(self):
        for copy in self.sent:
            copy.wait_send()


class ScatterUnit:
    SEMS = 8

    def __init__(self, place, unit, partial, target, halves, from_next, from_near, from_z, pair, send_sems, recv_sems):
        self.place = place
        name, first, step, self.width = unit
        self.rows = SHARD_ROWS[name]
        self.partial, self.target = partial, target
        self.mine = aligned(first + step * place.core, 128)
        self.other = aligned(first + step * (1 - place.core), 128)
        self.halves, self.from_next, self.from_near, self.from_z, self.pair_buffer = (
            halves,
            from_next,
            from_near,
            from_z,
            pair,
        )
        self.sems = (send_sems, recv_sems)
        self.sent = []

    @staticmethod
    def scratch(unit):
        name, _, _, width = unit
        rows = SHARD_ROWS[name]
        return [
            pltpu.VMEM((32 * rows, width), jnp.bfloat16),
            pltpu.VMEM((2, 8 * rows, width), jnp.bfloat16),
            pltpu.VMEM((8 * rows, width), jnp.bfloat16),
            pltpu.VMEM((3, 2 * rows, width), jnp.bfloat16),
            pltpu.VMEM((3, rows, width), jnp.float32),
        ]

    def push(self, source, target, index, device):
        copy = send(source, target, self.sems, index, device)
        self.sent.append(copy)
        return copy

    def group(self, dp):
        rows = 8 * self.rows
        return self.halves.at[pl.ds(aligned(dp * rows, 16), rows)]

    def to_partner(self):
        source = self.partial.at[:, pl.ds(self.other, self.width)]
        self.copies = [self.push(source, self.halves, 0, self.place.partner)]

    def landed(self):
        for copy in self.copies:
            copy.wait_recv()

    def add(self, former, latter, rows):
        step = 48 if rows % 48 == 0 else 64

        def body(index, carry):
            at = pl.ds(aligned(index * step, 16), step)
            former[at] = (former[at].astype(jnp.float32) + latter(at).astype(jnp.float32)).astype(jnp.bfloat16)
            return carry

        lax.fori_loop(0, rows // step, body, 0)

    def to_next(self):
        p = self.place
        self.landed()
        self.add(self.halves, lambda at: self.partial[at, pl.ds(self.mine, self.width)], 32 * self.rows)
        self.copies = [
            self.push(self.group(dp), self.from_next.at[i], 1 + i, p.at_next)
            for i, dp in enumerate((p.next, p.dp_far))
        ]

    def to_near(self):
        p = self.place
        self.landed()
        self.add(self.group(p.near), lambda at: self.from_next[1, at], 8 * self.rows)
        self.copies = [self.push(self.group(p.near), self.from_near, 3, p.at_near)]
        self.add(self.group(p.dp), lambda at: self.from_next[0, at], 8 * self.rows)

    def along_z(self):
        p = self.place
        self.landed()
        own = self.group(p.dp)
        self.add(own, lambda at: self.from_near[at], 8 * self.rows)
        self.copies = []
        for step in (1, 2, 3):
            z = lax.rem(p.z + step, 4)
            view = own.at[pl.ds(aligned(z * (2 * self.rows), 16), 2 * self.rows)]
            self.copies.append(self.push(view, self.from_z.at[step - 1], 3 + step, p.along_z(step)))

    def to_pair(self):
        p = self.place
        self.landed()
        rows = self.rows
        own = self.halves[pl.ds(aligned(p.chip * (2 * rows), 16), 2 * rows)].astype(jnp.float32)
        came = [self.from_z[i].astype(jnp.float32) for i in range(3)]
        block = (own + came[0]) + (came[1] + came[2])
        first = p.core == 0
        self.pair_buffer[0] = jnp.where(first, block[rows:], block[:rows])
        self.pair_buffer[1] = jnp.where(first, block[:rows], block[rows:])
        self.copies = [self.push(self.pair_buffer.at[0], self.pair_buffer.at[2], 7, p.partner)]

    def store(self):
        self.landed()
        self.target[:, pl.ds(self.mine, self.width)] = self.pair_buffer[1]
        self.target[:, pl.ds(self.other, self.width)] = self.pair_buffer[2]

    def finish(self):
        for copy in self.sent:
            copy.wait_send()


def staggered(units, stages):
    for tick in range(len(units) + len(stages) - 1):
        for late in range(len(stages) - 1, -1, -1):
            index = tick - late
            if 0 <= index < len(units):
                getattr(units[index], stages[late])()


def gather_kernel(*refs):
    shards, refs = dict(zip(NAMES, refs[:4])), refs[4:]
    small, refs = refs[0], refs[1:]
    fulls, refs = dict(zip(NAMES, refs[:4])), refs[4:]
    small_out, refs = refs[0], refs[1:]
    buffers, refs = refs[: 2 * len(UNITS)], refs[2 * len(UNITS) :]
    send_sems, recv_sems, *small_refs = refs
    place = Place()
    units = [
        GatherUnit(
            place, unit, shards[unit[0]], fulls[unit[0]], buffers[2 * i], buffers[2 * i + 1], send_sems.at[i], recv_sems.at[i]
        )
        for i, unit in enumerate(UNITS)
    ]
    place.greet()
    vector = SmallSum(place, small_refs[0], small_refs[1], small_refs[2:])
    vector.begin(small[...])
    for unit in units:
        unit.pair()
    vector.middle()
    units[0].along_z()
    units[1].along_z()
    vector.last()
    count = len(units)
    stages = ("to_near", "to_next", "to_core", "arrived")
    for tick in range(count + 3):
        if 2 <= tick + 2 < count:
            units[tick + 2].along_z()
        for late, stage in enumerate(stages):
            if 0 <= tick - late < count:
                getattr(units[tick - late], stage)()
        if tick == 0:
            small_out[...] = vector.end()
    for unit in units:
        unit.finish()


def gather(shards, small):
    vmem = pl.BlockSpec(memory_space=pltpu.VMEM)
    scratch = []
    for name, _, _, width in UNITS:
        scratch += [pltpu.VMEM((padded(SHARD_ROWS[name]), width), jnp.bfloat16)] * 2
    scratch += [pltpu.SemaphoreType.DMA((len(UNITS), GatherUnit.SEMS))] * 2
    out_shape = [jax.ShapeDtypeStruct((32 * SHARD_ROWS[n], COLUMNS[n]), jnp.bfloat16) for n in NAMES]
    out_shape.append(jax.ShapeDtypeStruct((16, WIDTH), jnp.float32))
    return pl.pallas_call(
        gather_kernel,
        name="gather_weights",
        out_shape=out_shape,
        in_specs=[vmem] * 5,
        out_specs=[vmem] * 5,
        scratch_shapes=scratch + SmallSum.scratch(),
        compiler_params=pltpu.CompilerParams(collective_id=0, has_side_effects=True, vmem_limit_bytes=VMEM_LIMIT),
    )(*[shards[n] for n in NAMES], small)


SCATTER_ORDER = (8, 9, 10, 4, 5, 6, 7, 3, 0, 1, 2)


def scatter_kernel(*refs):
    partials, refs = dict(zip(NAMES, refs[:4])), refs[4:]
    small, refs = refs[0], refs[1:]
    targets, refs = dict(zip(NAMES, refs[:4])), refs[4:]
    small_out, refs = refs[0], refs[1:]
    buffers, refs = refs[: 5 * len(UNITS)], refs[5 * len(UNITS) :]
    send_sems, recv_sems, *small_refs = refs
    place = Place()
    units = []
    for i in SCATTER_ORDER:
        name = UNITS[i][0]
        units.append(
            ScatterUnit(
                place, UNITS[i], partials[name], targets[name], *buffers[5 * i : 5 * i + 5], send_sems.at[i], recv_sems.at[i]
            )
        )
    place.greet()
    vector = SmallSum(place, small_refs[0], small_refs[1], small_refs[2:])
    vector.begin(small[...])
    units[0].to_partner()
    vector.middle()
    units[1].to_partner()
    vector.last()
    count = len(units)
    stages = ("to_next", "to_near", "along_z", "to_pair", "store")
    for tick in range(count + len(stages) - 1):
        if tick + 2 < count:
            units[tick + 2].to_partner()
        for late, stage in enumerate(stages):
            if 0 <= tick - late < count:
                getattr(units[tick - late], stage)()
        if tick == 0:
            small_out[...] = vector.end()
    for unit in units:
        unit.finish()


def scatter(partials, small):
    vmem = pl.BlockSpec(memory_space=pltpu.VMEM)
    scratch = []
    for unit in UNITS:
        scratch += ScatterUnit.scratch(unit)
    scratch += [pltpu.SemaphoreType.DMA((len(UNITS), ScatterUnit.SEMS))] * 2
    out_shape = [jax.ShapeDtypeStruct((SHARD_ROWS[n], COLUMNS[n]), jnp.float32) for n in NAMES]
    out_shape.append(jax.ShapeDtypeStruct((16, WIDTH), jnp.float32))
    return pl.pallas_call(
        scatter_kernel,
        name="scatter_gradients",
        out_shape=out_shape,
        in_specs=[vmem] * 5,
        out_specs=[vmem] * 5,
        scratch_shapes=scratch + SmallSum.scratch(),
        compiler_params=pltpu.CompilerParams(collective_id=1, has_side_effects=True, vmem_limit_bytes=VMEM_LIMIT),
    )(*[partials[n] for n in NAMES], small)


def device_number():
    return lax.axis_index("dp") * 8 + lax.axis_index("fsdp")


def spread(vectors, hidden_vector):
    number = device_number()
    stacked = jnp.stack([v.astype(jnp.float32) for v in vectors])
    placed = lax.dynamic_update_slice(jnp.zeros((16, WIDTH), jnp.float32), stacked, (0, 24 * number))
    return lax.dynamic_update_slice(
        placed, hidden_vector.astype(jnp.float32)[None], (8 + number // 8, 96 * (number % 8))
    )


def own_parts(total):
    number = device_number()
    parts = lax.dynamic_slice(total[:8], (0, 24 * number), (8, 24))
    hidden_part = lax.dynamic_slice(total, (8 + number // 8, 96 * (number % 8)), (1, 96))
    return [parts[i] for i in range(8)], hidden_part[0]


def plain_device(
    tokens,
    doc_ids,
    cotangent,
    first_gain,
    first_offset,
    qkv_weight,
    query_bias,
    value_bias,
    out_weight,
    out_bias,
    second_gain,
    second_offset,
    up_weight,
    up_bias,
    down_weight,
    down_bias,
):
    attn_full = (
        lax.all_gather(first_gain, ("dp", "fsdp"), axis=0, tiled=True),
        lax.all_gather(first_offset, ("dp", "fsdp"), axis=0, tiled=True),
        lax.all_gather(qkv_weight, ("dp", "fsdp"), axis=0, tiled=True),
        lax.all_gather(query_bias, ("dp", "fsdp"), axis=0, tiled=True),
        lax.all_gather(value_bias, ("dp", "fsdp"), axis=0, tiled=True),
        lax.all_gather(out_weight, ("dp", "fsdp"), axis=0, tiled=True),
        lax.all_gather(out_bias, ("dp", "fsdp"), axis=0, tiled=True),
    )
    model_width = tokens.shape[1]
    rows_here = doc_ids.shape[0]
    seq_len = doc_ids.shape[1]
    inputs = tokens.astype(jnp.float32)
    gain_one = attn_full[0].astype(jnp.float32)
    normed_one = layer_norm(inputs, gain_one, attn_full[1].astype(jnp.float32)).astype(jnp.bfloat16)
    projected = dense(normed_one, attn_full[2])
    queries = (projected[:, :model_width] + attn_full[3].astype(jnp.float32)).astype(jnp.bfloat16)
    keys = projected[:, model_width : 2 * model_width].astype(jnp.bfloat16)
    values = (projected[:, 2 * model_width :] + attn_full[4].astype(jnp.float32)).astype(
        jnp.bfloat16
    )
    row_shape = (rows_here, seq_len, HEADS, HEAD_DIM)
    queries = queries.reshape(row_shape)
    keys = keys.reshape(row_shape)
    values = values.reshape(row_shape)
    attended, logsums = lax.map(
        lambda row_item: attend_row(*row_item), (queries, keys, values, doc_ids)
    )
    attended = attended.reshape(-1, model_width)
    branch = dense(attended, attn_full[5]) + attn_full[6].astype(jnp.float32)
    middle = inputs + branch_scale * branch
    mlp_full = (
        lax.all_gather(second_gain, ("dp", "fsdp"), axis=0, tiled=True),
        lax.all_gather(second_offset, ("dp", "fsdp"), axis=0, tiled=True),
        lax.all_gather(up_weight, ("dp", "fsdp"), axis=0, tiled=True),
        lax.all_gather(up_bias, ("dp", "fsdp"), axis=0, tiled=True),
        lax.all_gather(down_weight, ("dp", "fsdp"), axis=0, tiled=True),
        lax.all_gather(down_bias, ("dp", "fsdp"), axis=0, tiled=True),
    )
    gain_two = mlp_full[0].astype(jnp.float32)
    normed_two = layer_norm(middle, gain_two, mlp_full[1].astype(jnp.float32)).astype(jnp.bfloat16)
    hidden = dense(normed_two, mlp_full[2]) + mlp_full[3].astype(jnp.float32)
    active, gelu_back = jax.vjp(lambda pre_act: jax.nn.gelu(pre_act, approximate=True), hidden)
    active = active.astype(jnp.bfloat16)
    outer = dense(active, mlp_full[4]) + mlp_full[5].astype(jnp.float32)
    layer_out = (middle + branch_scale * outer).astype(jnp.bfloat16)
    mlp_back = (
        lax.all_gather(second_gain, ("dp", "fsdp"), axis=0, tiled=True),
        lax.all_gather(up_weight, ("dp", "fsdp"), axis=0, tiled=True),
        lax.all_gather(down_weight, ("dp", "fsdp"), axis=0, tiled=True),
    )
    seed = cotangent.astype(jnp.float32)
    grad_outer = (branch_scale * seed).astype(jnp.bfloat16)
    grad_down_bias = jnp.sum(grad_outer.astype(jnp.float32), axis=0)
    grad_down_weight = contract_rows(active, grad_outer)
    grad_active = contract_cols(grad_outer, mlp_back[2])
    grad_hidden = gelu_back(grad_active)[0].astype(jnp.bfloat16)
    grad_up_bias = jnp.sum(grad_hidden.astype(jnp.float32), axis=0)
    grad_up_weight = contract_rows(normed_two, grad_hidden)
    grad_normed_two = contract_cols(grad_hidden, mlp_back[1])
    _, norm_two_back = jax.vjp(scaled_norm, middle, mlp_back[0].astype(jnp.float32))
    grad_middle_part, grad_second_gain = norm_two_back(grad_normed_two)
    grad_second_offset = jnp.sum(grad_normed_two, axis=0)
    grad_middle = seed + grad_middle_part
    mlp_shares = (
        grad_second_gain,
        grad_second_offset,
        grad_up_weight,
        grad_up_bias,
        grad_down_weight,
        grad_down_bias,
    )
    attn_back = (
        lax.all_gather(first_gain, ("dp", "fsdp"), axis=0, tiled=True),
        lax.all_gather(qkv_weight, ("dp", "fsdp"), axis=0, tiled=True),
        lax.all_gather(out_weight, ("dp", "fsdp"), axis=0, tiled=True),
    )
    grad_branch = (branch_scale * grad_middle).astype(jnp.bfloat16)
    grad_out_bias = jnp.sum(grad_branch.astype(jnp.float32), axis=0)
    grad_out_weight = contract_rows(attended, grad_branch)
    grad_attended = contract_cols(grad_branch, attn_back[2]).astype(jnp.bfloat16).reshape(row_shape)
    grad_queries, grad_keys, grad_values = lax.map(
        lambda row_item: attend_row_back(*row_item),
        (queries, keys, values, doc_ids, logsums, grad_attended),
    )
    grad_projected = jnp.concatenate(
        [
            grad_queries.reshape(-1, model_width),
            grad_keys.reshape(-1, model_width),
            grad_values.reshape(-1, model_width),
        ],
        axis=1,
    ).astype(jnp.bfloat16)
    grad_wide = grad_projected.astype(jnp.float32)
    grad_query_bias = jnp.sum(grad_wide[:, :model_width], axis=0)
    grad_value_bias = jnp.sum(grad_wide[:, 2 * model_width :], axis=0)
    grad_qkv_weight = contract_rows(normed_one, grad_projected)
    grad_normed_one = contract_cols(grad_projected, attn_back[1])
    _, norm_one_back = jax.vjp(scaled_norm, inputs, attn_back[0].astype(jnp.float32))
    grad_input_part, grad_first_gain = norm_one_back(grad_normed_one)
    grad_first_offset = jnp.sum(grad_normed_one, axis=0)
    grad_tokens = grad_middle + grad_input_part
    every_share = (
        lax.psum_scatter(grad_second_gain, ("dp", "fsdp"), scatter_dimension=0, tiled=True),
        lax.psum_scatter(grad_second_offset, ("dp", "fsdp"), scatter_dimension=0, tiled=True),
        lax.psum_scatter(grad_up_weight, ("dp", "fsdp"), scatter_dimension=0, tiled=True),
        lax.psum_scatter(grad_up_bias, ("dp", "fsdp"), scatter_dimension=0, tiled=True),
        lax.psum_scatter(grad_down_weight, ("dp", "fsdp"), scatter_dimension=0, tiled=True),
        lax.psum_scatter(grad_down_bias, ("dp", "fsdp"), scatter_dimension=0, tiled=True),
        lax.psum_scatter(grad_first_gain, ("dp", "fsdp"), scatter_dimension=0, tiled=True),
        lax.psum_scatter(grad_first_offset, ("dp", "fsdp"), scatter_dimension=0, tiled=True),
        lax.psum_scatter(grad_qkv_weight, ("dp", "fsdp"), scatter_dimension=0, tiled=True),
        lax.psum_scatter(grad_query_bias, ("dp", "fsdp"), scatter_dimension=0, tiled=True),
        lax.psum_scatter(grad_value_bias, ("dp", "fsdp"), scatter_dimension=0, tiled=True),
        lax.psum_scatter(grad_out_weight, ("dp", "fsdp"), scatter_dimension=0, tiled=True),
        lax.psum_scatter(grad_out_bias, ("dp", "fsdp"), scatter_dimension=0, tiled=True),
    )
    mlp_shares = every_share[:6]
    attn_shares = every_share[6:]
    return (
        layer_out,
        grad_tokens,
        attn_shares[0],
        attn_shares[1],
        attn_shares[2],
        attn_shares[3],
        attn_shares[4],
        attn_shares[5],
        attn_shares[6],
        mlp_shares[0],
        mlp_shares[1],
        mlp_shares[2],
        mlp_shares[3],
        mlp_shares[4],
        mlp_shares[5],
    )


def fast_device(
    tokens,
    doc_ids,
    cotangent,
    first_gain,
    first_offset,
    qkv_weight,
    query_bias,
    value_bias,
    out_weight,
    out_bias,
    second_gain,
    second_offset,
    up_weight,
    up_bias,
    down_weight,
    down_bias,
):
    shards = {"qkv": qkv_weight, "out": out_weight, "up": up_weight, "down": down_weight}
    vectors = (
        first_gain,
        first_offset,
        query_bias,
        value_bias,
        out_bias,
        second_gain,
        second_offset,
        down_bias,
    )
    qkv_full, out_full, up_full, down_full, small = gather(shards, spread(vectors, up_bias))
    attn_full = (small[0], small[1], qkv_full, small[2], small[3], out_full, small[4])
    mlp_full = (small[5], small[6], up_full, small[8:12].reshape(-1), down_full, small[7])
    attn_back = (small[0], qkv_full, out_full)
    mlp_back = (small[5], up_full, down_full)
    model_width = tokens.shape[1]
    rows_here = doc_ids.shape[0]
    seq_len = doc_ids.shape[1]
    inputs = tokens.astype(jnp.float32)
    gain_one = attn_full[0].astype(jnp.float32)
    normed_one = layer_norm(inputs, gain_one, attn_full[1].astype(jnp.float32)).astype(jnp.bfloat16)
    projected = dense(normed_one, attn_full[2])
    queries = (projected[:, :model_width] + attn_full[3].astype(jnp.float32)).astype(jnp.bfloat16)
    keys = projected[:, model_width : 2 * model_width].astype(jnp.bfloat16)
    values = (projected[:, 2 * model_width :] + attn_full[4].astype(jnp.float32)).astype(
        jnp.bfloat16
    )
    row_shape = (rows_here, seq_len, HEADS, HEAD_DIM)
    queries = queries.reshape(row_shape)
    keys = keys.reshape(row_shape)
    values = values.reshape(row_shape)
    attended, logsums = lax.map(
        lambda row_item: attend_row(*row_item), (queries, keys, values, doc_ids)
    )
    attended = attended.reshape(-1, model_width)
    branch = dense(attended, attn_full[5]) + attn_full[6].astype(jnp.float32)
    middle = inputs + branch_scale * branch
    gain_two = mlp_full[0].astype(jnp.float32)
    normed_two = layer_norm(middle, gain_two, mlp_full[1].astype(jnp.float32)).astype(jnp.bfloat16)
    hidden = dense(normed_two, mlp_full[2]) + mlp_full[3].astype(jnp.float32)
    active, gelu_back = jax.vjp(lambda pre_act: jax.nn.gelu(pre_act, approximate=True), hidden)
    active = active.astype(jnp.bfloat16)
    outer = dense(active, mlp_full[4]) + mlp_full[5].astype(jnp.float32)
    layer_out = (middle + branch_scale * outer).astype(jnp.bfloat16)
    seed = cotangent.astype(jnp.float32)
    grad_outer = (branch_scale * seed).astype(jnp.bfloat16)
    grad_down_bias = jnp.sum(grad_outer.astype(jnp.float32), axis=0)
    grad_down_weight = contract_rows(active, grad_outer)
    grad_active = contract_cols(grad_outer, mlp_back[2])
    grad_hidden = gelu_back(grad_active)[0].astype(jnp.bfloat16)
    grad_up_bias = jnp.sum(grad_hidden.astype(jnp.float32), axis=0)
    grad_up_weight = contract_rows(normed_two, grad_hidden)
    grad_normed_two = contract_cols(grad_hidden, mlp_back[1])
    _, norm_two_back = jax.vjp(scaled_norm, middle, mlp_back[0].astype(jnp.float32))
    grad_middle_part, grad_second_gain = norm_two_back(grad_normed_two)
    grad_second_offset = jnp.sum(grad_normed_two, axis=0)
    grad_middle = seed + grad_middle_part
    mlp_shares = (
        grad_second_gain,
        grad_second_offset,
        grad_up_weight,
        grad_up_bias,
        grad_down_weight,
        grad_down_bias,
    )
    grad_branch = (branch_scale * grad_middle).astype(jnp.bfloat16)
    grad_out_bias = jnp.sum(grad_branch.astype(jnp.float32), axis=0)
    grad_out_weight = contract_rows(attended, grad_branch)
    grad_attended = contract_cols(grad_branch, attn_back[2]).astype(jnp.bfloat16).reshape(row_shape)
    grad_queries, grad_keys, grad_values = lax.map(
        lambda row_item: attend_row_back(*row_item),
        (queries, keys, values, doc_ids, logsums, grad_attended),
    )
    grad_projected = jnp.concatenate(
        [
            grad_queries.reshape(-1, model_width),
            grad_keys.reshape(-1, model_width),
            grad_values.reshape(-1, model_width),
        ],
        axis=1,
    ).astype(jnp.bfloat16)
    grad_wide = grad_projected.astype(jnp.float32)
    grad_query_bias = jnp.sum(grad_wide[:, :model_width], axis=0)
    grad_value_bias = jnp.sum(grad_wide[:, 2 * model_width :], axis=0)
    grad_qkv_weight = contract_rows(normed_one, grad_projected)
    grad_normed_one = contract_cols(grad_projected, attn_back[1])
    _, norm_one_back = jax.vjp(scaled_norm, inputs, attn_back[0].astype(jnp.float32))
    grad_input_part, grad_first_gain = norm_one_back(grad_normed_one)
    grad_first_offset = jnp.sum(grad_normed_one, axis=0)
    grad_tokens = grad_middle + grad_input_part
    partials = {
        "qkv": grad_qkv_weight.astype(jnp.bfloat16),
        "out": grad_out_weight.astype(jnp.bfloat16),
        "up": grad_up_weight.astype(jnp.bfloat16),
        "down": grad_down_weight.astype(jnp.bfloat16),
    }
    small_grads = jnp.stack(
        [
            grad_first_gain,
            grad_first_offset,
            grad_query_bias,
            grad_value_bias,
            grad_out_bias,
            grad_second_gain,
            grad_second_offset,
            grad_down_bias,
        ]
    )
    small_grads = jnp.concatenate(
        [small_grads, grad_up_bias.reshape(4, WIDTH), jnp.zeros((4, WIDTH), jnp.float32)], axis=0
    )
    *matrices, total = scatter(partials, small_grads)
    parts, up_part = own_parts(total)
    return (
        layer_out,
        grad_tokens,
        parts[0],
        parts[1],
        matrices[0],
        parts[2],
        parts[3],
        matrices[1],
        parts[4],
        parts[5],
        parts[6],
        matrices[2],
        up_part,
        matrices[3],
        parts[7],
    )


def solution(mesh):
    placed = (
        P(("dp", "fsdp"), None),
        P(("dp", "fsdp"), None),
        P(("dp", "fsdp"), None),
        P(("dp", "fsdp")),
        P(("dp", "fsdp")),
        P(("dp", "fsdp"), None),
        P(("dp", "fsdp")),
        P(("dp", "fsdp")),
        P(("dp", "fsdp"), None),
        P(("dp", "fsdp")),
        P(("dp", "fsdp")),
        P(("dp", "fsdp")),
        P(("dp", "fsdp"), None),
        P(("dp", "fsdp")),
        P(("dp", "fsdp"), None),
        P(("dp", "fsdp")),
    )
    return jax.shard_map(
        fast_device if fits(mesh) else plain_device,
        mesh=mesh,
        in_specs=placed,
        out_specs=(
            P(("dp", "fsdp"), None),
            P(("dp", "fsdp"), None),
            P(("dp", "fsdp")),
            P(("dp", "fsdp")),
            P(("dp", "fsdp"), None),
            P(("dp", "fsdp")),
            P(("dp", "fsdp")),
            P(("dp", "fsdp"), None),
            P(("dp", "fsdp")),
            P(("dp", "fsdp")),
            P(("dp", "fsdp")),
            P(("dp", "fsdp"), None),
            P(("dp", "fsdp")),
            P(("dp", "fsdp"), None),
            P(("dp", "fsdp")),
        ),
        check_vma=False,
    )
```

```python
import jax
import jax.numpy as jnp
from jax import lax
from jax.experimental import pallas as pl
from jax.experimental.pallas import tpu as pltpu
from jax.sharding import PartitionSpec as P

HEADS = 12
HEAD_DIM = 64


norm_eps = 1e-05
branch_scale = 48.0 ** (-0.5)


def layer_norm(values, gains, offsets):
    average = jnp.mean(values, axis=-1, keepdims=True)
    centred = values - average
    variance = jnp.mean(centred * centred, axis=-1, keepdims=True)
    return centred * lax.rsqrt(variance + norm_eps) * gains + offsets


def scaled_norm(values, gains):
    return layer_norm(values, gains, 0.0)


def dense(former, latter):
    return jnp.dot(former, latter, preferred_element_type=jnp.float32)


def contract_rows(former, latter):
    return lax.dot_general(
        former, latter, (((0,), (0,)), ((), ())), preferred_element_type=jnp.float32
    )


def contract_cols(former, latter):
    return lax.dot_general(
        former, latter, (((1,), (1,)), ((), ())), preferred_element_type=jnp.float32
    )


def block_scores(queries, keys, documents, row_start, row_stop):
    score_scale = queries.shape[2] ** (-0.5)
    scores = (
        jnp.einsum(
            "qhd,khd->hqk",
            queries[row_start:row_stop],
            keys[:row_stop],
            preferred_element_type=jnp.float32,
        )
        * score_scale
    )
    positions = jnp.arange(row_stop)
    allowed = (documents[row_start:row_stop, None] == documents[None, :row_stop]) & (
        positions[None, :] <= positions[row_start:row_stop, None]
    )
    return jnp.where(allowed[None], scores, -1e30)


def attend_row(queries, keys, values, documents):
    seq_len = queries.shape[0]
    block_rows = min(512, seq_len)
    outputs = []
    logsums = []
    for row_start in range(0, seq_len, block_rows):
        row_stop = row_start + block_rows
        scores = block_scores(queries, keys, documents, row_start, row_stop)
        highest = jnp.max(scores, axis=-1, keepdims=True)
        raised = jnp.exp(scores - highest)
        summed = jnp.sum(raised, axis=-1, keepdims=True)
        weights = (raised / summed).astype(jnp.bfloat16)
        outputs.append(
            jnp.einsum(
                "hqk,khd->qhd", weights, values[:row_stop], preferred_element_type=jnp.float32
            )
        )
        logsums.append((highest + jnp.log(summed))[..., 0])
    return (jnp.concatenate(outputs, axis=0).astype(jnp.bfloat16), jnp.concatenate(logsums, axis=1))


def attend_row_back(queries, keys, values, documents, logsums, grad_out):
    seq_len = queries.shape[0]
    block_rows = min(512, seq_len)
    score_scale = queries.shape[2] ** (-0.5)
    query_parts = []
    grad_keys = jnp.zeros(keys.shape, jnp.float32)
    grad_values = jnp.zeros(values.shape, jnp.float32)
    for row_start in range(0, seq_len, block_rows):
        row_stop = row_start + block_rows
        scores = block_scores(queries, keys, documents, row_start, row_stop)
        probs = jnp.exp(scores - logsums[:, row_start:row_stop, None])
        incoming = grad_out[row_start:row_stop]
        grad_probs = jnp.einsum(
            "qhd,khd->hqk", incoming, values[:row_stop], preferred_element_type=jnp.float32
        )
        inner_sum = jnp.sum(probs * grad_probs, axis=-1, keepdims=True)
        grad_scores = (probs * (grad_probs - inner_sum)).astype(jnp.bfloat16)
        query_parts.append(
            jnp.einsum(
                "hqk,khd->qhd", grad_scores, keys[:row_stop], preferred_element_type=jnp.float32
            )
            * score_scale
        )
        key_term = (
            jnp.einsum(
                "hqk,qhd->khd",
                grad_scores,
                queries[row_start:row_stop],
                preferred_element_type=jnp.float32,
            )
            * score_scale
        )
        value_term = jnp.einsum(
            "hqk,qhd->khd", probs.astype(jnp.bfloat16), incoming, preferred_element_type=jnp.float32
        )
        padding = ((0, seq_len - row_stop), (0, 0), (0, 0))
        grad_keys = grad_keys + jnp.pad(key_term, padding)
        grad_values = grad_values + jnp.pad(value_term, padding)
    return (jnp.concatenate(query_parts, axis=0), grad_keys, grad_values)


def plain_device(
    tokens,
    doc_ids,
    cotangent,
    first_gain,
    first_offset,
    qkv_weight,
    query_bias,
    value_bias,
    out_weight,
    out_bias,
    second_gain,
    second_offset,
    up_weight,
    up_bias,
    down_weight,
    down_bias,
):
    attn_full = (
        lax.all_gather(first_gain, ("dp", "fsdp"), axis=0, tiled=True),
        lax.all_gather(first_offset, ("dp", "fsdp"), axis=0, tiled=True),
        lax.all_gather(qkv_weight, ("dp", "fsdp"), axis=0, tiled=True),
        lax.all_gather(query_bias, ("dp", "fsdp"), axis=0, tiled=True),
        lax.all_gather(value_bias, ("dp", "fsdp"), axis=0, tiled=True),
        lax.all_gather(out_weight, ("dp", "fsdp"), axis=0, tiled=True),
        lax.all_gather(out_bias, ("dp", "fsdp"), axis=0, tiled=True),
    )
    model_width = tokens.shape[1]
    rows_here = doc_ids.shape[0]
    seq_len = doc_ids.shape[1]
    inputs = tokens.astype(jnp.float32)
    gain_one = attn_full[0].astype(jnp.float32)
    normed_one = layer_norm(inputs, gain_one, attn_full[1].astype(jnp.float32)).astype(jnp.bfloat16)
    projected = dense(normed_one, attn_full[2])
    queries = (projected[:, :model_width] + attn_full[3].astype(jnp.float32)).astype(jnp.bfloat16)
    keys = projected[:, model_width : 2 * model_width].astype(jnp.bfloat16)
    values = (projected[:, 2 * model_width :] + attn_full[4].astype(jnp.float32)).astype(
        jnp.bfloat16
    )
    row_shape = (rows_here, seq_len, HEADS, HEAD_DIM)
    queries = queries.reshape(row_shape)
    keys = keys.reshape(row_shape)
    values = values.reshape(row_shape)
    attended, logsums = lax.map(
        lambda row_item: attend_row(*row_item), (queries, keys, values, doc_ids)
    )
    attended = attended.reshape(-1, model_width)
    branch = dense(attended, attn_full[5]) + attn_full[6].astype(jnp.float32)
    middle = inputs + branch_scale * branch
    mlp_full = (
        lax.all_gather(second_gain, ("dp", "fsdp"), axis=0, tiled=True),
        lax.all_gather(second_offset, ("dp", "fsdp"), axis=0, tiled=True),
        lax.all_gather(up_weight, ("dp", "fsdp"), axis=0, tiled=True),
        lax.all_gather(up_bias, ("dp", "fsdp"), axis=0, tiled=True),
        lax.all_gather(down_weight, ("dp", "fsdp"), axis=0, tiled=True),
        lax.all_gather(down_bias, ("dp", "fsdp"), axis=0, tiled=True),
    )
    gain_two = mlp_full[0].astype(jnp.float32)
    normed_two = layer_norm(middle, gain_two, mlp_full[1].astype(jnp.float32)).astype(jnp.bfloat16)
    hidden = dense(normed_two, mlp_full[2]) + mlp_full[3].astype(jnp.float32)
    active, gelu_back = jax.vjp(lambda pre_act: jax.nn.gelu(pre_act, approximate=True), hidden)
    active = active.astype(jnp.bfloat16)
    outer = dense(active, mlp_full[4]) + mlp_full[5].astype(jnp.float32)
    layer_out = (middle + branch_scale * outer).astype(jnp.bfloat16)
    mlp_back = (
        lax.all_gather(second_gain, ("dp", "fsdp"), axis=0, tiled=True),
        lax.all_gather(up_weight, ("dp", "fsdp"), axis=0, tiled=True),
        lax.all_gather(down_weight, ("dp", "fsdp"), axis=0, tiled=True),
    )
    seed = cotangent.astype(jnp.float32)
    grad_outer = (branch_scale * seed).astype(jnp.bfloat16)
    grad_down_bias = jnp.sum(grad_outer.astype(jnp.float32), axis=0)
    grad_down_weight = contract_rows(active, grad_outer)
    grad_active = contract_cols(grad_outer, mlp_back[2])
    grad_hidden = gelu_back(grad_active)[0].astype(jnp.bfloat16)
    grad_up_bias = jnp.sum(grad_hidden.astype(jnp.float32), axis=0)
    grad_up_weight = contract_rows(normed_two, grad_hidden)
    grad_normed_two = contract_cols(grad_hidden, mlp_back[1])
    _, norm_two_back = jax.vjp(scaled_norm, middle, mlp_back[0].astype(jnp.float32))
    grad_middle_part, grad_second_gain = norm_two_back(grad_normed_two)
    grad_second_offset = jnp.sum(grad_normed_two, axis=0)
    grad_middle = seed + grad_middle_part
    mlp_shares = (
        grad_second_gain,
        grad_second_offset,
        grad_up_weight,
        grad_up_bias,
        grad_down_weight,
        grad_down_bias,
    )
    attn_back = (
        lax.all_gather(first_gain, ("dp", "fsdp"), axis=0, tiled=True),
        lax.all_gather(qkv_weight, ("dp", "fsdp"), axis=0, tiled=True),
        lax.all_gather(out_weight, ("dp", "fsdp"), axis=0, tiled=True),
    )
    grad_branch = (branch_scale * grad_middle).astype(jnp.bfloat16)
    grad_out_bias = jnp.sum(grad_branch.astype(jnp.float32), axis=0)
    grad_out_weight = contract_rows(attended, grad_branch)
    grad_attended = contract_cols(grad_branch, attn_back[2]).astype(jnp.bfloat16).reshape(row_shape)
    grad_queries, grad_keys, grad_values = lax.map(
        lambda row_item: attend_row_back(*row_item),
        (queries, keys, values, doc_ids, logsums, grad_attended),
    )
    grad_projected = jnp.concatenate(
        [
            grad_queries.reshape(-1, model_width),
            grad_keys.reshape(-1, model_width),
            grad_values.reshape(-1, model_width),
        ],
        axis=1,
    ).astype(jnp.bfloat16)
    grad_wide = grad_projected.astype(jnp.float32)
    grad_query_bias = jnp.sum(grad_wide[:, :model_width], axis=0)
    grad_value_bias = jnp.sum(grad_wide[:, 2 * model_width :], axis=0)
    grad_qkv_weight = contract_rows(normed_one, grad_projected)
    grad_normed_one = contract_cols(grad_projected, attn_back[1])
    _, norm_one_back = jax.vjp(scaled_norm, inputs, attn_back[0].astype(jnp.float32))
    grad_input_part, grad_first_gain = norm_one_back(grad_normed_one)
    grad_first_offset = jnp.sum(grad_normed_one, axis=0)
    grad_tokens = grad_middle + grad_input_part
    every_share = (
        lax.psum_scatter(grad_second_gain, ("dp", "fsdp"), scatter_dimension=0, tiled=True),
        lax.psum_scatter(grad_second_offset, ("dp", "fsdp"), scatter_dimension=0, tiled=True),
        lax.psum_scatter(grad_up_weight, ("dp", "fsdp"), scatter_dimension=0, tiled=True),
        lax.psum_scatter(grad_up_bias, ("dp", "fsdp"), scatter_dimension=0, tiled=True),
        lax.psum_scatter(grad_down_weight, ("dp", "fsdp"), scatter_dimension=0, tiled=True),
        lax.psum_scatter(grad_down_bias, ("dp", "fsdp"), scatter_dimension=0, tiled=True),
        lax.psum_scatter(grad_first_gain, ("dp", "fsdp"), scatter_dimension=0, tiled=True),
        lax.psum_scatter(grad_first_offset, ("dp", "fsdp"), scatter_dimension=0, tiled=True),
        lax.psum_scatter(grad_qkv_weight, ("dp", "fsdp"), scatter_dimension=0, tiled=True),
        lax.psum_scatter(grad_query_bias, ("dp", "fsdp"), scatter_dimension=0, tiled=True),
        lax.psum_scatter(grad_value_bias, ("dp", "fsdp"), scatter_dimension=0, tiled=True),
        lax.psum_scatter(grad_out_weight, ("dp", "fsdp"), scatter_dimension=0, tiled=True),
        lax.psum_scatter(grad_out_bias, ("dp", "fsdp"), scatter_dimension=0, tiled=True),
    )
    mlp_shares = every_share[:6]
    attn_shares = every_share[6:]
    return (
        layer_out,
        grad_tokens,
        attn_shares[0],
        attn_shares[1],
        attn_shares[2],
        attn_shares[3],
        attn_shares[4],
        attn_shares[5],
        attn_shares[6],
        mlp_shares[0],
        mlp_shares[1],
        mlp_shares[2],
        mlp_shares[3],
        mlp_shares[4],
        mlp_shares[5],
    )


MESH = pl.DeviceIdType.MESH
F32 = jnp.float32
BF16 = jnp.bfloat16
WIDTH = 768
HIDDEN = 3072
TOKENS = 1024
QKV = 3 * WIDTH
PAIRS = 6
QUERY_ROWS = 256
KEY_WINDOWS = ((0, 256), (0, 512), (0, 768), (256, 1024))
DOCUMENTS = 6
FAR_BELOW = 2.0**100
STRIP = 128
TILE = 256
VMEM_LIMIT = 63 * 2**20
GELU_A = 0.7978845608028654
GELU_B = 0.044715

GATHER_UNITS = (
    ("qkv", 0, 384),
    ("qkv", 768, 384),
    ("qkv", 1536, 384),
    ("out", 0, 384),
    ("down", 0, 128),
    ("down", 128, 128),
    ("down", 256, 128),
    ("up", 0, 384),
    ("up", 768, 384),
    ("up", 1536, 384),
    ("up", 2304, 384),
)
SCATTER_UNITS = (
    ("up", 0, 384),
    ("up", 768, 384),
    ("up", 1536, 384),
    ("up", 2304, 384),
    ("down", 0, 128),
    ("down", 128, 128),
    ("down", 256, 128),
    ("out", 0, 384),
    ("qkv", 0, 384),
    ("qkv", 768, 384),
    ("qkv", 1536, 384),
)
SHARD_ROWS = {"qkv": 24, "out": 24, "up": 24, "down": 96}
COLUMNS = {"qkv": QKV, "out": WIDTH, "up": HIDDEN, "down": WIDTH}
NAMES = ("qkv", "out", "up", "down")


def fits(mesh):
    return mesh.shape["dp"] == 4 and mesh.shape["fsdp"] == 8


def padded(rows):
    return -(-rows // 16) * 16


def aligned(value, step):
    return pl.multiple_of(value, step)


def dot_nt(a, b):
    return lax.dot_general(a, b, (((1,), (1,)), ((), ())), preferred_element_type=F32)


def dot_nn(a, b):
    return lax.dot_general(a, b, (((1,), (0,)), ((), ())), preferred_element_type=F32)


def dot_tn(a, b):
    return lax.dot_general(a, b, (((0,), (0,)), ((), ())), preferred_element_type=F32)


class Place:
    def __init__(self):
        self.dp = lax.axis_index("dp")
        self.fsdp = lax.axis_index("fsdp")
        self.core = lax.rem(self.fsdp, 2)
        self.z = lax.div(self.fsdp, 2)
        x = lax.rem(self.dp, 2)
        y = lax.div(self.dp, 2)
        self.dp_x = y * 2 + (1 - x)
        self.dp_y = (1 - y) * 2 + x
        self.dp_far = 3 - self.dp
        core = self.core
        self.near = self.dp_x * (1 - core) + self.dp_y * core
        self.next = self.dp_y * (1 - core) + self.dp_x * core
        self.chip = self.dp * 4 + self.z
        self.partner = (self.dp, self.z * 2 + (1 - core))
        self.at_near = (self.near, self.fsdp)
        self.at_next = (self.next, self.fsdp)

    def along_z(self, step):
        z = lax.rem(self.z + step, 4)
        return (self.dp, z * 2 + self.core)

    def greet(self):
        barrier = pltpu.get_barrier_semaphore()
        others = [self.partner, (self.dp_x, self.fsdp), (self.dp_y, self.fsdp), (self.dp_far, self.fsdp)]
        others += [self.along_z(step) for step in (1, 2, 3)]
        for other in others:
            pl.semaphore_signal(barrier, inc=1, device_id=other, device_id_type=MESH)
        pl.semaphore_wait(barrier, len(others))


def remote(source, target, sems, index, device):
    return pltpu.make_async_remote_copy(
        src_ref=source,
        dst_ref=target,
        send_sem=sems[0].at[index],
        recv_sem=sems[1].at[index],
        device_id=device,
        device_id_type=MESH,
    )


class SmallSum:
    def __init__(self, place, buffers, landed, sems):
        self.place, self.buffers, self.landed, self.sems = place, buffers, landed, sems

    @staticmethod
    def scratch():
        return [
            pltpu.VMEM((3, 16, WIDTH), F32),
            pltpu.VMEM((7, 16, WIDTH), F32),
            pltpu.SemaphoreType.DMA((7,)),
            pltpu.SemaphoreType.DMA((7,)),
        ]

    def copies(self, stage):
        p = self.place
        if stage == 0:
            devices = [p.partner]
        elif stage == 1:
            devices = [(dp, p.fsdp) for dp in (p.dp_x, p.dp_y, p.dp_far)]
        else:
            devices = [p.along_z(step) for step in (1, 2, 3)]
        first = (0, 1, 4)[stage]
        return [
            remote(self.buffers.at[stage], self.landed.at[first + i], self.sems, first + i, device)
            for i, device in enumerate(devices)
        ]

    def begin(self, value):
        self.buffers[0] = value
        for copy in self.copies(0):
            copy.start()

    def middle(self):
        for copy in self.copies(0):
            copy.wait()
        self.buffers[1] = self.buffers[0] + self.landed[0]
        for copy in self.copies(1):
            copy.start()

    def last(self):
        for copy in self.copies(1):
            copy.wait()
        self.buffers[2] = (self.buffers[1] + self.landed[1]) + (self.landed[2] + self.landed[3])
        for copy in self.copies(2):
            copy.start()

    def end(self):
        for copy in self.copies(2):
            copy.wait()
        return (self.buffers[2] + self.landed[4]) + (self.landed[5] + self.landed[6])


class GatherUnit:
    SEMS = 11

    def __init__(self, place, unit, shard, full, pair_out, pair_in, send_sems, recv_sems):
        self.place = place
        self.name, self.first, self.width = unit
        self.rows = SHARD_ROWS[self.name]
        self.shard, self.full = shard, full
        self.pair_out, self.pair_in = pair_out, pair_in
        self.sems = (send_sems, recv_sems)

    def part_of(self, core):
        if self.name != "qkv":
            return self.shard[:, pl.ds(aligned(self.first + 384 * core, 128), self.width)]
        start = self.first // 3 + 128 * core
        parts = [self.shard[:, pl.ds(aligned(start + WIDTH * i, 128), 128)] for i in range(3)]
        return jnp.concatenate(parts, axis=1)

    def columns(self):
        return pl.ds(aligned(self.first + 384 * self.place.core, 128), self.width)

    def group(self, dp):
        rows = 8 * self.rows
        return self.full.at[pl.ds(aligned(dp * rows, 16), rows), self.columns()]

    def block(self):
        rows = 2 * self.rows
        return self.full.at[pl.ds(aligned(self.place.chip * rows, 16), rows), self.columns()]

    def copy(self, index):
        p = self.place
        if index == 0:
            return remote(self.pair_out, self.pair_in, self.sems, 0, p.partner)
        if index < 4:
            return remote(self.block(), self.block(), self.sems, index, p.along_z(index))
        dp = (p.dp, p.dp, p.near, p.dp, p.near, p.next, p.dp_far)[index - 4]
        device = p.at_near if index == 4 else p.at_next if index < 7 else p.partner
        return remote(self.group(dp), self.group(dp), self.sems, index, device)

    def start(self, *indices):
        for index in indices:
            self.copy(index).start()

    def landed(self, *indices):
        for index in indices:
            self.copy(index).wait_recv()

    def pair(self):
        self.pair_out[0 : self.rows] = self.part_of(1 - self.place.core)
        if self.rows % 16:
            rest = padded(self.rows) - self.rows
            self.pair_out[self.rows :] = jnp.zeros((rest, self.width), BF16)
        self.start(0)

    def along_z(self):
        self.landed(0)
        own = self.part_of(self.place.core).astype(F32)
        came = self.pair_in[0 : self.rows].astype(F32)
        first = self.place.core == 0
        block = jnp.concatenate([jnp.where(first, own, came), jnp.where(first, came, own)], axis=0)
        self.block()[...] = block.astype(BF16)
        self.start(1, 2, 3)

    def to_near(self):
        self.landed(1, 2, 3)
        self.start(4, 5, 7)

    def to_next(self):
        self.landed(4)
        self.start(6, 8)

    def to_core(self):
        self.landed(5)
        self.start(9)
        self.landed(6)
        self.start(10)

    def arrived(self):
        self.landed(7, 8, 9, 10)

    def finish(self):
        for index in range(self.SEMS):
            self.copy(index).wait_send()


class ScatterUnit:
    SEMS = 8

    def __init__(self, place, unit, partial, target, halves, from_next, from_near, from_z, pair, send_sems, recv_sems):
        self.place = place
        self.name, self.first, self.width = unit
        self.rows = SHARD_ROWS[self.name]
        self.partial, self.target = partial, target
        self.halves, self.from_next, self.from_near = halves, from_next, from_near
        self.from_z, self.pair_buffer = from_z, pair
        self.sems = (send_sems, recv_sems)

    @staticmethod
    def scratch(unit):
        name, _, width = unit
        rows = SHARD_ROWS[name]
        return [
            pltpu.VMEM((32 * rows, width), BF16),
            pltpu.VMEM((2, 8 * rows, width), BF16),
            pltpu.VMEM((8 * rows, width), BF16),
            pltpu.VMEM((3, 2 * rows, width), BF16),
            pltpu.VMEM((3, rows, width), F32),
        ]

    def columns(self, core):
        first = 0 if self.name == "qkv" else self.first
        return pl.ds(aligned(first + 384 * core, 128), self.width)

    def group(self, dp):
        rows = 8 * self.rows
        return self.halves.at[pl.ds(aligned(dp * rows, 16), rows)]

    def z_block(self, step):
        z = lax.rem(self.place.z + step, 4)
        rows = 2 * self.rows
        return self.halves.at[pl.ds(aligned((self.place.dp * 4 + z) * rows, 16), rows)]

    def copy(self, index):
        p = self.place
        if index == 0:
            source = self.partial.at[pl.ds(0, 32 * self.rows), self.columns(1 - p.core)]
            return remote(source, self.halves, self.sems, 0, p.partner)
        if index < 3:
            dp = (p.next, p.dp_far)[index - 1]
            return remote(self.group(dp), self.from_next.at[index - 1], self.sems, index, p.at_next)
        if index == 3:
            return remote(self.group(p.near), self.from_near, self.sems, 3, p.at_near)
        if index < 7:
            step = index - 3
            return remote(self.z_block(step), self.from_z.at[step - 1], self.sems, index, p.along_z(step))
        return remote(self.pair_buffer.at[0], self.pair_buffer.at[2], self.sems, 7, p.partner)

    def start(self, *indices):
        for index in indices:
            self.copy(index).start()

    def landed(self, *indices):
        for index in indices:
            self.copy(index).wait_recv()

    def add(self, former, latter, rows):
        step = 192

        def body(index, carry):
            at = pl.ds(aligned(index * step, 16), step)
            former[at] = (former[at].astype(F32) + latter(at).astype(F32)).astype(BF16)
            return carry

        lax.fori_loop(0, rows // step, body, 0)

    def to_partner(self):
        self.start(0)

    def to_next(self):
        self.landed(0)
        mine = self.columns(self.place.core)
        self.add(self.halves, lambda at: self.partial[at, mine], 32 * self.rows)
        self.start(1, 2)

    def to_near(self):
        p = self.place
        self.landed(1, 2)
        self.add(self.group(p.near), lambda at: self.from_next[1, at], 8 * self.rows)
        self.start(3)
        self.add(self.group(p.dp), lambda at: self.from_next[0, at], 8 * self.rows)

    def along_z(self):
        self.landed(3)
        self.add(self.group(self.place.dp), lambda at: self.from_near[at], 8 * self.rows)
        self.start(4, 5, 6)

    def to_pair(self):
        self.landed(4, 5, 6)
        rows = self.rows
        came = [self.from_z[i].astype(F32) for i in range(3)]
        block = (self.z_block(0)[...].astype(F32) + came[0]) + (came[1] + came[2])
        first = self.place.core == 0
        self.pair_buffer[0] = jnp.where(first, block[rows:], block[:rows])
        self.pair_buffer[1] = jnp.where(first, block[:rows], block[rows:])
        self.start(7)

    def store(self):
        self.landed(7)
        for source, core in ((1, self.place.core), (2, 1 - self.place.core)):
            if self.name != "qkv":
                self.target[:, self.columns(core)] = self.pair_buffer[source]
                continue
            start = self.first // 3 + 128 * core
            for i in range(3):
                columns = pl.ds(aligned(start + WIDTH * i, 128), 128)
                self.target[:, columns] = self.pair_buffer[source, :, 128 * i : 128 * i + 128]

    def finish(self):
        for index in range(self.SEMS):
            self.copy(index).wait_send()


STAGES = {
    "P": "to_partner",
    "A": "to_next",
    "B": "to_near",
    "Z": "along_z",
    "D": "to_pair",
    "S": "store",
    "z": "along_z",
    "n": "to_near",
    "x": "to_next",
    "c": "to_core",
    "r": "arrived",
}


def run_stages(units, text):
    for step in text.split():
        getattr(units[int(step[1:])], STAGES[step[0]])()


def strips(body, carry=0):
    def run(index, carry):
        return body(pl.ds(aligned(index * STRIP, STRIP), STRIP), carry)

    return lax.fori_loop(0, TOKENS // STRIP, run, carry)


def standardized(values):
    average = jnp.mean(values, axis=-1, keepdims=True)
    centred = values - average
    variance = jnp.mean(centred * centred, axis=-1, keepdims=True)
    scale = lax.rsqrt(variance + norm_eps)
    return centred * scale, scale


def back_through_norm(grad, xhat, scale, gains):
    lifted = grad * gains
    return scale * (
        lifted
        - jnp.mean(lifted, axis=-1, keepdims=True)
        - xhat * jnp.mean(lifted * xhat, axis=-1, keepdims=True)
    )


def column_sum(values):
    return jnp.sum(values, axis=0, keepdims=True)


def gelu_and_slope(h):
    square = h * h
    bent = GELU_A + GELU_A * GELU_B * square
    gate = 0.5 + 0.5 * jnp.tanh(h * bent)
    active = h * gate
    slope = gate + active * (1.0 - gate) * (6.0 * bent - 4.0 * GELU_A)
    return active, slope


def document_lanes(documents, query_side, key_side):
    lane = lax.rem(lax.broadcasted_iota(jnp.int32, (TOKENS, 128), 1), 64)
    own = jnp.broadcast_to(documents.astype(F32), (128, TOKENS)).T == lane.astype(F32)
    query_side[...] = jnp.where(own, 1.0, 0.0).astype(BF16)
    key_side[...] = jnp.where(own | (lane >= DOCUMENTS), 0.0, -FAR_BELOW).astype(BF16)


def causal_corner(causal):
    key = lax.broadcasted_iota(jnp.int32, (QUERY_ROWS, QUERY_ROWS), 0)
    query = lax.broadcasted_iota(jnp.int32, (QUERY_ROWS, QUERY_ROWS), 1)
    causal[...] = jnp.where(key <= query, 0.0, -FAR_BELOW)


class Pair:
    def __init__(self, wide, pair, block, query_side, key_side):
        start, stop = KEY_WINDOWS[block]
        self.keys = pl.ds(start, stop - start)
        self.rows = pl.ds(block * QUERY_ROWS, QUERY_ROWS)
        first = pair * 384
        self.at = [pl.ds(aligned(first + 128 * i, 128), 128) for i in range(3)]
        self.q = wide[self.rows, self.at[0]]
        self.k = wide[self.keys, self.at[1]]
        self.v = wide[self.keys, self.at[2]]
        self.query_side, self.key_side = query_side[self.rows], key_side[self.keys]
        self.start, self.stop = start, stop

    def choose(self, head, inside, outside):
        low = lax.broadcasted_iota(jnp.int32, inside.shape, 1) < 64
        return jnp.where(low, inside, outside) if head == 0 else jnp.where(low, outside, inside)

    def only(self, head, values):
        return self.choose(head, values, jnp.zeros_like(values))

    def scores(self, head, causal):
        scores = dot_nt(self.choose(head, self.k, self.key_side), self.choose(head, self.q, self.query_side))
        wide = self.stop - self.start - QUERY_ROWS
        corner = scores[wide:] + causal[...]
        return jnp.concatenate([scores[:wide], corner], axis=0) if wide else corner


def attend(wide, pair, block, query_side, key_side, causal, attended, logsums):
    p = Pair(wide, pair, block, query_side, key_side)
    weights, sums = [], []
    for head in range(2):
        scores = p.scores(head, causal)
        highest = jnp.max(scores, axis=0, keepdims=True)
        raised = jnp.exp(scores - highest)
        summed = column_sum(raised)
        weights.append(raised.astype(BF16))
        sums.append(jnp.broadcast_to(summed, (HEAD_DIM, QUERY_ROWS)))
        logsums[2 * pair + head, :, p.rows] = highest + jnp.log(summed)
    values = jnp.concatenate([p.only(head, p.v) for head in range(2)], axis=0)
    out = dot_tn(values, jnp.concatenate(weights, axis=0)) / jnp.concatenate(sums, axis=0)
    attended[p.rows, pl.ds(aligned(pair * 128, 128), 128)] = out.T.astype(BF16)


def attend_back(wide, pair, block, query_side, key_side, causal, attended, grad_attended, logsums, key_sum, value_sum):
    p = Pair(wide, pair, block, query_side, key_side)
    features = pl.ds(aligned(pair * 128, 128), 128)
    incoming = grad_attended[p.rows, features]
    inner = (incoming.astype(F32) * attended[p.rows, features].astype(F32)).T
    probs, slopes = [], []
    for head in range(2):
        delta = column_sum(inner[64 * head : 64 * head + 64])
        prob = jnp.exp(p.scores(head, causal) - logsums[2 * pair + head, :, p.rows])
        grad_prob = dot_nt(p.v, p.only(head, incoming))
        probs.append(prob.astype(BF16))
        slopes.append((prob * (grad_prob - delta)).astype(BF16))
    both = lambda values: jnp.concatenate([p.only(head, values) for head in range(2)], axis=0)
    value_part = dot_nn(jnp.concatenate(probs, axis=1), both(incoming))
    key_part = dot_nn(jnp.concatenate(slopes, axis=1), both(p.q))
    query_part = dot_tn(both(p.k), jnp.concatenate(slopes, axis=0))
    wide[p.rows, p.at[0]] = (query_part.T * HEAD_DIM**-0.5).astype(BF16)
    inside = p.stop - p.start - QUERY_ROWS
    if inside:
        earlier = pl.ds(p.start, inside)
        key_sum[earlier] += key_part[:inside]
        value_sum[earlier] += value_part[:inside]
    newest = pl.ds(p.stop - QUERY_ROWS, QUERY_ROWS)
    key_sum[newest] = key_part[inside:]
    value_sum[newest] = value_part[inside:]


def layer_kernel(*refs):
    refs = list(refs)

    def take(count):
        taken = refs[:count]
        del refs[:count]
        return taken

    tokens, documents, cotangent = take(3)
    shards = dict(zip(NAMES, take(4)))
    (small,) = take(1)
    layer_out, grad_tokens = take(2)
    targets = dict(zip(NAMES, take(4)))
    (small_out,) = take(1)
    weights = dict(zip(NAMES, take(4)))
    wq, wo, wu, wd = (weights[name] for name in NAMES)
    wide, norm, norm_t, attended, seed, act, act_t, slope = take(8)
    middle, outer, grad_norm = take(3)
    logsums, query_side, key_side, causal, vectors, qkv_bias, qkv_scale, sums = take(8)
    pair_buffers = take(2 * len(GATHER_UNITS))
    scatter_buffers = take(5 * len(SCATTER_UNITS))
    gather_sems, scatter_sems = take(2), take(2)
    first_small, last_small = take(4), take(4)
    (local_sems,) = take(1)

    place = Place()
    coming = [
        GatherUnit(
            place,
            unit,
            shards[unit[0]],
            weights[unit[0]],
            *pair_buffers[2 * i : 2 * i + 2],
            gather_sems[0].at[i],
            gather_sems[1].at[i],
        )
        for i, unit in enumerate(GATHER_UNITS)
    ]
    partials = {"up": wu, "down": wd, "out": wo}
    qkv_partials = (slope, act_t, norm)
    leaving = [
        ScatterUnit(
            place,
            unit,
            partials[unit[0]] if unit[0] != "qkv" else qkv_partials[unit[1] // WIDTH],
            targets[unit[0]],
            *scatter_buffers[5 * i : 5 * i + 5],
            scatter_sems[0].at[i],
            scatter_sems[1].at[i],
        )
        for i, unit in enumerate(SCATTER_UNITS)
    ]

    def gathering(text):
        run_stages(coming, text)

    def scattering(text):
        run_stages(leaving, text)

    place.greet()
    total = SmallSum(place, first_small[0], first_small[1], first_small[2:])
    total.begin(small[...])
    for unit in coming:
        unit.pair()
    gathering("z0")
    total.middle()
    gathering("z1")
    total.last()
    gathering("z2 n0")
    document_lanes(documents[...], query_side, key_side)
    causal_corner(causal)
    vectors[...] = total.end()
    gathering("x0 n1 z3")
    gain_one, offset_one = vectors[0:1], vectors[1:2]
    for pair in range(PAIRS):
        at = slice(128 * pair, 128 * pair + 128)
        first = 384 * pair
        qkv_bias[:, first : first + 128] = vectors[2:3, at]
        qkv_bias[:, first + 128 : first + 256] = jnp.zeros((1, 128), F32)
        qkv_bias[:, first + 256 : first + 384] = vectors[3:4, at]
        qkv_scale[:, first : first + 128] = jnp.full((1, 128), HEAD_DIM**-0.5, F32)
        qkv_scale[:, first + 128 : first + 384] = jnp.ones((1, 256), F32)

    def norm_one(rows, carry):
        xhat, _ = standardized(tokens[rows].astype(F32))
        norm[rows] = (xhat * gain_one + offset_one).astype(BF16)
        return carry

    strips(norm_one)
    gathering("c0 x1 n2 z4")

    def forward_group(group, carry):
        for number, text in enumerate(("r0", "c1 x2 n3 z5 r1", "c3 x4 n5 z7 r2")):
            pl.when(group == number)(lambda text=text: gathering(text))
        for n in range(3):
            columns = pl.ds(aligned(group * WIDTH + n * TILE, 128), TILE)
            projected = dot_nn(norm[...], wq[:, columns]) + qkv_bias[:, columns]
            wide[:, columns] = (projected * qkv_scale[:, columns]).astype(BF16)

        def forward_pair(half, carry):
            pair = 2 * group + half
            for block in range(4):
                attend(wide, pair, block, query_side, key_side, causal, attended, logsums)
            for number, text in ((2, "c2 x3 n4 z6"), (4, "c4 x5 n6 z8 r3"), (5, "c5 x6 n7 z9")):
                pl.when(pair == number)(lambda text=text: gathering(text))
            return carry

        return lax.fori_loop(0, 2, forward_pair, carry)

    lax.fori_loop(0, 3, forward_group, 0)

    for n in range(3):
        at = slice(n * TILE, n * TILE + TILE)
        branch = dot_nn(attended[...], wo[:, at]) + vectors[4:5, at]
        middle[:, at] = tokens[:, at].astype(F32) + branch_scale * branch
    gathering("c6 x7 n8 z10 r4")
    gain_two, offset_two = vectors[5:6], vectors[6:7]

    def norm_two(rows, down_bias):
        xhat, _ = standardized(middle[rows])
        norm[rows] = (xhat * gain_two + offset_two).astype(BF16)
        scaled = (branch_scale * cotangent[rows].astype(F32)).astype(BF16)
        seed[rows] = scaled
        outer[rows] = jnp.zeros((STRIP, WIDTH), F32)
        grad_norm[rows] = jnp.zeros((STRIP, WIDTH), F32)
        return down_bias + column_sum(scaled.astype(F32))

    sums[7:8] = strips(norm_two, jnp.zeros((1, WIDTH), F32))
    norm_t[0:WIDTH] = norm[...].T
    norm_t[WIDTH:] = jnp.ones((16, TOKENS), BF16)
    gathering("c7 x8 n9 r5 r6 r7")

    def feed_forward(step, carry):
        for n in range(3):
            at = slice(n * TILE, n * TILE + TILE)
            columns = pl.ds(aligned(step * WIDTH + n * TILE, 128), TILE)
            bias = vectors[pl.ds(8 + step, 1), at]
            hidden = dot_nn(norm[...], wu[:, columns]) + bias
            grad_active = dot_nt(seed[...], wd[columns])
            active, bent = gelu_and_slope(hidden)
            act[:, at] = active.astype(BF16)
            slope[:, at] = (grad_active * bent).astype(BF16)
        here = pl.ds(aligned(step * WIDTH, 128), WIDTH)
        for n in range(3):
            at = slice(n * TILE, n * TILE + TILE)
            outer[:, at] += dot_nn(act[...], wd[here, at])
            grad_norm[:, at] += dot_nt(slope[...], wu[at, here])
        for number, text in enumerate(("c8 x9 n10", "c9 x10", "c10", "")):
            pl.when(step == number)(lambda text=text: gathering(text))
        for number in range(4):
            def own_columns(number=number):
                coming[7 + number].finish()
                if number == 0:
                    for unit in coming[:7]:
                        unit.finish()

            pl.when(step == number)(own_columns)
        act_t[...] = act[...].T
        for n in range(3):
            at = slice(n * TILE, n * TILE + TILE)
            columns = pl.ds(aligned(step * WIDTH + n * TILE, 128), TILE)
            grad = dot_nn(norm_t[...], slope[:, at])
            wu[:, columns] = grad[:WIDTH].astype(BF16)
            sums[pl.ds(8 + step, 1), at] = grad[WIDTH : WIDTH + 1]
            wd[here, at] = dot_nn(act_t[...], seed[:, at]).astype(BF16)
        for number, text in enumerate(("P0", "P1 A0", "B0 A1 P2", "Z0 B1 A2 P3 P4")):
            pl.when(step == number)(lambda text=text: scattering(text))
        for number, text in enumerate(("r8", "r9", "r10", "")):
            pl.when(step == number)(lambda text=text: gathering(text))
        return carry

    lax.fori_loop(0, 4, feed_forward, 0)

    def back_two(rows, carry):
        mid = middle[rows]
        slope[rows] = (mid + branch_scale * (outer[rows] + vectors[7:8])).astype(BF16)
        xhat, scale = standardized(mid)
        grad = grad_norm[rows]
        grad_middle = cotangent[rows].astype(F32) + back_through_norm(grad, xhat, scale, gain_two)
        middle[rows] = grad_middle
        grad_branch = (branch_scale * grad_middle).astype(BF16)
        seed[rows] = grad_branch
        parts = (column_sum(grad_branch.astype(F32)), column_sum(grad * xhat), column_sum(grad))
        return tuple(former + part for former, part in zip(carry, parts))

    zero = jnp.zeros((1, WIDTH), F32)
    sums[4:5], sums[5:6], sums[6:7] = strips(back_two, (zero, zero, zero))
    out_copy = pltpu.make_async_copy(slope, layer_out, local_sems.at[0])
    out_copy.start()
    scattering("D0 Z1 B2 A3 P5")

    for n in range(3):
        at = slice(n * TILE, n * TILE + TILE)
        act[:, at] = dot_nt(seed[...], wo[at]).astype(BF16)
    scattering("S0 D1 Z2 B3 A4 P6")
    act_t[...] = attended[...].T
    for n in range(3):
        at = slice(n * TILE, n * TILE + TILE)
        wo[:, at] = dot_nn(act_t[...], seed[:, at]).astype(BF16)
    scattering("S1 D2 Z3 B4 A5 P7")
    strips(norm_one)
    norm_t[0:WIDTH] = norm[...].T
    out_copy.wait()

    key_sum, value_sum = outer.at[:, 0:128], outer.at[:, 128:256]
    pair_texts = (
        "S2 D3 Z4 B5 A6",
        "S3 D4 Z5 B6 A7",
        "S4 D5 Z6 B7",
        "S5 D6 Z7 A8",
        "S6 D7 B8",
        "S7 Z8 A9",
    )

    def backward_group(group, carry):
        def backward_pair(half, carry):
            pair = 2 * group + half
            for block in range(4):
                attend_back(
                    wide, pair, block, query_side, key_side, causal, attended, act, logsums, key_sum, value_sum
                )
            first = pair * 384
            wide[:, pl.ds(aligned(first + 128, 128), 128)] = key_sum[...].astype(BF16)
            wide[:, pl.ds(aligned(first + 256, 128), 128)] = value_sum[...].astype(BF16)
            for number, text in enumerate(pair_texts):
                pl.when(pair == number)(lambda text=text: scattering(text))
            return carry

        lax.fori_loop(0, 2, backward_pair, carry)
        for number in range(3):
            def weight_grads(number=number):
                partial = qkv_partials[number]
                rows = []
                for n in range(3):
                    at = slice(n * TILE, n * TILE + TILE)
                    columns = slice(number * WIDTH + n * TILE, number * WIDTH + n * TILE + TILE)
                    grad = dot_nn(norm_t[...], wide[:, columns])
                    partial[0:WIDTH, at] = grad[:WIDTH].astype(BF16)
                    rows.append(grad[WIDTH : WIDTH + 1])
                row = jnp.concatenate(rows, axis=1)
                at = slice(number * 256, number * 256 + 256)
                sums[2:3, at] = jnp.concatenate([row[:, 0:128], row[:, 384:512]], axis=1)
                sums[3:4, at] = jnp.concatenate([row[:, 256:384], row[:, 640:768]], axis=1)
                scattering(("P8", "P9", "P10")[number])

            pl.when(group == number)(weight_grads)
        return carry

    lax.fori_loop(0, 3, backward_group, 0)

    for n in range(3):
        at = slice(n * TILE, n * TILE + TILE)
        grad_norm[:, at] = dot_nt(wide[...], wq[at])
    scattering("D8 B9 A10")

    def back_one(rows, carry):
        xhat, scale = standardized(tokens[rows].astype(F32))
        grad = grad_norm[rows]
        middle[rows] += back_through_norm(grad, xhat, scale, gain_one)
        return carry[0] + column_sum(grad * xhat), carry[1] + column_sum(grad)

    sums[0:1], sums[1:2] = strips(back_one, (zero, zero))
    tokens_copy = pltpu.make_async_copy(middle, grad_tokens, local_sems.at[1])
    tokens_copy.start()
    sums[12:16] = jnp.zeros((4, WIDTH), F32)
    total = SmallSum(place, last_small[0], last_small[1], last_small[2:])
    total.begin(sums[...])
    scattering("S8 Z9 B10")
    total.middle()
    scattering("D9 Z10")
    total.last()
    scattering("S9 D10")
    small_out[...] = total.end()
    scattering("S10")
    for unit in leaving:
        unit.finish()
    tokens_copy.wait()


def layer(tokens, documents, cotangent, shards, small):
    vmem = pl.BlockSpec(memory_space=pltpu.VMEM)
    anywhere = pl.BlockSpec(memory_space=pl.ANY)
    out_shape = [jax.ShapeDtypeStruct((TOKENS, WIDTH), BF16), jax.ShapeDtypeStruct((TOKENS, WIDTH), F32)]
    out_shape += [jax.ShapeDtypeStruct((SHARD_ROWS[n], COLUMNS[n]), F32) for n in NAMES]
    out_shape.append(jax.ShapeDtypeStruct((16, WIDTH), F32))
    scratch = [pltpu.VMEM((32 * SHARD_ROWS[n], COLUMNS[n]), BF16) for n in NAMES]
    scratch += [
        pltpu.VMEM((TOKENS, QKV), BF16),
        pltpu.VMEM((TOKENS, WIDTH), BF16),
        pltpu.VMEM((WIDTH + 16, TOKENS), BF16),
        pltpu.VMEM((TOKENS, WIDTH), BF16),
        pltpu.VMEM((TOKENS, WIDTH), BF16),
        pltpu.VMEM((TOKENS, WIDTH), BF16),
        pltpu.VMEM((WIDTH, TOKENS), BF16),
        pltpu.VMEM((TOKENS, WIDTH), BF16),
        pltpu.VMEM((TOKENS, WIDTH), F32),
        pltpu.VMEM((TOKENS, WIDTH), F32),
        pltpu.VMEM((TOKENS, WIDTH), F32),
        pltpu.VMEM((HEADS, 1, TOKENS), F32),
        pltpu.VMEM((TOKENS, 128), BF16),
        pltpu.VMEM((TOKENS, 128), BF16),
        pltpu.VMEM((QUERY_ROWS, QUERY_ROWS), F32),
        pltpu.VMEM((16, WIDTH), F32),
        pltpu.VMEM((1, QKV), F32),
        pltpu.VMEM((1, QKV), F32),
        pltpu.VMEM((16, WIDTH), F32),
    ]
    for name, _, width in GATHER_UNITS:
        scratch += [pltpu.VMEM((padded(SHARD_ROWS[name]), width), BF16)] * 2
    for unit in SCATTER_UNITS:
        scratch += ScatterUnit.scratch(unit)
    scratch += [pltpu.SemaphoreType.DMA((len(GATHER_UNITS), GatherUnit.SEMS))] * 2
    scratch += [pltpu.SemaphoreType.DMA((len(SCATTER_UNITS), ScatterUnit.SEMS))] * 2
    scratch += SmallSum.scratch() + SmallSum.scratch()
    scratch.append(pltpu.SemaphoreType.DMA((2,)))
    return pl.pallas_call(
        layer_kernel,
        name="layer",
        out_shape=out_shape,
        in_specs=[vmem] * 8,
        out_specs=[anywhere] * 2 + [vmem] * 5,
        scratch_shapes=scratch,
        compiler_params=pltpu.CompilerParams(collective_id=0, has_side_effects=True, vmem_limit_bytes=VMEM_LIMIT),
        cost_estimate=pl.CostEstimate(flops=50 * 10**9, bytes_accessed=30 * 10**6, transcendentals=20 * 10**6),
    )(tokens, documents, cotangent, *[shards[n] for n in NAMES], small)


def device_number():
    return lax.axis_index("dp") * 8 + lax.axis_index("fsdp")


def spread(vectors, hidden_vector):
    number = device_number()
    stacked = jnp.stack([v.astype(F32) for v in vectors])
    placed = lax.dynamic_update_slice(jnp.zeros((16, WIDTH), F32), stacked, (0, 24 * number))
    return lax.dynamic_update_slice(placed, hidden_vector.astype(F32)[None], (8 + number // 8, 96 * (number % 8)))


def own_parts(total):
    number = device_number()
    parts = lax.dynamic_slice(total[:8], (0, 24 * number), (8, 24))
    hidden_part = lax.dynamic_slice(total, (8 + number // 8, 96 * (number % 8)), (1, 96))
    return [parts[i] for i in range(8)], hidden_part[0]


def fused_device(
    tokens,
    doc_ids,
    cotangent,
    first_gain,
    first_offset,
    qkv_weight,
    query_bias,
    value_bias,
    out_weight,
    out_bias,
    second_gain,
    second_offset,
    up_weight,
    up_bias,
    down_weight,
    down_bias,
):
    shards = {"qkv": qkv_weight, "out": out_weight, "up": up_weight, "down": down_weight}
    vectors = (
        first_gain,
        first_offset,
        query_bias,
        value_bias,
        out_bias,
        second_gain,
        second_offset,
        down_bias,
    )
    layer_out, grad_tokens, *matrices, total = layer(
        tokens, doc_ids, cotangent, shards, spread(vectors, up_bias)
    )
    parts, up_part = own_parts(total)
    return (
        layer_out,
        grad_tokens,
        parts[0],
        parts[1],
        matrices[0],
        parts[2],
        parts[3],
        matrices[1],
        parts[4],
        parts[5],
        parts[6],
        matrices[2],
        up_part,
        matrices[3],
        parts[7],
    )


def solution(mesh):
    placed = (
        P(("dp", "fsdp"), None),
        P(("dp", "fsdp"), None),
        P(("dp", "fsdp"), None),
        P(("dp", "fsdp")),
        P(("dp", "fsdp")),
        P(("dp", "fsdp"), None),
        P(("dp", "fsdp")),
        P(("dp", "fsdp")),
        P(("dp", "fsdp"), None),
        P(("dp", "fsdp")),
        P(("dp", "fsdp")),
        P(("dp", "fsdp")),
        P(("dp", "fsdp"), None),
        P(("dp", "fsdp")),
        P(("dp", "fsdp"), None),
        P(("dp", "fsdp")),
    )
    return jax.shard_map(
        fused_device if fits(mesh) else plain_device,
        mesh=mesh,
        in_specs=placed,
        out_specs=(
            P(("dp", "fsdp"), None),
            P(("dp", "fsdp"), None),
            P(("dp", "fsdp")),
            P(("dp", "fsdp")),
            P(("dp", "fsdp"), None),
            P(("dp", "fsdp")),
            P(("dp", "fsdp")),
            P(("dp", "fsdp"), None),
            P(("dp", "fsdp")),
            P(("dp", "fsdp")),
            P(("dp", "fsdp")),
            P(("dp", "fsdp"), None),
            P(("dp", "fsdp")),
            P(("dp", "fsdp"), None),
            P(("dp", "fsdp")),
        ),
        check_vma=False,
    )
```

```python
import jax
import jax.numpy as jnp
from jax import lax
from jax.experimental import pallas as pl
from jax.experimental.pallas import tpu as pltpu
from jax.sharding import PartitionSpec as P

HEADS = 12
HEAD_DIM = 64


norm_eps = 1e-05
branch_scale = 48.0 ** (-0.5)


def layer_norm(values, gains, offsets):
    average = jnp.mean(values, axis=-1, keepdims=True)
    centred = values - average
    variance = jnp.mean(centred * centred, axis=-1, keepdims=True)
    return centred * lax.rsqrt(variance + norm_eps) * gains + offsets


def scaled_norm(values, gains):
    return layer_norm(values, gains, 0.0)


def dense(former, latter):
    return jnp.dot(former, latter, preferred_element_type=jnp.float32)


def contract_rows(former, latter):
    return lax.dot_general(
        former, latter, (((0,), (0,)), ((), ())), preferred_element_type=jnp.float32
    )


def contract_cols(former, latter):
    return lax.dot_general(
        former, latter, (((1,), (1,)), ((), ())), preferred_element_type=jnp.float32
    )


def block_scores(queries, keys, documents, row_start, row_stop):
    score_scale = queries.shape[2] ** (-0.5)
    scores = (
        jnp.einsum(
            "qhd,khd->hqk",
            queries[row_start:row_stop],
            keys[:row_stop],
            preferred_element_type=jnp.float32,
        )
        * score_scale
    )
    positions = jnp.arange(row_stop)
    allowed = (documents[row_start:row_stop, None] == documents[None, :row_stop]) & (
        positions[None, :] <= positions[row_start:row_stop, None]
    )
    return jnp.where(allowed[None], scores, -1e30)


def attend_row(queries, keys, values, documents):
    seq_len = queries.shape[0]
    block_rows = min(512, seq_len)
    outputs = []
    logsums = []
    for row_start in range(0, seq_len, block_rows):
        row_stop = row_start + block_rows
        scores = block_scores(queries, keys, documents, row_start, row_stop)
        highest = jnp.max(scores, axis=-1, keepdims=True)
        raised = jnp.exp(scores - highest)
        summed = jnp.sum(raised, axis=-1, keepdims=True)
        weights = (raised / summed).astype(jnp.bfloat16)
        outputs.append(
            jnp.einsum(
                "hqk,khd->qhd", weights, values[:row_stop], preferred_element_type=jnp.float32
            )
        )
        logsums.append((highest + jnp.log(summed))[..., 0])
    return (jnp.concatenate(outputs, axis=0).astype(jnp.bfloat16), jnp.concatenate(logsums, axis=1))


def attend_row_back(queries, keys, values, documents, logsums, grad_out):
    seq_len = queries.shape[0]
    block_rows = min(512, seq_len)
    score_scale = queries.shape[2] ** (-0.5)
    query_parts = []
    grad_keys = jnp.zeros(keys.shape, jnp.float32)
    grad_values = jnp.zeros(values.shape, jnp.float32)
    for row_start in range(0, seq_len, block_rows):
        row_stop = row_start + block_rows
        scores = block_scores(queries, keys, documents, row_start, row_stop)
        probs = jnp.exp(scores - logsums[:, row_start:row_stop, None])
        incoming = grad_out[row_start:row_stop]
        grad_probs = jnp.einsum(
            "qhd,khd->hqk", incoming, values[:row_stop], preferred_element_type=jnp.float32
        )
        inner_sum = jnp.sum(probs * grad_probs, axis=-1, keepdims=True)
        grad_scores = (probs * (grad_probs - inner_sum)).astype(jnp.bfloat16)
        query_parts.append(
            jnp.einsum(
                "hqk,khd->qhd", grad_scores, keys[:row_stop], preferred_element_type=jnp.float32
            )
            * score_scale
        )
        key_term = (
            jnp.einsum(
                "hqk,qhd->khd",
                grad_scores,
                queries[row_start:row_stop],
                preferred_element_type=jnp.float32,
            )
            * score_scale
        )
        value_term = jnp.einsum(
            "hqk,qhd->khd", probs.astype(jnp.bfloat16), incoming, preferred_element_type=jnp.float32
        )
        padding = ((0, seq_len - row_stop), (0, 0), (0, 0))
        grad_keys = grad_keys + jnp.pad(key_term, padding)
        grad_values = grad_values + jnp.pad(value_term, padding)
    return (jnp.concatenate(query_parts, axis=0), grad_keys, grad_values)


def plain_device(
    tokens,
    doc_ids,
    cotangent,
    first_gain,
    first_offset,
    qkv_weight,
    query_bias,
    value_bias,
    out_weight,
    out_bias,
    second_gain,
    second_offset,
    up_weight,
    up_bias,
    down_weight,
    down_bias,
):
    attn_full = (
        lax.all_gather(first_gain, ("dp", "fsdp"), axis=0, tiled=True),
        lax.all_gather(first_offset, ("dp", "fsdp"), axis=0, tiled=True),
        lax.all_gather(qkv_weight, ("dp", "fsdp"), axis=0, tiled=True),
        lax.all_gather(query_bias, ("dp", "fsdp"), axis=0, tiled=True),
        lax.all_gather(value_bias, ("dp", "fsdp"), axis=0, tiled=True),
        lax.all_gather(out_weight, ("dp", "fsdp"), axis=0, tiled=True),
        lax.all_gather(out_bias, ("dp", "fsdp"), axis=0, tiled=True),
    )
    model_width = tokens.shape[1]
    rows_here = doc_ids.shape[0]
    seq_len = doc_ids.shape[1]
    inputs = tokens.astype(jnp.float32)
    gain_one = attn_full[0].astype(jnp.float32)
    normed_one = layer_norm(inputs, gain_one, attn_full[1].astype(jnp.float32)).astype(jnp.bfloat16)
    projected = dense(normed_one, attn_full[2])
    queries = (projected[:, :model_width] + attn_full[3].astype(jnp.float32)).astype(jnp.bfloat16)
    keys = projected[:, model_width : 2 * model_width].astype(jnp.bfloat16)
    values = (projected[:, 2 * model_width :] + attn_full[4].astype(jnp.float32)).astype(
        jnp.bfloat16
    )
    row_shape = (rows_here, seq_len, HEADS, HEAD_DIM)
    queries = queries.reshape(row_shape)
    keys = keys.reshape(row_shape)
    values = values.reshape(row_shape)
    attended, logsums = lax.map(
        lambda row_item: attend_row(*row_item), (queries, keys, values, doc_ids)
    )
    attended = attended.reshape(-1, model_width)
    branch = dense(attended, attn_full[5]) + attn_full[6].astype(jnp.float32)
    middle = inputs + branch_scale * branch
    mlp_full = (
        lax.all_gather(second_gain, ("dp", "fsdp"), axis=0, tiled=True),
        lax.all_gather(second_offset, ("dp", "fsdp"), axis=0, tiled=True),
        lax.all_gather(up_weight, ("dp", "fsdp"), axis=0, tiled=True),
        lax.all_gather(up_bias, ("dp", "fsdp"), axis=0, tiled=True),
        lax.all_gather(down_weight, ("dp", "fsdp"), axis=0, tiled=True),
        lax.all_gather(down_bias, ("dp", "fsdp"), axis=0, tiled=True),
    )
    gain_two = mlp_full[0].astype(jnp.float32)
    normed_two = layer_norm(middle, gain_two, mlp_full[1].astype(jnp.float32)).astype(jnp.bfloat16)
    hidden = dense(normed_two, mlp_full[2]) + mlp_full[3].astype(jnp.float32)
    active, gelu_back = jax.vjp(lambda pre_act: jax.nn.gelu(pre_act, approximate=True), hidden)
    active = active.astype(jnp.bfloat16)
    outer = dense(active, mlp_full[4]) + mlp_full[5].astype(jnp.float32)
    layer_out = (middle + branch_scale * outer).astype(jnp.bfloat16)
    mlp_back = (
        lax.all_gather(second_gain, ("dp", "fsdp"), axis=0, tiled=True),
        lax.all_gather(up_weight, ("dp", "fsdp"), axis=0, tiled=True),
        lax.all_gather(down_weight, ("dp", "fsdp"), axis=0, tiled=True),
    )
    seed = cotangent.astype(jnp.float32)
    grad_outer = (branch_scale * seed).astype(jnp.bfloat16)
    grad_down_bias = jnp.sum(grad_outer.astype(jnp.float32), axis=0)
    grad_down_weight = contract_rows(active, grad_outer)
    grad_active = contract_cols(grad_outer, mlp_back[2])
    grad_hidden = gelu_back(grad_active)[0].astype(jnp.bfloat16)
    grad_up_bias = jnp.sum(grad_hidden.astype(jnp.float32), axis=0)
    grad_up_weight = contract_rows(normed_two, grad_hidden)
    grad_normed_two = contract_cols(grad_hidden, mlp_back[1])
    _, norm_two_back = jax.vjp(scaled_norm, middle, mlp_back[0].astype(jnp.float32))
    grad_middle_part, grad_second_gain = norm_two_back(grad_normed_two)
    grad_second_offset = jnp.sum(grad_normed_two, axis=0)
    grad_middle = seed + grad_middle_part
    mlp_shares = (
        grad_second_gain,
        grad_second_offset,
        grad_up_weight,
        grad_up_bias,
        grad_down_weight,
        grad_down_bias,
    )
    attn_back = (
        lax.all_gather(first_gain, ("dp", "fsdp"), axis=0, tiled=True),
        lax.all_gather(qkv_weight, ("dp", "fsdp"), axis=0, tiled=True),
        lax.all_gather(out_weight, ("dp", "fsdp"), axis=0, tiled=True),
    )
    grad_branch = (branch_scale * grad_middle).astype(jnp.bfloat16)
    grad_out_bias = jnp.sum(grad_branch.astype(jnp.float32), axis=0)
    grad_out_weight = contract_rows(attended, grad_branch)
    grad_attended = contract_cols(grad_branch, attn_back[2]).astype(jnp.bfloat16).reshape(row_shape)
    grad_queries, grad_keys, grad_values = lax.map(
        lambda row_item: attend_row_back(*row_item),
        (queries, keys, values, doc_ids, logsums, grad_attended),
    )
    grad_projected = jnp.concatenate(
        [
            grad_queries.reshape(-1, model_width),
            grad_keys.reshape(-1, model_width),
            grad_values.reshape(-1, model_width),
        ],
        axis=1,
    ).astype(jnp.bfloat16)
    grad_wide = grad_projected.astype(jnp.float32)
    grad_query_bias = jnp.sum(grad_wide[:, :model_width], axis=0)
    grad_value_bias = jnp.sum(grad_wide[:, 2 * model_width :], axis=0)
    grad_qkv_weight = contract_rows(normed_one, grad_projected)
    grad_normed_one = contract_cols(grad_projected, attn_back[1])
    _, norm_one_back = jax.vjp(scaled_norm, inputs, attn_back[0].astype(jnp.float32))
    grad_input_part, grad_first_gain = norm_one_back(grad_normed_one)
    grad_first_offset = jnp.sum(grad_normed_one, axis=0)
    grad_tokens = grad_middle + grad_input_part
    every_share = (
        lax.psum_scatter(grad_second_gain, ("dp", "fsdp"), scatter_dimension=0, tiled=True),
        lax.psum_scatter(grad_second_offset, ("dp", "fsdp"), scatter_dimension=0, tiled=True),
        lax.psum_scatter(grad_up_weight, ("dp", "fsdp"), scatter_dimension=0, tiled=True),
        lax.psum_scatter(grad_up_bias, ("dp", "fsdp"), scatter_dimension=0, tiled=True),
        lax.psum_scatter(grad_down_weight, ("dp", "fsdp"), scatter_dimension=0, tiled=True),
        lax.psum_scatter(grad_down_bias, ("dp", "fsdp"), scatter_dimension=0, tiled=True),
        lax.psum_scatter(grad_first_gain, ("dp", "fsdp"), scatter_dimension=0, tiled=True),
        lax.psum_scatter(grad_first_offset, ("dp", "fsdp"), scatter_dimension=0, tiled=True),
        lax.psum_scatter(grad_qkv_weight, ("dp", "fsdp"), scatter_dimension=0, tiled=True),
        lax.psum_scatter(grad_query_bias, ("dp", "fsdp"), scatter_dimension=0, tiled=True),
        lax.psum_scatter(grad_value_bias, ("dp", "fsdp"), scatter_dimension=0, tiled=True),
        lax.psum_scatter(grad_out_weight, ("dp", "fsdp"), scatter_dimension=0, tiled=True),
        lax.psum_scatter(grad_out_bias, ("dp", "fsdp"), scatter_dimension=0, tiled=True),
    )
    mlp_shares = every_share[:6]
    attn_shares = every_share[6:]
    return (
        layer_out,
        grad_tokens,
        attn_shares[0],
        attn_shares[1],
        attn_shares[2],
        attn_shares[3],
        attn_shares[4],
        attn_shares[5],
        attn_shares[6],
        mlp_shares[0],
        mlp_shares[1],
        mlp_shares[2],
        mlp_shares[3],
        mlp_shares[4],
        mlp_shares[5],
    )


MESH = pl.DeviceIdType.MESH
F32 = jnp.float32
BF16 = jnp.bfloat16
WIDTH = 768
HIDDEN = 3072
TOKENS = 1024
QKV = 3 * WIDTH
PAIRS = 6
QUERY_ROWS = 256
KEY_WINDOWS = ((0, 256), (0, 512), (0, 768), (256, 1024))
DOCUMENTS = 6
FAR_BELOW = 2.0**100
STRIP = 128
TILE = 256
VMEM_LIMIT = 63 * 2**20
GELU_A = 0.7978845608028654
GELU_B = 0.044715

GATHER_UNITS = (("qkv", 0), ("qkv", 1), ("qkv", 2), ("out", 0)) + tuple(
    (name, part) for part in range(4) for name in ("up", "down")
)
SCATTER_UNITS = GATHER_UNITS[4:] + GATHER_UNITS[3:4] + GATHER_UNITS[:3]
ROWS = 24
HALF = 384
SHARDS = {"qkv": (24, 2304), "out": (24, 768), "up": (24, 3072), "down": (96, 768)}
NAMES = ("qkv", "out", "up", "down")
DEVICES = 32
HIDDEN_PARTS = 4


def fits(mesh):
    return mesh.shape["dp"] == 4 and mesh.shape["fsdp"] == 8


def aligned(value, step):
    return pl.multiple_of(value, step)


def dot_nt(a, b):
    return lax.dot_general(a, b, (((1,), (1,)), ((), ())), preferred_element_type=F32)


def dot_nn(a, b):
    return lax.dot_general(a, b, (((1,), (0,)), ((), ())), preferred_element_type=F32)


def dot_tn(a, b):
    return lax.dot_general(a, b, (((0,), (0,)), ((), ())), preferred_element_type=F32)


class Place:
    def __init__(self):
        self.dp = lax.axis_index("dp")
        self.fsdp = lax.axis_index("fsdp")
        self.core = lax.rem(self.fsdp, 2)
        self.z = lax.div(self.fsdp, 2)
        x = lax.rem(self.dp, 2)
        y = lax.div(self.dp, 2)
        self.dp_x = y * 2 + (1 - x)
        self.dp_y = (1 - y) * 2 + x
        self.dp_far = 3 - self.dp
        core = self.core
        self.near = self.dp_x * (1 - core) + self.dp_y * core
        self.next = self.dp_y * (1 - core) + self.dp_x * core
        self.chip = self.dp * 4 + self.z
        self.number = self.dp * 8 + self.fsdp
        self.partner = (self.dp, self.z * 2 + (1 - core))
        self.at_near = (self.near, self.fsdp)
        self.at_next = (self.next, self.fsdp)

    def along_z(self, step):
        z = lax.rem(self.z + step, 4)
        return (self.dp, z * 2 + self.core)

    def greet(self):
        barrier = pltpu.get_barrier_semaphore()
        others = [self.partner, (self.dp_x, self.fsdp), (self.dp_y, self.fsdp), (self.dp_far, self.fsdp)]
        others += [self.along_z(step) for step in (1, 2, 3)]
        for other in others:
            pl.semaphore_signal(barrier, inc=1, device_id=other, device_id_type=MESH)
        pl.semaphore_wait(barrier, len(others))


def remote(source, target, sems, index, device):
    return pltpu.make_async_remote_copy(
        src_ref=source,
        dst_ref=target,
        send_sem=sems[0].at[index],
        recv_sem=sems[1].at[index],
        device_id=device,
        device_id_type=MESH,
    )


class SmallSum:
    def __init__(self, place, source, target, buffers, landed, send_sems, recv_sems):
        self.place, self.source, self.target = place, source, target
        self.buffers, self.landed, self.sems = buffers, landed, (send_sems, recv_sems)

    @staticmethod
    def scratch(shape, dtype):
        return [
            pltpu.VMEM((3, *shape), dtype),
            pltpu.VMEM((7, *shape), dtype),
            pltpu.SemaphoreType.DMA((7,)),
            pltpu.SemaphoreType.DMA((7,)),
        ]

    def copies(self, stage):
        p = self.place
        if stage == 0:
            devices = [p.partner]
        elif stage == 1:
            devices = [(dp, p.fsdp) for dp in (p.dp_x, p.dp_y, p.dp_far)]
        else:
            devices = [p.along_z(step) for step in (1, 2, 3)]
        first = (0, 1, 4)[stage]
        return [
            remote(self.buffers.at[stage], self.landed.at[first + i], self.sems, first + i, device)
            for i, device in enumerate(devices)
        ]

    def begin(self):
        self.buffers[0] = self.source[...].astype(self.buffers.dtype)
        for copy in self.copies(0):
            copy.start()

    def middle(self):
        for copy in self.copies(0):
            copy.wait()
        self.buffers[1] = self.buffers[0] + self.landed[0]
        for copy in self.copies(1):
            copy.start()

    def later(self):
        for copy in self.copies(1):
            copy.wait()
        self.buffers[2] = (self.buffers[1] + self.landed[1]) + (self.landed[2] + self.landed[3])
        for copy in self.copies(2):
            copy.start()

    def end(self):
        for copy in self.copies(2):
            copy.wait()
        total = (self.buffers[2] + self.landed[4]) + (self.landed[5] + self.landed[6])
        self.target[...] = total.astype(self.target.dtype)


class GatherUnit:
    SEMS = 11

    def __init__(self, place, unit, shard, full, pair_out, pair_in, send_sems, recv_sems):
        self.place = place
        self.name, self.part = unit
        self.shard, self.full = shard, full
        self.pair_out, self.pair_in = pair_out, pair_in
        self.sems = (send_sems, recv_sems)

    def columns_of(self, core):
        if self.name == "qkv":
            start = 2 * self.part * 128 + 128 * core
            parts = [self.shard[:, pl.ds(aligned(start + WIDTH * i, 128), 128)] for i in range(3)]
            return jnp.concatenate(parts, axis=1).astype(F32)
        start = WIDTH * self.part if self.name == "up" else 0
        columns = self.shard[:, pl.ds(aligned(start + HALF * core, 128), HALF)].astype(F32)
        return columns[ROWS * self.part : ROWS * self.part + ROWS] if self.name == "down" else columns

    def rows_at(self, first, count):
        columns = pl.ds(aligned(HALF * self.place.core, 128), HALF)
        return self.full.at[pl.ds(aligned(first, 16), count), columns]

    def group(self, dp):
        return self.rows_at(dp * (8 * ROWS), 8 * ROWS)

    def block(self, dp=None):
        chip = self.place.chip if dp is None else dp * 4 + self.place.z
        return self.rows_at(chip * (2 * ROWS), 2 * ROWS)

    def copy(self, index):
        p = self.place
        if index == 0:
            return remote(self.pair_out, self.pair_in, self.sems, 0, p.partner)
        if index < 4:
            return remote(self.block(), self.block(), self.sems, index, p.along_z(index))
        dp = (p.dp, p.dp, p.near, p.dp, p.near, p.next, p.dp_far)[index - 4]
        device = p.at_near if index == 4 else p.at_next if index < 7 else p.partner
        return remote(self.group(dp), self.group(dp), self.sems, index, device)

    def start(self, *indices):
        for index in indices:
            self.copy(index).start()

    def landed(self, *indices):
        for index in indices:
            self.copy(index).wait_recv()

    def pair(self):
        self.pair_out[0:ROWS] = self.columns_of(1 - self.place.core).astype(BF16)
        self.pair_out[ROWS:] = jnp.zeros((32 - ROWS, HALF), BF16)
        self.start(0)

    def assemble(self):
        self.landed(0)
        own = self.columns_of(self.place.core)
        came = self.pair_in[0:ROWS].astype(F32)
        first = self.place.core == 0
        block = jnp.concatenate([jnp.where(first, own, came), jnp.where(first, came, own)], axis=0)
        self.block()[...] = block.astype(BF16)

    def along_z(self):
        self.assemble()
        self.start(1, 2, 3)

    def to_near(self):
        self.landed(1, 2, 3)
        self.start(4, 7)

    def to_next(self):
        self.landed(4)
        self.start(5, 6, 8)

    def to_core(self):
        self.landed(5)
        self.start(9)
        self.landed(6)
        self.start(10)

    def arrived(self):
        self.landed(7, 8, 9, 10)

    def finish(self):
        for index in range(self.SEMS):
            self.copy(index).wait_send()


class ScatterUnit:
    SEMS = 8

    def __init__(self, place, unit, partial, target, halves, from_next, from_near, from_z, pair, send_sems, recv_sems):
        self.place = place
        self.name, self.part = unit
        self.partial, self.target = partial, target
        self.halves, self.from_next, self.from_near = halves, from_next, from_near
        self.from_z, self.pair_buffer = from_z, pair
        self.sems = (send_sems, recv_sems)

    @staticmethod
    def scratch():
        return [
            pltpu.VMEM((WIDTH, HALF), BF16),
            pltpu.VMEM((2, 8 * ROWS, HALF), BF16),
            pltpu.VMEM((8 * ROWS, HALF), BF16),
            pltpu.VMEM((3, 2 * ROWS, HALF), BF16),
            pltpu.VMEM((3, ROWS, HALF), F32),
        ]

    def columns(self, core):
        return pl.ds(aligned(HALF * core, 128), HALF)

    def group(self, dp):
        return self.halves.at[pl.ds(aligned(dp * (8 * ROWS), 16), 8 * ROWS)]

    def z_block(self, step, dp=None):
        chip = (self.place.dp if dp is None else dp) * 4 + lax.rem(self.place.z + step, 4)
        return self.halves.at[pl.ds(aligned(chip * (2 * ROWS), 16), 2 * ROWS)]

    def copy(self, index):
        p = self.place
        if index == 0:
            source = self.partial.at[pl.ds(0, WIDTH), self.columns(1 - p.core)]
            return remote(source, self.halves, self.sems, 0, p.partner)
        if index < 3:
            dp = (p.next, p.dp_far)[index - 1]
            return remote(self.group(dp), self.from_next.at[index - 1], self.sems, index, p.at_next)
        if index == 3:
            return remote(self.group(p.near), self.from_near, self.sems, 3, p.at_near)
        if index < 7:
            step = index - 3
            return remote(self.z_block(step), self.from_z.at[step - 1], self.sems, index, p.along_z(step))
        return remote(self.pair_buffer.at[0], self.pair_buffer.at[2], self.sems, 7, p.partner)

    def start(self, *indices):
        for index in indices:
            self.copy(index).start()

    def landed(self, *indices):
        for index in indices:
            self.copy(index).wait_recv()

    def add(self, former, latter, rows):
        step = 192

        def body(index, carry):
            at = pl.ds(aligned(index * step, 16), step)
            former[at] = (former[at].astype(F32) + latter(at).astype(F32)).astype(BF16)
            return carry

        lax.fori_loop(0, rows // step, body, 0)

    def to_partner(self):
        self.start(0)

    def to_next(self):
        self.landed(0)
        mine = self.columns(self.place.core)
        self.add(self.halves, lambda at: self.partial[at, mine], WIDTH)
        self.start(1, 2)

    def to_near(self):
        p = self.place
        self.landed(1, 2)
        self.add(self.group(p.near), lambda at: self.from_next[1, at], 8 * ROWS)
        self.start(3)
        self.add(self.group(p.dp), lambda at: self.from_next[0, at], 8 * ROWS)

    def along_z(self):
        self.landed(3)
        self.add(self.group(self.place.dp), lambda at: self.from_near[at], 8 * ROWS)
        self.start(4, 5, 6)

    def to_pair(self):
        self.landed(4, 5, 6)
        came = [self.from_z[i].astype(F32) for i in range(3)]
        self.halve((self.z_block(0)[...].astype(F32) + came[0]) + (came[1] + came[2]))
        self.start(7)

    def halve(self, block):
        first = self.place.core == 0
        self.pair_buffer[0] = jnp.where(first, block[ROWS:], block[:ROWS])
        self.pair_buffer[1] = jnp.where(first, block[:ROWS], block[ROWS:])

    def store(self):
        self.landed(7)
        self.put()

    def put(self):
        for source, core in ((1, self.place.core), (2, 1 - self.place.core)):
            if self.name == "qkv":
                start = 2 * self.part * 128 + 128 * core
                for i in range(3):
                    columns = pl.ds(aligned(start + WIDTH * i, 128), 128)
                    self.target[:, columns] = self.pair_buffer[source, :, 128 * i : 128 * i + 128]
            elif self.name == "down":
                self.target[ROWS * self.part : ROWS * self.part + ROWS, self.columns(core)] = self.pair_buffer[source]
            else:
                start = WIDTH * self.part + HALF * core
                self.target[:, pl.ds(aligned(start, 128), HALF)] = self.pair_buffer[source]

    def finish(self):
        for index in range(self.SEMS):
            self.copy(index).wait_send()


STAGES = {
    "P": "to_partner",
    "A": "to_next",
    "B": "to_near",
    "Z": "along_z",
    "D": "to_pair",
    "S": "store",
    "p": "pair",
    "z": "along_z",
    "n": "to_near",
    "x": "to_next",
    "c": "to_core",
    "r": "arrived",
    "b": "begin",
    "m": "middle",
    "l": "later",
    "e": "end",
}


def strips(body, carry=0):
    def run(index, carry):
        return body(pl.ds(aligned(index * STRIP, STRIP), STRIP), carry)

    return lax.fori_loop(0, TOKENS // STRIP, run, carry)


def standardized(values):
    average = jnp.mean(values, axis=-1, keepdims=True)
    centred = values - average
    variance = jnp.mean(centred * centred, axis=-1, keepdims=True)
    scale = lax.rsqrt(variance + norm_eps)
    return centred * scale, scale


def back_through_norm(grad, xhat, scale, gains):
    lifted = grad * gains
    return scale * (
        lifted
        - jnp.mean(lifted, axis=-1, keepdims=True)
        - xhat * jnp.mean(lifted * xhat, axis=-1, keepdims=True)
    )


def column_sum(values):
    return jnp.sum(values, axis=0, keepdims=True)


def gelu_and_slope(h):
    square = h * h
    bent = GELU_A + GELU_A * GELU_B * square
    gate = 0.5 + 0.5 * jnp.tanh(h * bent)
    active = h * gate
    slope = gate + active * (1.0 - gate) * (6.0 * bent - 4.0 * GELU_A)
    return active, slope


def document_lanes(documents, query_side, key_side):
    lane = lax.rem(lax.broadcasted_iota(jnp.int32, (TOKENS, 128), 1), 64)
    own = jnp.broadcast_to(documents.astype(F32), (128, TOKENS)).T == lane.astype(F32)
    query_side[...] = jnp.where(own, 1.0, 0.0).astype(BF16)
    key_side[...] = jnp.where(own | (lane >= DOCUMENTS), 0.0, -FAR_BELOW).astype(BF16)


def causal_corner(causal):
    key = lax.broadcasted_iota(jnp.int32, (QUERY_ROWS, QUERY_ROWS), 0)
    query = lax.broadcasted_iota(jnp.int32, (QUERY_ROWS, QUERY_ROWS), 1)
    causal[...] = jnp.where(key <= query, 0.0, -FAR_BELOW)


class Pair:
    def __init__(self, wide, pair, block, query_side, key_side):
        start, stop = KEY_WINDOWS[block]
        self.keys = pl.ds(start, stop - start)
        self.rows = pl.ds(block * QUERY_ROWS, QUERY_ROWS)
        first = pair * 384
        self.at = [pl.ds(aligned(first + 128 * i, 128), 128) for i in range(3)]
        self.q = wide[self.rows, self.at[0]]
        self.k = wide[self.keys, self.at[1]]
        self.v = wide[self.keys, self.at[2]]
        self.query_side, self.key_side = query_side[self.rows], key_side[self.keys]
        self.start, self.stop = start, stop

    def choose(self, head, inside, outside):
        low = lax.broadcasted_iota(jnp.int32, inside.shape, 1) < 64
        return jnp.where(low, inside, outside) if head == 0 else jnp.where(low, outside, inside)

    def only(self, head, values):
        return self.choose(head, values, jnp.zeros_like(values))

    def scores(self, head, causal):
        scores = dot_nt(self.choose(head, self.k, self.key_side), self.choose(head, self.q, self.query_side))
        wide = self.stop - self.start - QUERY_ROWS
        corner = scores[wide:] + causal[...]
        return jnp.concatenate([scores[:wide], corner], axis=0) if wide else corner


def attend(wide, pair, block, query_side, key_side, causal, attended, logsums):
    p = Pair(wide, pair, block, query_side, key_side)
    weights, sums = [], []
    for head in range(2):
        scores = p.scores(head, causal)
        highest = jnp.max(scores, axis=0, keepdims=True)
        raised = jnp.exp(scores - highest)
        summed = column_sum(raised)
        weights.append(raised.astype(BF16))
        sums.append(jnp.broadcast_to(summed, (HEAD_DIM, QUERY_ROWS)))
        logsums[2 * pair + head, :, p.rows] = highest + jnp.log(summed)
    values = jnp.concatenate([p.only(head, p.v) for head in range(2)], axis=0)
    out = dot_tn(values, jnp.concatenate(weights, axis=0)) / jnp.concatenate(sums, axis=0)
    attended[p.rows, pl.ds(aligned(pair * 128, 128), 128)] = out.T.astype(BF16)


def attend_back(wide, pair, block, query_side, key_side, causal, attended, grad_attended, logsums, key_sum, value_sum):
    p = Pair(wide, pair, block, query_side, key_side)
    features = pl.ds(aligned(pair * 128, 128), 128)
    incoming = grad_attended[p.rows, features]
    inner = (incoming.astype(F32) * attended[p.rows, features].astype(F32)).T
    probs, slopes = [], []
    for head in range(2):
        delta = column_sum(inner[64 * head : 64 * head + 64])
        prob = jnp.exp(p.scores(head, causal) - logsums[2 * pair + head, :, p.rows])
        grad_prob = dot_nt(p.v, p.only(head, incoming))
        probs.append(prob.astype(BF16))
        slopes.append((prob * (grad_prob - delta)).astype(BF16))
    both = lambda values: jnp.concatenate([p.only(head, values) for head in range(2)], axis=0)
    value_part = dot_nn(jnp.concatenate(probs, axis=1), both(incoming))
    key_part = dot_nn(jnp.concatenate(slopes, axis=1), both(p.q))
    query_part = dot_tn(both(p.k), jnp.concatenate(slopes, axis=0))
    wide[p.rows, p.at[0]] = (query_part.T * HEAD_DIM**-0.5).astype(BF16)
    inside = p.stop - p.start - QUERY_ROWS
    if inside:
        earlier = pl.ds(p.start, inside)
        key_sum[earlier] += key_part[:inside]
        value_sum[earlier] += value_part[:inside]
    newest = pl.ds(p.stop - QUERY_ROWS, QUERY_ROWS)
    key_sum[newest] = key_part[inside:]
    value_sum[newest] = value_part[inside:]


PLAN = {
    "greet": "b0 p0 p1 p2",
    "packed": "m0 z0 p3 p4 p5",
    "group0": "n0 z3 p6 n1 z4 p7 x0 n2 z5 p8 x1 n3 z6 p9 c0 x2 n4 z7 p10 r0",
    "pair0": "x3",
    "pair1": "c1 x4",
    "group1": "n5 z8 p11 n6 z9 r1",
    "qkv1": "c2",
    "pair2": "n7 z10",
    "pair3": "c3 x5",
    "group2": "r2",
    "qkv2": "x6",
    "pair5": "c4 x7",
    "joined": "r3",
    "branch": "n8 z11",
    "norm": "c5 n9 n10",
    "step0": "r4 r5",
    "hidden0": "c6 x8 x9",
    "outer0": "c7 n11",
    "grads0": "x10 P0 P1",
    "step1": "r6 r7",
    "hidden1": "c8 x11 A0",
    "outer1": "c9 A1",
    "grads1": "c10 P2 P3",
    "step2": "r8 r9",
    "hidden2": "c11 A2 A3",
    "outer2": "B0",
    "grads2": "B1 P4 P5",
    "step3": "r10 r11",
    "hidden3": "Z0 B2 A4 A5",
    "outer3": "Z1",
    "grads3": "D0 Z2 B3 P6 P7",
    "back": "D1 B4 S0 A6 A7",
    "attended": "D2 Z3 S1",
    "out": "S2 P8",
    "first": "Z4 B5 A8 b1",
    "pair_back0": "D3 B6 m1",
    "pair_back1": "D4 Z5 B7 S3 l1",
    "qkv_grads0": "Z6 S4 P9",
    "pair_back2": "D5 Z7 B8 A9 e1",
    "pair_back3": "D6 S5",
    "qkv_grads1": "Z8 D7 S6 P10",
    "pair_back4": "B9 S7 A10",
    "pair_back5": "D8",
    "qkv_grads2": "Z9 S8 P11",
    "tokens0": "B10",
    "tokens1": "A11",
    "half": "b2 D9 Z10",
    "last": "m2 S9 B11 l2 Z11 D10 S10 D11 S11 e2",
    "documents": "l0 z1 z2",
    "vectors": "e0",
}


def layer_kernel(*refs):
    refs = list(refs)

    def take(count):
        taken = refs[:count]
        del refs[:count]
        return taken

    tokens_in, documents, cotangent_in = take(3)
    shards = dict(zip(NAMES, take(4)))
    (packed,) = take(1)
    layer_out, grad_tokens = take(2)
    targets = dict(zip(NAMES, take(4)))
    (small_out,) = take(1)
    wq, wo, wu, wd = take(4)
    tokens, cotangent, wide, norm, norm_t, attended, seed, act, act_t, slope = take(10)
    middle, outer, grad_norm = take(3)
    logsums, query_side, key_side, causal, vectors, qkv_bias, qkv_scale, early = take(8)
    late, up_shard, up_target = take(3)
    pair_buffers = take(2 * len(GATHER_UNITS))
    scatter_buffers = take(5 * len(SCATTER_UNITS))
    gather_sems, scatter_sems = take(2), take(2)
    small_refs = [take(4) for _ in range(3)]
    (local_sems,) = take(1)

    place = Place()
    up_natural, shards["up"] = shards["up"], up_shard
    up_out, targets["up"] = targets["up"], up_target

    def part(index):
        return slice(WIDTH * index, WIDTH * index + WIDTH)

    def whole(name, index):
        if name == "out":
            return wo
        return wd.at[part(index)] if name == "down" else {"qkv": wq, "up": wu}[name].at[:, part(index)]

    coming = [
        GatherUnit(
            place,
            unit,
            shards[unit[0]],
            whole(*unit),
            *pair_buffers[2 * i : 2 * i + 2],
            gather_sems[0].at[i],
            gather_sems[1].at[i],
        )
        for i, unit in enumerate(GATHER_UNITS)
    ]
    qkv_partials = (slope.at[0:WIDTH], act_t.at[:, 0:WIDTH], norm.at[0:WIDTH])
    leaving = [
        ScatterUnit(
            place,
            unit,
            qkv_partials[unit[1]] if unit[0] == "qkv" else whole(*unit),
            targets[unit[0]],
            *scatter_buffers[5 * i : 5 * i + 5],
            scatter_sems[0].at[i],
            scatter_sems[1].at[i],
        )
        for i, unit in enumerate(SCATTER_UNITS)
    ]

    vector_sums = [
        SmallSum(place, source, target, *refs)
        for source, target, refs in zip((vectors, early, late), (vectors, early, late), small_refs)
    ]

    def run(text):
        for step in text.split():
            units = vector_sums if step[0] in "bmle" else coming if step[0].islower() else leaving
            getattr(units[int(step[1:])], STAGES[step[0]])()

    def after(name, index=None, count=0):
        if index is None:
            run(PLAN.get(name, ""))
            return
        for number in range(count):
            text = PLAN.get(name + str(number), "")
            if text:
                pl.when(index == number)(lambda text=text: run(text))

    loads = [
        pltpu.make_async_copy(source, target, local_sems.at[2 + i])
        for i, (source, target) in enumerate(((tokens_in, tokens), (cotangent_in, cotangent)))
    ]
    for load in loads:
        load.start()
    vectors[...] = jnp.zeros_like(vectors)
    for row in range(12):
        vectors[row : row + 1, 0:ROWS] = packed[:, ROWS * row : ROWS * row + ROWS]
    vectors[...] = pltpu.roll(vectors[...], place.number * ROWS, 1)
    place.greet()
    after("greet")
    up = up_natural[...].astype(F32)
    step = ROWS * HIDDEN_PARTS
    up_shard[...] = jnp.concatenate(
        [up[:, step * d + ROWS * j : step * d + ROWS * j + ROWS] for j in range(HIDDEN_PARTS) for d in range(DEVICES)],
        axis=1,
    ).astype(BF16)
    after("packed")
    document_lanes(documents[...], query_side, key_side)
    causal_corner(causal)
    after("documents")
    for load in loads:
        load.wait()
    after("vectors")
    gain_one, offset_one = vectors[0:1], vectors[1:2]
    for pair in range(PAIRS):
        at = slice(128 * pair, 128 * pair + 128)
        first = 384 * pair
        qkv_bias[:, first : first + 128] = vectors[2:3, at]
        qkv_bias[:, first + 128 : first + 256] = jnp.zeros((1, 128), F32)
        qkv_bias[:, first + 256 : first + 384] = vectors[3:4, at]
        qkv_scale[:, first : first + 128] = jnp.full((1, 128), HEAD_DIM**-0.5, F32)
        qkv_scale[:, first + 128 : first + 384] = jnp.ones((1, 256), F32)

    def norm_one(rows, carry):
        xhat, _ = standardized(tokens[rows].astype(F32))
        norm[rows] = (xhat * gain_one + offset_one).astype(BF16)
        return carry

    strips(norm_one)
    after("one")

    def forward_group(group, carry):
        after("group", group, 3)
        for n in range(3):
            columns = pl.ds(aligned(group * WIDTH + n * TILE, 128), TILE)
            projected = dot_nn(norm[...], wq[:, columns]) + qkv_bias[:, columns]
            wide[:, columns] = (projected * qkv_scale[:, columns]).astype(BF16)
        after("qkv", group, 3)

        def forward_pair(half, carry):
            pair = 2 * group + half
            for block in range(4):
                attend(wide, pair, block, query_side, key_side, causal, attended, logsums)
            after("pair", pair, PAIRS)
            return carry

        return lax.fori_loop(0, 2, forward_pair, carry)

    lax.fori_loop(0, 3, forward_group, 0)

    after("joined")
    for n in range(3):
        at = slice(n * TILE, n * TILE + TILE)
        branch = dot_nn(attended[...], wo[:, at]) + vectors[4:5, at]
        middle[:, at] = tokens[:, at].astype(F32) + branch_scale * branch
    after("branch")
    gain_two, offset_two = vectors[5:6], vectors[6:7]

    def norm_two(rows, down_bias):
        xhat, _ = standardized(middle[rows])
        norm[rows] = (xhat * gain_two + offset_two).astype(BF16)
        scaled = (branch_scale * cotangent[rows].astype(F32)).astype(BF16)
        seed[rows] = scaled
        outer[rows] = jnp.zeros((STRIP, WIDTH), F32)
        grad_norm[rows] = jnp.zeros((STRIP, WIDTH), F32)
        return down_bias + column_sum(scaled.astype(F32))

    early[3:4] = strips(norm_two, jnp.zeros((1, WIDTH), F32))
    norm_t[0:WIDTH] = norm[...].T
    norm_t[WIDTH:] = jnp.ones((16, TOKENS), BF16)
    after("norm")

    def feed_forward(step, carry):
        here = pl.ds(aligned(step * WIDTH, 128), WIDTH)
        after("step", step, 4)
        for n in range(3):
            at = slice(n * TILE, n * TILE + TILE)
            columns = pl.ds(aligned(step * WIDTH + n * TILE, 128), TILE)
            bias = vectors[pl.ds(8 + step, 1), at]
            hidden = dot_nn(norm[...], wu[:, columns]) + bias
            grad_active = dot_nt(seed[...], wd[columns])
            active, bent = gelu_and_slope(hidden)
            act[:, at] = active.astype(BF16)
            slope[:, at] = (grad_active * bent).astype(BF16)
        after("hidden", step, 4)
        for n in range(3):
            at = slice(n * TILE, n * TILE + TILE)
            outer[:, at] += dot_nn(act[...], wd[here, at])
            grad_norm[:, at] += dot_nt(slope[...], wu[at, here])
        after("outer", step, 4)
        for number in range(4):
            def sent(number=number):
                for unit in coming[4 + 2 * number : 6 + 2 * number]:
                    unit.finish()

            pl.when(step == number)(sent)
        act_t[...] = act[...].T
        for n in range(3):
            at = slice(n * TILE, n * TILE + TILE)
            columns = pl.ds(aligned(step * WIDTH + n * TILE, 128), TILE)
            grad = dot_nn(norm_t[...], slope[:, at])
            wu[:, columns] = grad[:WIDTH].astype(BF16)
            early[pl.ds(4 + step, 1), at] = grad[WIDTH : WIDTH + 1]
            wd[here, at] = dot_nn(act_t[...], seed[:, at]).astype(BF16)
        after("grads", step, 4)
        return carry

    lax.fori_loop(0, 4, feed_forward, 0)

    def back_two(rows, carry):
        mid = middle[rows]
        slope[rows] = (mid + branch_scale * (outer[rows] + vectors[7:8])).astype(BF16)
        xhat, scale = standardized(mid)
        grad = grad_norm[rows]
        grad_middle = cotangent[rows].astype(F32) + back_through_norm(grad, xhat, scale, gain_two)
        middle[rows] = grad_middle
        grad_branch = (branch_scale * grad_middle).astype(BF16)
        seed[rows] = grad_branch
        parts = (column_sum(grad_branch.astype(F32)), column_sum(grad * xhat), column_sum(grad))
        return tuple(former + part for former, part in zip(carry, parts))

    zero = jnp.zeros((1, WIDTH), F32)
    early[0:1], early[1:2], early[2:3] = strips(back_two, (zero, zero, zero))
    out_copy = pltpu.make_async_copy(slope, layer_out, local_sems.at[0])
    out_copy.start()
    after("back")

    for n in range(3):
        at = slice(n * TILE, n * TILE + TILE)
        act[:, at] = dot_nt(seed[...], wo[at]).astype(BF16)
    after("attended")
    for unit in coming[:4]:
        unit.finish()
    act_t[...] = attended[...].T
    for n in range(3):
        at = slice(n * TILE, n * TILE + TILE)
        wo[:, at] = dot_nn(act_t[...], seed[:, at]).astype(BF16)
    after("out")
    strips(norm_one)
    norm_t[0:WIDTH] = norm[...].T
    out_copy.wait()
    after("first")

    key_sum, value_sum = outer.at[:, 0:128], outer.at[:, 128:256]

    def backward_group(group, carry):
        def backward_pair(half, carry):
            pair = 2 * group + half
            for block in range(4):
                attend_back(
                    wide, pair, block, query_side, key_side, causal, attended, act, logsums, key_sum, value_sum
                )
            first = pair * 384
            wide[:, pl.ds(aligned(first + 128, 128), 128)] = key_sum[...].astype(BF16)
            wide[:, pl.ds(aligned(first + 256, 128), 128)] = value_sum[...].astype(BF16)
            after("pair_back", pair, PAIRS)
            return carry

        lax.fori_loop(0, 2, backward_pair, carry)
        for number in range(3):
            def weight_grads(number=number):
                rows = []
                for n in range(3):
                    at = slice(n * TILE, n * TILE + TILE)
                    columns = slice(number * WIDTH + n * TILE, number * WIDTH + n * TILE + TILE)
                    grad = dot_nn(norm_t[...], wide[:, columns])
                    qkv_partials[number][:, at] = grad[:WIDTH].astype(BF16)
                    rows.append(grad[WIDTH : WIDTH + 1])
                row = jnp.concatenate(rows, axis=1)
                at = slice(number * 256, number * 256 + 256)
                late[2:3, at] = jnp.concatenate([row[:, 0:128], row[:, 384:512]], axis=1)
                late[3:4, at] = jnp.concatenate([row[:, 256:384], row[:, 640:768]], axis=1)
                after("qkv_grads" + str(number))

            pl.when(group == number)(weight_grads)
        return carry

    lax.fori_loop(0, 3, backward_group, 0)

    for n in range(3):
        at = slice(n * TILE, n * TILE + TILE)
        grad_norm[:, at] = dot_nt(wide[...], wq[at])
        after("tokens" + str(n))

    def back_one(rows, carry):
        xhat, scale = standardized(tokens[rows].astype(F32))
        grad = grad_norm[rows]
        middle[rows] += back_through_norm(grad, xhat, scale, gain_one)
        return carry[0] + column_sum(grad * xhat), carry[1] + column_sum(grad)

    late[0:1], late[1:2] = strips(back_one, (zero, zero))
    tokens_copy = pltpu.make_async_copy(middle, grad_tokens, local_sems.at[1])
    tokens_copy.start()
    after("half")
    up = up_target[...]
    up_out[...] = jnp.concatenate(
        [
            up[:, WIDTH * j + ROWS * d : WIDTH * j + ROWS * d + ROWS]
            for d in range(DEVICES)
            for j in range(HIDDEN_PARTS)
        ],
        axis=1,
    )
    after("last")
    back = lax.rem(DEVICES - place.number, DEVICES) * ROWS
    small_out[0:8] = pltpu.roll(early[...], back, 1)[:, 0:128]
    small_out[8:12] = pltpu.roll(late[...], back, 1)[:, 0:128]
    small_out[12:16] = jnp.zeros((4, 128), F32)
    for unit in leaving:
        unit.finish()
    tokens_copy.wait()


def layer(tokens, documents, cotangent, shards, packed):
    vmem = pl.BlockSpec(memory_space=pltpu.VMEM)
    anywhere = pl.BlockSpec(memory_space=pl.ANY)
    out_shape = [jax.ShapeDtypeStruct((TOKENS, WIDTH), BF16), jax.ShapeDtypeStruct((TOKENS, WIDTH), F32)]
    out_shape += [jax.ShapeDtypeStruct(SHARDS[n], F32) for n in NAMES]
    out_shape.append(jax.ShapeDtypeStruct((16, 128), F32))
    scratch = [
        pltpu.VMEM((WIDTH, QKV), BF16),
        pltpu.VMEM((WIDTH, WIDTH), BF16),
        pltpu.VMEM((WIDTH, HIDDEN), BF16),
        pltpu.VMEM((HIDDEN, WIDTH), BF16),
        pltpu.VMEM((TOKENS, WIDTH), BF16),
        pltpu.VMEM((TOKENS, WIDTH), BF16),
        pltpu.VMEM((TOKENS, QKV), BF16),
        pltpu.VMEM((TOKENS, WIDTH), BF16),
        pltpu.VMEM((WIDTH + 16, TOKENS), BF16),
        pltpu.VMEM((TOKENS, WIDTH), BF16),
        pltpu.VMEM((TOKENS, WIDTH), BF16),
        pltpu.VMEM((TOKENS, WIDTH), BF16),
        pltpu.VMEM((WIDTH, TOKENS), BF16),
        pltpu.VMEM((TOKENS, WIDTH), BF16),
        pltpu.VMEM((TOKENS, WIDTH), F32),
        pltpu.VMEM((TOKENS, WIDTH), F32),
        pltpu.VMEM((TOKENS, WIDTH), F32),
        pltpu.VMEM((HEADS, 1, TOKENS), F32),
        pltpu.VMEM((TOKENS, 128), BF16),
        pltpu.VMEM((TOKENS, 128), BF16),
        pltpu.VMEM((QUERY_ROWS, QUERY_ROWS), F32),
        pltpu.VMEM((16, WIDTH), F32),
        pltpu.VMEM((1, QKV), F32),
        pltpu.VMEM((1, QKV), F32),
        pltpu.VMEM((8, WIDTH), F32),
        pltpu.VMEM((4, WIDTH), F32),
        pltpu.VMEM(SHARDS["up"], BF16),
        pltpu.VMEM(SHARDS["up"], F32),
    ]
    scratch += [pltpu.VMEM((32, HALF), BF16)] * (2 * len(GATHER_UNITS))
    for _ in SCATTER_UNITS:
        scratch += ScatterUnit.scratch()
    scratch += [pltpu.SemaphoreType.DMA((len(GATHER_UNITS), GatherUnit.SEMS))] * 2
    scratch += [pltpu.SemaphoreType.DMA((len(SCATTER_UNITS), ScatterUnit.SEMS))] * 2
    for shape, dtype in (((16, WIDTH), BF16), ((8, WIDTH), F32), ((4, WIDTH), F32)):
        scratch += SmallSum.scratch(shape, dtype)
    scratch.append(pltpu.SemaphoreType.DMA((4,)))
    return pl.pallas_call(
        layer_kernel,
        name="layer",
        out_shape=out_shape,
        in_specs=[anywhere, vmem, anywhere] + [vmem] * 5,
        out_specs=[anywhere] * 2 + [vmem] * 5,
        scratch_shapes=scratch,
        compiler_params=pltpu.CompilerParams(collective_id=0, has_side_effects=True, vmem_limit_bytes=VMEM_LIMIT),
        cost_estimate=pl.CostEstimate(flops=50 * 10**9, bytes_accessed=30 * 10**6, transcendentals=20 * 10**6),
    )(tokens, documents, cotangent, *[shards[n] for n in NAMES], packed)


def results_kernel(*refs):
    sources, parts, targets, vectors = refs[:6], refs[6], refs[7:13], refs[13:22]
    held, (sems_in, sems_out) = refs[22:28], refs[28:]
    copies_in = [pltpu.make_async_copy(a, b, sems_in.at[i]) for i, (a, b) in enumerate(zip(sources, held))]
    copies_out = [pltpu.make_async_copy(a, b, sems_out.at[i]) for i, (a, b) in enumerate(zip(held, targets))]
    for copy in copies_in:
        copy.start()
    for target, row in zip(vectors, (8, 9, 10, 11, 0, 1, 2, 3)):
        target[...] = parts[row, 0:ROWS]
    vectors[8][...] = jnp.concatenate([parts[4 + j : 5 + j, 0:ROWS] for j in range(HIDDEN_PARTS)], axis=1)[0]
    for copy_in, copy_out in zip(copies_in, copies_out):
        copy_in.wait()
        copy_out.start()
    for copy in copies_out:
        copy.wait()


def results(arrays, parts):
    vmem = pl.BlockSpec(memory_space=pltpu.VMEM)
    anywhere = pl.BlockSpec(memory_space=pl.ANY)
    out_shape = [jax.ShapeDtypeStruct(a.shape, a.dtype) for a in arrays]
    out_shape += [jax.ShapeDtypeStruct((ROWS,), F32)] * 8 + [jax.ShapeDtypeStruct((ROWS * HIDDEN_PARTS,), F32)]
    scratch = [pltpu.VMEM(a.shape, a.dtype) for a in arrays]
    return pl.pallas_call(
        results_kernel,
        name="results",
        out_shape=out_shape,
        in_specs=[anywhere] * 6 + [vmem],
        out_specs=[anywhere] * 6 + [vmem] * 9,
        scratch_shapes=scratch + [pltpu.SemaphoreType.DMA((6,))] * 2,
        compiler_params=pltpu.CompilerParams(vmem_limit_bytes=VMEM_LIMIT),
    )(*arrays, parts)


def fused_device(
    tokens,
    doc_ids,
    cotangent,
    first_gain,
    first_offset,
    qkv_weight,
    query_bias,
    value_bias,
    out_weight,
    out_bias,
    second_gain,
    second_offset,
    up_weight,
    up_bias,
    down_weight,
    down_bias,
):
    shards = {"qkv": qkv_weight, "out": out_weight, "up": up_weight, "down": down_weight}
    vectors = (
        first_gain,
        first_offset,
        query_bias,
        value_bias,
        out_bias,
        second_gain,
        second_offset,
        down_bias,
        up_bias,
        jnp.zeros((96,), BF16),
    )
    packed = jnp.concatenate(vectors).astype(F32)[None]
    *arrays, parts = layer(tokens, doc_ids, cotangent, shards, packed)
    layer_out, grad_tokens, grad_qkv, grad_out, grad_up, grad_down, *small = results(arrays, parts)
    return (
        layer_out,
        grad_tokens,
        small[0],
        small[1],
        grad_qkv,
        small[2],
        small[3],
        grad_out,
        small[4],
        small[5],
        small[6],
        grad_up,
        small[8],
        grad_down,
        small[7],
    )


def solution(mesh):
    placed = (
        P(("dp", "fsdp"), None),
        P(("dp", "fsdp"), None),
        P(("dp", "fsdp"), None),
        P(("dp", "fsdp")),
        P(("dp", "fsdp")),
        P(("dp", "fsdp"), None),
        P(("dp", "fsdp")),
        P(("dp", "fsdp")),
        P(("dp", "fsdp"), None),
        P(("dp", "fsdp")),
        P(("dp", "fsdp")),
        P(("dp", "fsdp")),
        P(("dp", "fsdp"), None),
        P(("dp", "fsdp")),
        P(("dp", "fsdp"), None),
        P(("dp", "fsdp")),
    )
    return jax.shard_map(
        fused_device if fits(mesh) else plain_device,
        mesh=mesh,
        in_specs=placed,
        out_specs=(
            P(("dp", "fsdp"), None),
            P(("dp", "fsdp"), None),
            P(("dp", "fsdp")),
            P(("dp", "fsdp")),
            P(("dp", "fsdp"), None),
            P(("dp", "fsdp")),
            P(("dp", "fsdp")),
            P(("dp", "fsdp"), None),
            P(("dp", "fsdp")),
            P(("dp", "fsdp")),
            P(("dp", "fsdp")),
            P(("dp", "fsdp"), None),
            P(("dp", "fsdp")),
            P(("dp", "fsdp"), None),
            P(("dp", "fsdp")),
        ),
        check_vma=False,
    )
```

```python
import jax
import jax.numpy as jnp
from jax import lax
from jax.experimental import pallas as pl
from jax.experimental.pallas import tpu as pltpu
from jax.sharding import PartitionSpec as P

HEADS = 12
HEAD_DIM = 64


norm_eps = 1e-05
branch_scale = 48.0 ** (-0.5)


def layer_norm(values, gains, offsets):
    average = jnp.mean(values, axis=-1, keepdims=True)
    centred = values - average
    variance = jnp.mean(centred * centred, axis=-1, keepdims=True)
    return centred * lax.rsqrt(variance + norm_eps) * gains + offsets


def scaled_norm(values, gains):
    return layer_norm(values, gains, 0.0)


def dense(former, latter):
    return jnp.dot(former, latter, preferred_element_type=jnp.float32)


def contract_rows(former, latter):
    return lax.dot_general(
        former, latter, (((0,), (0,)), ((), ())), preferred_element_type=jnp.float32
    )


def contract_cols(former, latter):
    return lax.dot_general(
        former, latter, (((1,), (1,)), ((), ())), preferred_element_type=jnp.float32
    )


def block_scores(queries, keys, documents, row_start, row_stop):
    score_scale = queries.shape[2] ** (-0.5)
    scores = (
        jnp.einsum(
            "qhd,khd->hqk",
            queries[row_start:row_stop],
            keys[:row_stop],
            preferred_element_type=jnp.float32,
        )
        * score_scale
    )
    positions = jnp.arange(row_stop)
    allowed = (documents[row_start:row_stop, None] == documents[None, :row_stop]) & (
        positions[None, :] <= positions[row_start:row_stop, None]
    )
    return jnp.where(allowed[None], scores, -1e30)


def attend_row(queries, keys, values, documents):
    seq_len = queries.shape[0]
    block_rows = min(512, seq_len)
    outputs = []
    logsums = []
    for row_start in range(0, seq_len, block_rows):
        row_stop = row_start + block_rows
        scores = block_scores(queries, keys, documents, row_start, row_stop)
        highest = jnp.max(scores, axis=-1, keepdims=True)
        raised = jnp.exp(scores - highest)
        summed = jnp.sum(raised, axis=-1, keepdims=True)
        weights = (raised / summed).astype(jnp.bfloat16)
        outputs.append(
            jnp.einsum(
                "hqk,khd->qhd", weights, values[:row_stop], preferred_element_type=jnp.float32
            )
        )
        logsums.append((highest + jnp.log(summed))[..., 0])
    return (jnp.concatenate(outputs, axis=0).astype(jnp.bfloat16), jnp.concatenate(logsums, axis=1))


def attend_row_back(queries, keys, values, documents, logsums, grad_out):
    seq_len = queries.shape[0]
    block_rows = min(512, seq_len)
    score_scale = queries.shape[2] ** (-0.5)
    query_parts = []
    grad_keys = jnp.zeros(keys.shape, jnp.float32)
    grad_values = jnp.zeros(values.shape, jnp.float32)
    for row_start in range(0, seq_len, block_rows):
        row_stop = row_start + block_rows
        scores = block_scores(queries, keys, documents, row_start, row_stop)
        probs = jnp.exp(scores - logsums[:, row_start:row_stop, None])
        incoming = grad_out[row_start:row_stop]
        grad_probs = jnp.einsum(
            "qhd,khd->hqk", incoming, values[:row_stop], preferred_element_type=jnp.float32
        )
        inner_sum = jnp.sum(probs * grad_probs, axis=-1, keepdims=True)
        grad_scores = (probs * (grad_probs - inner_sum)).astype(jnp.bfloat16)
        query_parts.append(
            jnp.einsum(
                "hqk,khd->qhd", grad_scores, keys[:row_stop], preferred_element_type=jnp.float32
            )
            * score_scale
        )
        key_term = (
            jnp.einsum(
                "hqk,qhd->khd",
                grad_scores,
                queries[row_start:row_stop],
                preferred_element_type=jnp.float32,
            )
            * score_scale
        )
        value_term = jnp.einsum(
            "hqk,qhd->khd", probs.astype(jnp.bfloat16), incoming, preferred_element_type=jnp.float32
        )
        padding = ((0, seq_len - row_stop), (0, 0), (0, 0))
        grad_keys = grad_keys + jnp.pad(key_term, padding)
        grad_values = grad_values + jnp.pad(value_term, padding)
    return (jnp.concatenate(query_parts, axis=0), grad_keys, grad_values)


def plain_device(
    tokens,
    doc_ids,
    cotangent,
    first_gain,
    first_offset,
    qkv_weight,
    query_bias,
    value_bias,
    out_weight,
    out_bias,
    second_gain,
    second_offset,
    up_weight,
    up_bias,
    down_weight,
    down_bias,
):
    attn_full = (
        lax.all_gather(first_gain, ("dp", "fsdp"), axis=0, tiled=True),
        lax.all_gather(first_offset, ("dp", "fsdp"), axis=0, tiled=True),
        lax.all_gather(qkv_weight, ("dp", "fsdp"), axis=0, tiled=True),
        lax.all_gather(query_bias, ("dp", "fsdp"), axis=0, tiled=True),
        lax.all_gather(value_bias, ("dp", "fsdp"), axis=0, tiled=True),
        lax.all_gather(out_weight, ("dp", "fsdp"), axis=0, tiled=True),
        lax.all_gather(out_bias, ("dp", "fsdp"), axis=0, tiled=True),
    )
    model_width = tokens.shape[1]
    rows_here = doc_ids.shape[0]
    seq_len = doc_ids.shape[1]
    inputs = tokens.astype(jnp.float32)
    gain_one = attn_full[0].astype(jnp.float32)
    normed_one = layer_norm(inputs, gain_one, attn_full[1].astype(jnp.float32)).astype(jnp.bfloat16)
    projected = dense(normed_one, attn_full[2])
    queries = (projected[:, :model_width] + attn_full[3].astype(jnp.float32)).astype(jnp.bfloat16)
    keys = projected[:, model_width : 2 * model_width].astype(jnp.bfloat16)
    values = (projected[:, 2 * model_width :] + attn_full[4].astype(jnp.float32)).astype(
        jnp.bfloat16
    )
    row_shape = (rows_here, seq_len, HEADS, HEAD_DIM)
    queries = queries.reshape(row_shape)
    keys = keys.reshape(row_shape)
    values = values.reshape(row_shape)
    attended, logsums = lax.map(
        lambda row_item: attend_row(*row_item), (queries, keys, values, doc_ids)
    )
    attended = attended.reshape(-1, model_width)
    branch = dense(attended, attn_full[5]) + attn_full[6].astype(jnp.float32)
    middle = inputs + branch_scale * branch
    mlp_full = (
        lax.all_gather(second_gain, ("dp", "fsdp"), axis=0, tiled=True),
        lax.all_gather(second_offset, ("dp", "fsdp"), axis=0, tiled=True),
        lax.all_gather(up_weight, ("dp", "fsdp"), axis=0, tiled=True),
        lax.all_gather(up_bias, ("dp", "fsdp"), axis=0, tiled=True),
        lax.all_gather(down_weight, ("dp", "fsdp"), axis=0, tiled=True),
        lax.all_gather(down_bias, ("dp", "fsdp"), axis=0, tiled=True),
    )
    gain_two = mlp_full[0].astype(jnp.float32)
    normed_two = layer_norm(middle, gain_two, mlp_full[1].astype(jnp.float32)).astype(jnp.bfloat16)
    hidden = dense(normed_two, mlp_full[2]) + mlp_full[3].astype(jnp.float32)
    active, gelu_back = jax.vjp(lambda pre_act: jax.nn.gelu(pre_act, approximate=True), hidden)
    active = active.astype(jnp.bfloat16)
    outer = dense(active, mlp_full[4]) + mlp_full[5].astype(jnp.float32)
    layer_out = (middle + branch_scale * outer).astype(jnp.bfloat16)
    mlp_back = (
        lax.all_gather(second_gain, ("dp", "fsdp"), axis=0, tiled=True),
        lax.all_gather(up_weight, ("dp", "fsdp"), axis=0, tiled=True),
        lax.all_gather(down_weight, ("dp", "fsdp"), axis=0, tiled=True),
    )
    seed = cotangent.astype(jnp.float32)
    grad_outer = (branch_scale * seed).astype(jnp.bfloat16)
    grad_down_bias = jnp.sum(grad_outer.astype(jnp.float32), axis=0)
    grad_down_weight = contract_rows(active, grad_outer)
    grad_active = contract_cols(grad_outer, mlp_back[2])
    grad_hidden = gelu_back(grad_active)[0].astype(jnp.bfloat16)
    grad_up_bias = jnp.sum(grad_hidden.astype(jnp.float32), axis=0)
    grad_up_weight = contract_rows(normed_two, grad_hidden)
    grad_normed_two = contract_cols(grad_hidden, mlp_back[1])
    _, norm_two_back = jax.vjp(scaled_norm, middle, mlp_back[0].astype(jnp.float32))
    grad_middle_part, grad_second_gain = norm_two_back(grad_normed_two)
    grad_second_offset = jnp.sum(grad_normed_two, axis=0)
    grad_middle = seed + grad_middle_part
    mlp_shares = (
        grad_second_gain,
        grad_second_offset,
        grad_up_weight,
        grad_up_bias,
        grad_down_weight,
        grad_down_bias,
    )
    attn_back = (
        lax.all_gather(first_gain, ("dp", "fsdp"), axis=0, tiled=True),
        lax.all_gather(qkv_weight, ("dp", "fsdp"), axis=0, tiled=True),
        lax.all_gather(out_weight, ("dp", "fsdp"), axis=0, tiled=True),
    )
    grad_branch = (branch_scale * grad_middle).astype(jnp.bfloat16)
    grad_out_bias = jnp.sum(grad_branch.astype(jnp.float32), axis=0)
    grad_out_weight = contract_rows(attended, grad_branch)
    grad_attended = contract_cols(grad_branch, attn_back[2]).astype(jnp.bfloat16).reshape(row_shape)
    grad_queries, grad_keys, grad_values = lax.map(
        lambda row_item: attend_row_back(*row_item),
        (queries, keys, values, doc_ids, logsums, grad_attended),
    )
    grad_projected = jnp.concatenate(
        [
            grad_queries.reshape(-1, model_width),
            grad_keys.reshape(-1, model_width),
            grad_values.reshape(-1, model_width),
        ],
        axis=1,
    ).astype(jnp.bfloat16)
    grad_wide = grad_projected.astype(jnp.float32)
    grad_query_bias = jnp.sum(grad_wide[:, :model_width], axis=0)
    grad_value_bias = jnp.sum(grad_wide[:, 2 * model_width :], axis=0)
    grad_qkv_weight = contract_rows(normed_one, grad_projected)
    grad_normed_one = contract_cols(grad_projected, attn_back[1])
    _, norm_one_back = jax.vjp(scaled_norm, inputs, attn_back[0].astype(jnp.float32))
    grad_input_part, grad_first_gain = norm_one_back(grad_normed_one)
    grad_first_offset = jnp.sum(grad_normed_one, axis=0)
    grad_tokens = grad_middle + grad_input_part
    every_share = (
        lax.psum_scatter(grad_second_gain, ("dp", "fsdp"), scatter_dimension=0, tiled=True),
        lax.psum_scatter(grad_second_offset, ("dp", "fsdp"), scatter_dimension=0, tiled=True),
        lax.psum_scatter(grad_up_weight, ("dp", "fsdp"), scatter_dimension=0, tiled=True),
        lax.psum_scatter(grad_up_bias, ("dp", "fsdp"), scatter_dimension=0, tiled=True),
        lax.psum_scatter(grad_down_weight, ("dp", "fsdp"), scatter_dimension=0, tiled=True),
        lax.psum_scatter(grad_down_bias, ("dp", "fsdp"), scatter_dimension=0, tiled=True),
        lax.psum_scatter(grad_first_gain, ("dp", "fsdp"), scatter_dimension=0, tiled=True),
        lax.psum_scatter(grad_first_offset, ("dp", "fsdp"), scatter_dimension=0, tiled=True),
        lax.psum_scatter(grad_qkv_weight, ("dp", "fsdp"), scatter_dimension=0, tiled=True),
        lax.psum_scatter(grad_query_bias, ("dp", "fsdp"), scatter_dimension=0, tiled=True),
        lax.psum_scatter(grad_value_bias, ("dp", "fsdp"), scatter_dimension=0, tiled=True),
        lax.psum_scatter(grad_out_weight, ("dp", "fsdp"), scatter_dimension=0, tiled=True),
        lax.psum_scatter(grad_out_bias, ("dp", "fsdp"), scatter_dimension=0, tiled=True),
    )
    mlp_shares = every_share[:6]
    attn_shares = every_share[6:]
    return (
        layer_out,
        grad_tokens,
        attn_shares[0],
        attn_shares[1],
        attn_shares[2],
        attn_shares[3],
        attn_shares[4],
        attn_shares[5],
        attn_shares[6],
        mlp_shares[0],
        mlp_shares[1],
        mlp_shares[2],
        mlp_shares[3],
        mlp_shares[4],
        mlp_shares[5],
    )


MESH = pl.DeviceIdType.MESH
F32 = jnp.float32
BF16 = jnp.bfloat16
WIDTH = 768
HIDDEN = 3072
TOKENS = 1024
QKV = 3 * WIDTH
PAIRS = 6
QUERY_ROWS = 256
KEY_WINDOWS = ((0, 256), (0, 512), (0, 768), (256, 1024))
DOCUMENTS = 6
FAR_BELOW = 2.0**100
STRIP = 256
TILE = 256
VMEM_LIMIT = 63 * 2**20
GELU_A = 0.7978845608028654
GELU_B = 0.044715

GATHER_UNITS = tuple(("qkv", 0, first, 128) for first in (0, 128, 256))
GATHER_UNITS += (("qkv", 1, 0, 384), ("qkv", 2, 0, 384), ("out", 0, 0, 384))
GATHER_UNITS += tuple((name, part, 0, 384) for part in range(4) for name in ("up", "down"))
SCATTER_UNITS = GATHER_UNITS[6:] + (("out", 0, 0, 384), ("qkv", 0, 0, 384), ("qkv", 1, 0, 384))
SCATTER_UNITS += tuple(("qkv", 2, first, 128) for first in (0, 128, 256))
ROWS = 24
HALF = 384
SHARDS = {"qkv": (24, 2304), "out": (24, 768), "up": (24, 3072), "down": (96, 768)}
NAMES = ("qkv", "out", "up", "down")
DEVICES = 32
HIDDEN_PARTS = 4


def fits(mesh):
    return mesh.shape["dp"] == 4 and mesh.shape["fsdp"] == 8


def aligned(value, step):
    return pl.multiple_of(value, step)


def dot_nt(a, b):
    return lax.dot_general(a, b, (((1,), (1,)), ((), ())), preferred_element_type=F32)


def dot_nn(a, b):
    return lax.dot_general(a, b, (((1,), (0,)), ((), ())), preferred_element_type=F32)


def dot_tn(a, b):
    return lax.dot_general(a, b, (((0,), (0,)), ((), ())), preferred_element_type=F32)


class Place:
    def __init__(self):
        self.dp = lax.axis_index("dp")
        self.fsdp = lax.axis_index("fsdp")
        self.core = lax.rem(self.fsdp, 2)
        self.z = lax.div(self.fsdp, 2)
        x = lax.rem(self.dp, 2)
        y = lax.div(self.dp, 2)
        self.dp_x = y * 2 + (1 - x)
        self.dp_y = (1 - y) * 2 + x
        self.dp_far = 3 - self.dp
        core = self.core
        self.near = self.dp_x * (1 - core) + self.dp_y * core
        self.next = self.dp_y * (1 - core) + self.dp_x * core
        self.chip = self.dp * 4 + self.z
        self.number = self.dp * 8 + self.fsdp
        self.partner = (self.dp, self.z * 2 + (1 - core))
        self.at_near = (self.near, self.fsdp)
        self.at_next = (self.next, self.fsdp)

    def along_z(self, step):
        z = lax.rem(self.z + step, 4)
        return (self.dp, z * 2 + self.core)

    def greet(self):
        barrier = pltpu.get_barrier_semaphore()
        others = [self.partner, (self.dp_x, self.fsdp), (self.dp_y, self.fsdp), (self.dp_far, self.fsdp)]
        others += [self.along_z(step) for step in (1, 2, 3)]
        for other in others:
            pl.semaphore_signal(barrier, inc=1, device_id=other, device_id_type=MESH)
        pl.semaphore_wait(barrier, len(others))


def remote(source, target, sems, index, device):
    return pltpu.make_async_remote_copy(
        src_ref=source,
        dst_ref=target,
        send_sem=sems[0].at[index],
        recv_sem=sems[1].at[index],
        device_id=device,
        device_id_type=MESH,
    )


class SmallSum:
    def __init__(self, place, source, target, buffers, landed, send_sems, recv_sems):
        self.place, self.source, self.target = place, source, target
        self.buffers, self.landed, self.sems = buffers, landed, (send_sems, recv_sems)

    @staticmethod
    def scratch(shape, dtype):
        return [
            pltpu.VMEM((3, *shape), dtype),
            pltpu.VMEM((7, *shape), dtype),
            pltpu.SemaphoreType.DMA((7,)),
            pltpu.SemaphoreType.DMA((7,)),
        ]

    def copies(self, stage):
        p = self.place
        if stage == 0:
            devices = [p.partner]
        elif stage == 1:
            devices = [(dp, p.fsdp) for dp in (p.dp_x, p.dp_y, p.dp_far)]
        else:
            devices = [p.along_z(step) for step in (1, 2, 3)]
        first = (0, 1, 4)[stage]
        return [
            remote(self.buffers.at[stage], self.landed.at[first + i], self.sems, first + i, device)
            for i, device in enumerate(devices)
        ]

    def begin(self):
        self.buffers[0] = self.source[...].astype(self.buffers.dtype)
        for copy in self.copies(0):
            copy.start()

    def middle(self):
        for copy in self.copies(0):
            copy.wait()
        self.buffers[1] = self.buffers[0] + self.landed[0]
        for copy in self.copies(1):
            copy.start()

    def later(self):
        for copy in self.copies(1):
            copy.wait()
        self.buffers[2] = (self.buffers[1] + self.landed[1]) + (self.landed[2] + self.landed[3])
        for copy in self.copies(2):
            copy.start()

    def end(self):
        for copy in self.copies(2):
            copy.wait()
        total = (self.buffers[2] + self.landed[4]) + (self.landed[5] + self.landed[6])
        self.target[...] = total.astype(self.target.dtype)


class GatherUnit:
    SEMS = 11

    def __init__(self, place, unit, shard, full, pair_out, pair_in, send_sems, recv_sems):
        self.place = place
        self.name, self.part, self.first, self.width = unit
        self.shard, self.full = shard, full
        self.pair_out, self.pair_in = pair_out, pair_in
        self.sems = (send_sems, recv_sems)

    def columns_of(self, core):
        if self.name == "qkv":
            start = 2 * self.part * 128 + 128 * core
            chosen = range(self.first // 128, (self.first + self.width) // 128)
            parts = [self.shard[:, pl.ds(aligned(start + WIDTH * i, 128), 128)] for i in chosen]
            return jnp.concatenate(parts, axis=1).astype(F32)
        start = WIDTH * self.part if self.name == "up" else 0
        columns = self.shard[:, pl.ds(aligned(start + HALF * core + self.first, 128), self.width)].astype(F32)
        return columns[ROWS * self.part : ROWS * self.part + ROWS] if self.name == "down" else columns

    def rows_at(self, first, count):
        columns = pl.ds(aligned(HALF * self.place.core + self.first, 128), self.width)
        return self.full.at[pl.ds(aligned(first, 16), count), columns]

    def group(self, dp):
        return self.rows_at(dp * (8 * ROWS), 8 * ROWS)

    def block(self, dp=None):
        chip = self.place.chip if dp is None else dp * 4 + self.place.z
        return self.rows_at(chip * (2 * ROWS), 2 * ROWS)

    def copy(self, index):
        p = self.place
        if index == 0:
            return remote(self.pair_out, self.pair_in, self.sems, 0, p.partner)
        if index < 4:
            return remote(self.block(), self.block(), self.sems, index, p.along_z(index))
        dp = (p.dp, p.dp, p.near, p.dp, p.near, p.next, p.dp_far)[index - 4]
        device = p.at_near if index == 4 else p.at_next if index < 7 else p.partner
        return remote(self.group(dp), self.group(dp), self.sems, index, device)

    def start(self, *indices):
        for index in indices:
            self.copy(index).start()

    def landed(self, *indices):
        for index in indices:
            self.copy(index).wait_recv()

    def pair(self):
        self.pair_out[0:ROWS] = self.columns_of(1 - self.place.core).astype(BF16)
        self.pair_out[ROWS:] = jnp.zeros((32 - ROWS, self.width), BF16)
        self.start(0)

    def assemble(self):
        self.landed(0)
        own = self.columns_of(self.place.core)
        came = self.pair_in[0:ROWS].astype(F32)
        first = self.place.core == 0
        block = jnp.concatenate([jnp.where(first, own, came), jnp.where(first, came, own)], axis=0)
        self.block()[...] = block.astype(BF16)

    def along_z(self):
        self.assemble()
        self.start(1, 2, 3)

    def to_near(self):
        self.landed(1, 2, 3)
        self.start(4, 7)

    def to_next(self):
        self.landed(4)
        self.start(5, 6, 8)

    def to_core(self):
        self.landed(5)
        self.start(9)
        self.landed(6)
        self.start(10)

    def arrived(self):
        self.landed(7, 8, 9, 10)

    def finish(self):
        for index in range(self.SEMS):
            self.copy(index).wait_send()


class ScatterUnit:
    SEMS = 8

    def __init__(self, place, unit, partial, target, halves, from_next, from_near, from_z, pair, send_sems, recv_sems):
        self.place = place
        self.name, self.part, self.first, self.width = unit
        self.partial, self.target = partial, target
        self.halves, self.from_next, self.from_near = halves, from_next, from_near
        self.from_z, self.pair_buffer = from_z, pair
        self.sems = (send_sems, recv_sems)

    @staticmethod
    def scratch(width):
        return [
            pltpu.VMEM((WIDTH, width), BF16),
            pltpu.VMEM((2, 8 * ROWS, width), BF16),
            pltpu.VMEM((8 * ROWS, width), BF16),
            pltpu.VMEM((3, 2 * ROWS, width), BF16),
            pltpu.VMEM((3, ROWS, width), F32),
        ]

    def columns(self, core):
        return pl.ds(aligned(HALF * core + self.first, 128), self.width)

    def group(self, dp):
        return self.halves.at[pl.ds(aligned(dp * (8 * ROWS), 16), 8 * ROWS)]

    def z_block(self, step, dp=None):
        chip = (self.place.dp if dp is None else dp) * 4 + lax.rem(self.place.z + step, 4)
        return self.halves.at[pl.ds(aligned(chip * (2 * ROWS), 16), 2 * ROWS)]

    def copy(self, index):
        p = self.place
        if index == 0:
            source = self.partial.at[pl.ds(0, WIDTH), self.columns(1 - p.core)]
            return remote(source, self.halves, self.sems, 0, p.partner)
        if index < 3:
            dp = (p.next, p.dp_far)[index - 1]
            return remote(self.group(dp), self.from_next.at[index - 1], self.sems, index, p.at_next)
        if index == 3:
            return remote(self.group(p.near), self.from_near, self.sems, 3, p.at_near)
        if index < 7:
            step = index - 3
            return remote(self.z_block(step), self.from_z.at[step - 1], self.sems, index, p.along_z(step))
        return remote(self.pair_buffer.at[0], self.pair_buffer.at[2], self.sems, 7, p.partner)

    def start(self, *indices):
        for index in indices:
            self.copy(index).start()

    def landed(self, *indices):
        for index in indices:
            self.copy(index).wait_recv()

    def add(self, former, latter, rows):
        step = 192

        def body(index, carry):
            at = pl.ds(aligned(index * step, 16), step)
            former[at] = former[at] + latter(at)
            return carry

        lax.fori_loop(0, rows // step, body, 0)

    def to_partner(self):
        self.start(0)

    def to_next(self):
        self.landed(0)
        mine = self.columns(self.place.core)
        self.add(self.halves, lambda at: self.partial[at, mine], WIDTH)
        self.start(1, 2)

    def to_near(self):
        p = self.place
        self.landed(1, 2)
        self.add(self.group(p.near), lambda at: self.from_next[1, at], 8 * ROWS)
        self.start(3)
        self.add(self.group(p.dp), lambda at: self.from_next[0, at], 8 * ROWS)

    def along_z(self):
        self.landed(3)
        self.add(self.group(self.place.dp), lambda at: self.from_near[at], 8 * ROWS)
        self.start(4, 5, 6)

    def to_pair(self):
        self.landed(4, 5, 6)
        came = [self.from_z[i].astype(F32) for i in range(3)]
        self.halve((self.z_block(0)[...].astype(F32) + came[0]) + (came[1] + came[2]))
        self.start(7)

    def halve(self, block):
        first = self.place.core == 0
        self.pair_buffer[0] = jnp.where(first, block[ROWS:], block[:ROWS])
        self.pair_buffer[1] = jnp.where(first, block[:ROWS], block[ROWS:])

    def store(self):
        self.landed(7)
        self.put()

    def put(self):
        for source, core in ((1, self.place.core), (2, 1 - self.place.core)):
            if self.name == "qkv":
                start = 2 * self.part * 128 + 128 * core
                for number in range(self.width // 128):
                    columns = pl.ds(aligned(start + WIDTH * (self.first // 128 + number), 128), 128)
                    self.target[:, columns] = self.pair_buffer[source, :, 128 * number : 128 * number + 128]
            elif self.name == "down":
                self.target[ROWS * self.part : ROWS * self.part + ROWS, self.columns(core)] = self.pair_buffer[source]
            else:
                start = WIDTH * self.part + HALF * core + self.first
                self.target[:, pl.ds(aligned(start, 128), self.width)] = self.pair_buffer[source]

    def finish(self):
        for index in range(self.SEMS):
            self.copy(index).wait_send()


class Stage:
    def __init__(self, kind, method):
        self.kind, self.method = kind, method

    def __getitem__(self, unit):
        return self.kind, self.method, unit


p, z, n = Stage(0, "pair"), Stage(0, "along_z"), Stage(0, "to_near")
x, c, r = Stage(0, "to_next"), Stage(0, "to_core"), Stage(0, "arrived")
G, A, B = Stage(1, "to_partner"), Stage(1, "to_next"), Stage(1, "to_near")
Z, D, S = Stage(1, "along_z"), Stage(1, "to_pair"), Stage(1, "store")
b, m, l, e = Stage(2, "begin"), Stage(2, "middle"), Stage(2, "later"), Stage(2, "end")


def strips(body, carry=0):
    def run(index, carry):
        return body(pl.ds(aligned(index * STRIP, STRIP), STRIP), carry)

    return lax.fori_loop(0, TOKENS // STRIP, run, carry)


def standardized(values):
    average = jnp.mean(values, axis=-1, keepdims=True)
    centred = values - average
    variance = jnp.mean(centred * centred, axis=-1, keepdims=True)
    scale = lax.rsqrt(variance + norm_eps)
    return centred * scale, scale


def back_through_norm(grad, xhat, scale, gains):
    lifted = grad * gains
    return scale * (
        lifted
        - jnp.mean(lifted, axis=-1, keepdims=True)
        - xhat * jnp.mean(lifted * xhat, axis=-1, keepdims=True)
    )


def column_sum(values):
    return jnp.sum(values, axis=0, keepdims=True)


def gelu_and_slope(h):
    square = h * h
    bent = GELU_A + GELU_A * GELU_B * square
    gate = 0.5 + 0.5 * jnp.tanh(h * bent)
    active = h * gate
    slope = gate + active * (1.0 - gate) * (6.0 * bent - 4.0 * GELU_A)
    return active, slope


def document_lanes(documents, query_side, key_side):
    lane = lax.rem(lax.broadcasted_iota(jnp.int32, (TOKENS, 128), 1), 64)
    own = jnp.broadcast_to(documents.astype(F32), (128, TOKENS)).T == lane.astype(F32)
    query_side[...] = jnp.where(own, 1.0, 0.0).astype(BF16)
    key_side[...] = jnp.where(own | (lane >= DOCUMENTS), 0.0, -FAR_BELOW).astype(BF16)


def causal_corner(causal):
    key = lax.broadcasted_iota(jnp.int32, (QUERY_ROWS, QUERY_ROWS), 0)
    query = lax.broadcasted_iota(jnp.int32, (QUERY_ROWS, QUERY_ROWS), 1)
    causal[...] = jnp.where(key <= query, 0.0, -FAR_BELOW)


class Pair:
    def __init__(self, wide, pair, block, query_side, key_side):
        start, stop = KEY_WINDOWS[block]
        self.keys = pl.ds(start, stop - start)
        self.rows = pl.ds(block * QUERY_ROWS, QUERY_ROWS)
        first = pair * 384
        self.at = [pl.ds(aligned(first + 128 * i, 128), 128) for i in range(3)]
        self.q = wide[self.rows, self.at[0]]
        self.k = wide[self.keys, self.at[1]]
        self.v = wide[self.keys, self.at[2]]
        self.query_side, self.key_side = query_side[self.rows], key_side[self.keys]
        self.start, self.stop = start, stop

    def choose(self, head, inside, outside):
        low = lax.broadcasted_iota(jnp.int32, inside.shape, 1) < 64
        return jnp.where(low, inside, outside) if head == 0 else jnp.where(low, outside, inside)

    def only(self, head, values):
        return self.choose(head, values, jnp.zeros_like(values))

    def scores(self, head, causal):
        scores = dot_nt(self.choose(head, self.k, self.key_side), self.choose(head, self.q, self.query_side))
        wide = self.stop - self.start - QUERY_ROWS
        corner = scores[wide:] + causal[...]
        return jnp.concatenate([scores[:wide], corner], axis=0) if wide else corner


def attend(wide, pair, block, query_side, key_side, causal, attended, logsums):
    p = Pair(wide, pair, block, query_side, key_side)
    weights, sums = [], []
    for head in range(2):
        scores = p.scores(head, causal)
        highest = jnp.max(scores, axis=0, keepdims=True)
        raised = jnp.exp(scores - highest)
        summed = column_sum(raised)
        weights.append(raised.astype(BF16))
        sums.append(jnp.broadcast_to(summed, (HEAD_DIM, QUERY_ROWS)))
        logsums[2 * pair + head, :, p.rows] = highest + jnp.log(summed)
    values = jnp.concatenate([p.only(head, p.v) for head in range(2)], axis=0)
    out = dot_tn(values, jnp.concatenate(weights, axis=0)) / jnp.concatenate(sums, axis=0)
    attended[p.rows, pl.ds(aligned(pair * 128, 128), 128)] = out.T.astype(BF16)


def attend_back(
    wide, pair, block, query_side, key_side, causal, attended, grad_attended, logsums, query_grad, key_sum, value_sum
):
    p = Pair(wide, pair, block, query_side, key_side)
    features = pl.ds(aligned(pair * 128, 128), 128)
    incoming = grad_attended[p.rows, features]
    inner = (incoming.astype(F32) * attended[p.rows, features].astype(F32)).T
    probs, slopes = [], []
    for head in range(2):
        delta = column_sum(inner[64 * head : 64 * head + 64])
        prob = jnp.exp(p.scores(head, causal) - logsums[2 * pair + head, :, p.rows])
        grad_prob = dot_nt(p.v, p.only(head, incoming))
        probs.append(prob.astype(BF16))
        slopes.append((prob * (grad_prob - delta)).astype(BF16))
    both = lambda values: jnp.concatenate([p.only(head, values) for head in range(2)], axis=0)
    value_part = dot_nn(jnp.concatenate(probs, axis=1), both(incoming))
    key_part = dot_nn(jnp.concatenate(slopes, axis=1), both(p.q))
    query_part = dot_tn(both(p.k), jnp.concatenate(slopes, axis=0))
    query_grad[:, p.rows] = (query_part * HEAD_DIM**-0.5).astype(BF16)
    inside = p.stop - p.start - QUERY_ROWS
    if inside:
        earlier = pl.ds(p.start, inside)
        key_sum[earlier] += key_part[:inside]
        value_sum[earlier] += value_part[:inside]
    newest = pl.ds(p.stop - QUERY_ROWS, QUERY_ROWS)
    key_sum[newest] = key_part[inside:]
    value_sum[newest] = value_part[inside:]


PLAN = dict(
        greet=(p[1], p[4],),
        packed=(p[8], p[5], p[2], p[12], z[1], p[10], p[0], p[6], b[0], z[2], m[0], p[7], p[3], p[11], z[0],
        z[3],),
        documents=(n[1], p[13], n[2], n[0], z[4], z[5], l[0], z[6], p[9], x[1],),
        vectors=(z[7], z[8], x[2], n[3], z[9], c[1], x[0], n[4], x[3], c[0], z[13], x[4], n[5], r[1], c[2],
        e[0],),
        one=(r[0], c[3],),
        seed=(n[6], r[2],),
        qkv0=(x[5],),
        pair0=(n[7], c[4],),
        pair1=(z[11],),
        group1=(n[8], z[10], r[3],),
        qkv1=(x[6], r[4], n[9], z[12],),
        pair2=(x[7],),
        qkv2=(x[9], c[5],),
        pair5=(x[8], n[10],),
        joined=(c[6], r[5],),
        branch=(c[7],),
        norm=(r[6],),
        step0=(r[7], n[12], n[11], c[9], n[13],),
        hidden0=(x[10], r[9],),
        outer0=(c[8],),
        step1=(G[0], x[11], r[8], G[1],),
        hidden1=(A[0], c[10], x[12],),
        outer1=(c[11], r[10],),
        grads1=(x[13], G[3], r[11],),
        step2=(A[1],),
        hidden2=(c[12],),
        outer2=(G[2], A[3], c[13],),
        grads2=(A[2],),
        step3=(B[1], r[12], G[5], r[13],),
        hidden3=(B[0], G[4],),
        outer3=(A[4], A[5],),
        grads3=(G[6], B[2],),
        back=(B[3], Z[0],),
        attended=(Z[1], A[6], b[1],),
        first=(G[7], B[4],),
        pair_back0=(m[1], A[7], Z[2],),
        pair_back1=(Z[4],),
        qkv_grads0=(l[1], B[5], G[8], Z[3], G[9], B[6],),
        pair_back2=(A[9],),
        pair_back3=(B[7],),
        qkv_grads1=(Z[5], A[8], Z[6], G[10],),
        pair_back4=(A[10], Z[7], B[9],),
        qkv_grads2=(G[12], D[1], G[13], B[8],),
        tokens0=(Z[9], G[11], D[2], D[0], A[12], D[4], B[10],),
        tokens1=(A[13], Z[8], A[11],),
        half=(Z[10], B[13], b[2], D[3], B[12], m[2], D[5], D[6], B[11], S[5], e[1], D[9], Z[13], S[4], S[6],
        S[3], Z[12], Z[11], D[7], D[8], l[2], D[13], S[1], D[10], S[7], S[8], S[9], S[13], S[2], D[12], S[0],
        D[11], S[12],),
        last=(S[10], e[2], S[11],),
)


def layer_kernel(*refs):
    refs = list(refs)

    def take(count):
        taken = refs[:count]
        del refs[:count]
        return taken

    tokens_in, documents, cotangent_in = take(3)
    shards = dict(zip(NAMES, take(4)))
    (packed,) = take(1)
    layer_out, grad_tokens = take(2)
    targets = dict(zip(NAMES, take(4)))
    (small_out,) = take(1)
    wq, wo, wu, wd = take(4)
    tokens, cotangent, wide, norm, norm_t, attended, seed, act, act_t, slope = take(10)
    middle, outer, grad_norm = take(3)
    logsums, query_side, key_side, causal, vectors, qkv_bias, qkv_scale, early = take(8)
    late, up_shard, up_target, first_t = take(4)
    pair_buffers = take(2 * len(GATHER_UNITS))
    scatter_buffers = take(5 * len(SCATTER_UNITS))
    gather_sems, scatter_sems = take(2), take(2)
    small_refs = [take(4) for _ in range(3)]
    (local_sems,) = take(1)

    place = Place()
    up_natural, shards["up"] = shards["up"], up_shard
    up_out, targets["up"] = targets["up"], up_target

    def part(index):
        return slice(WIDTH * index, WIDTH * index + WIDTH)

    def whole(name, index):
        if name == "out":
            return wo
        return wd.at[part(index)] if name == "down" else {"qkv": wq, "up": wu}[name].at[:, part(index)]

    coming = [
        GatherUnit(
            place,
            unit,
            shards[unit[0]],
            whole(*unit[:2]),
            *pair_buffers[2 * i : 2 * i + 2],
            gather_sems[0].at[i],
            gather_sems[1].at[i],
        )
        for i, unit in enumerate(GATHER_UNITS)
    ]
    qkv_partials = (slope.at[0:WIDTH], act_t.at[:, 0:WIDTH], norm.at[0:WIDTH])
    leaving = [
        ScatterUnit(
            place,
            unit,
            qkv_partials[unit[1]] if unit[0] == "qkv" else whole(*unit[:2]),
            targets[unit[0]],
            *scatter_buffers[5 * i : 5 * i + 5],
            scatter_sems[0].at[i],
            scatter_sems[1].at[i],
        )
        for i, unit in enumerate(SCATTER_UNITS)
    ]

    vector_sums = [
        SmallSum(place, source, target, *refs)
        for source, target, refs in zip((vectors, early, late), (vectors, early, late), small_refs)
    ]

    def run(steps):
        for kind, method, unit in steps:
            getattr((coming, leaving, vector_sums)[kind][unit], method)()

    def after(name, index=None, count=0):
        if index is None:
            run(PLAN.get(name, ()))
            return
        for number in range(count):
            steps = PLAN.get(name + str(number), ())
            if steps:
                pl.when(index == number)(lambda steps=steps: run(steps))

    loads = [
        pltpu.make_async_copy(source, target, local_sems.at[2 + i])
        for i, (source, target) in enumerate(((tokens_in, tokens), (cotangent_in, cotangent)))
    ]
    for load in loads:
        load.start()
    vectors[...] = jnp.zeros_like(vectors)
    for row in range(12):
        vectors[row : row + 1, 0:ROWS] = packed[:, ROWS * row : ROWS * row + ROWS]
    vectors[...] = pltpu.roll(vectors[...], place.number * ROWS, 1)
    place.greet()
    after("greet")
    up = up_natural[...].astype(F32)
    step = ROWS * HIDDEN_PARTS
    up_shard[...] = jnp.concatenate(
        [up[:, step * d + ROWS * j : step * d + ROWS * j + ROWS] for j in range(HIDDEN_PARTS) for d in range(DEVICES)],
        axis=1,
    ).astype(BF16)
    after("packed")
    document_lanes(documents[...], query_side, key_side)
    causal_corner(causal)
    after("documents")
    for load in loads:
        load.wait()
    after("vectors")
    gain_one, offset_one = vectors[0:1], vectors[1:2]
    for pair in range(PAIRS):
        at = slice(128 * pair, 128 * pair + 128)
        first = 384 * pair
        qkv_bias[:, first : first + 128] = vectors[2:3, at]
        qkv_bias[:, first + 128 : first + 256] = jnp.zeros((1, 128), F32)
        qkv_bias[:, first + 256 : first + 384] = vectors[3:4, at]
        qkv_scale[:, first : first + 128] = jnp.full((1, 128), HEAD_DIM**-0.5, F32)
        qkv_scale[:, first + 128 : first + 384] = jnp.ones((1, 256), F32)

    def norm_one(rows, carry):
        xhat, _ = standardized(tokens[rows].astype(F32))
        norm[rows] = (xhat * gain_one + offset_one).astype(BF16)
        return carry

    strips(norm_one)
    after("one")
    first_t[0:WIDTH] = norm[...].T
    first_t[WIDTH:] = jnp.ones((16, TOKENS), BF16)

    def seed_one(rows, down_bias):
        scaled = (branch_scale * cotangent[rows].astype(F32)).astype(BF16)
        seed[rows] = scaled
        outer[rows] = jnp.zeros((STRIP, WIDTH), F32)
        grad_norm[rows] = jnp.zeros((STRIP, WIDTH), F32)
        return down_bias + column_sum(scaled.astype(F32))

    early[3:4] = strips(seed_one, jnp.zeros((1, WIDTH), F32))
    after("seed")

    def forward_group(group, carry):
        after("group", group, 3)
        for n in range(3):
            columns = pl.ds(aligned(group * WIDTH + n * TILE, 128), TILE)
            projected = dot_nn(norm[...], wq[:, columns]) + qkv_bias[:, columns]
            wide[:, columns] = (projected * qkv_scale[:, columns]).astype(BF16)
        after("qkv", group, 3)

        def forward_pair(half, carry):
            pair = 2 * group + half
            for block in range(4):
                attend(wide, pair, block, query_side, key_side, causal, attended, logsums)
            after("pair", pair, PAIRS)
            return carry

        return lax.fori_loop(0, 2, forward_pair, carry)

    lax.fori_loop(0, 3, forward_group, 0)

    after("joined")
    for n in range(3):
        at = slice(n * TILE, n * TILE + TILE)
        branch = dot_nn(attended[...], wo[:, at]) + vectors[4:5, at]
        middle[:, at] = tokens[:, at].astype(F32) + branch_scale * branch
    after("branch")
    gain_two, offset_two = vectors[5:6], vectors[6:7]

    def norm_two(rows, carry):
        xhat, _ = standardized(middle[rows])
        norm[rows] = (xhat * gain_two + offset_two).astype(BF16)
        return carry

    strips(norm_two)
    norm_t[0:WIDTH] = norm[...].T
    norm_t[WIDTH:] = jnp.ones((16, TOKENS), BF16)
    after("norm")

    def feed_forward(step, carry):
        here = pl.ds(aligned(step * WIDTH, 128), WIDTH)
        after("step", step, 4)
        for n in range(3):
            at = slice(n * TILE, n * TILE + TILE)
            columns = pl.ds(aligned(step * WIDTH + n * TILE, 128), TILE)
            bias = vectors[pl.ds(8 + step, 1), at]
            hidden = dot_nn(norm[...], wu[:, columns]) + bias
            grad_active = dot_nt(seed[...], wd[columns])
            active, bent = gelu_and_slope(hidden)
            act[:, at] = active.astype(BF16)
            slope[:, at] = (grad_active * bent).astype(BF16)
        after("hidden", step, 4)
        for n in range(3):
            at = slice(n * TILE, n * TILE + TILE)
            outer[:, at] += dot_nn(act[...], wd[here, at])
            grad_norm[:, at] += dot_nt(slope[...], wu[at, here])
        after("outer", step, 4)
        for number in range(4):
            def sent(number=number):
                for unit in coming[6 + 2 * number : 8 + 2 * number]:
                    unit.finish()

            pl.when(step == number)(sent)
        act_t[...] = act[...].T
        for n in range(3):
            at = slice(n * TILE, n * TILE + TILE)
            columns = pl.ds(aligned(step * WIDTH + n * TILE, 128), TILE)
            grad = dot_nn(norm_t[...], slope[:, at])
            wu[:, columns] = grad[:WIDTH].astype(BF16)
            early[pl.ds(4 + step, 1), at] = grad[WIDTH : WIDTH + 1]
            wd[here, at] = dot_nn(act_t[...], seed[:, at]).astype(BF16)
        after("grads", step, 4)
        return carry

    lax.fori_loop(0, 4, feed_forward, 0)

    def back_two(rows, carry):
        mid = middle[rows]
        slope[rows] = (mid + branch_scale * (outer[rows] + vectors[7:8])).astype(BF16)
        xhat, scale = standardized(mid)
        grad = grad_norm[rows]
        grad_middle = cotangent[rows].astype(F32) + back_through_norm(grad, xhat, scale, gain_two)
        middle[rows] = grad_middle
        grad_branch = (branch_scale * grad_middle).astype(BF16)
        seed[rows] = grad_branch
        parts = (column_sum(grad_branch.astype(F32)), column_sum(grad * xhat), column_sum(grad))
        return tuple(former + part for former, part in zip(carry, parts))

    zero = jnp.zeros((1, WIDTH), F32)
    early[0:1], early[1:2], early[2:3] = strips(back_two, (zero, zero, zero))
    out_copy = pltpu.make_async_copy(slope, layer_out, local_sems.at[0])
    out_copy.start()
    after("back")

    for n in range(3):
        at = slice(n * TILE, n * TILE + TILE)
        act[:, at] = dot_nt(seed[...], wo[at]).astype(BF16)
    after("attended")
    for unit in coming[:6]:
        unit.finish()
    act_t[...] = attended[...].T
    for n in range(3):
        at = slice(n * TILE, n * TILE + TILE)
        wo[:, at] = dot_nn(act_t[...], seed[:, at]).astype(BF16)
    after("out")
    out_copy.wait()
    after("first")

    query_grad = norm_t.at[0:128]
    key_sum, value_sum = outer.at[:, 0:128], outer.at[:, 128:256]

    def backward_group(group, carry):
        def backward_pair(half, carry):
            pair = 2 * group + half
            for block in range(4):
                attend_back(
                    wide,
                    pair,
                    block,
                    query_side,
                    key_side,
                    causal,
                    attended,
                    act,
                    logsums,
                    query_grad,
                    key_sum,
                    value_sum,
                )
            first = pair * 384
            wide[:, pl.ds(aligned(first, 128), 128)] = query_grad[...].T
            wide[:, pl.ds(aligned(first + 128, 128), 128)] = key_sum[...].astype(BF16)
            wide[:, pl.ds(aligned(first + 256, 128), 128)] = value_sum[...].astype(BF16)
            after("pair_back", pair, PAIRS)
            return carry

        lax.fori_loop(0, 2, backward_pair, carry)
        for number in range(3):
            def weight_grads(number=number):
                rows = []
                for n in range(3):
                    at = slice(n * TILE, n * TILE + TILE)
                    columns = slice(number * WIDTH + n * TILE, number * WIDTH + n * TILE + TILE)
                    grad = dot_nn(first_t[...], wide[:, columns])
                    qkv_partials[number][:, at] = grad[:WIDTH].astype(BF16)
                    rows.append(grad[WIDTH : WIDTH + 1])
                row = jnp.concatenate(rows, axis=1)
                at = slice(number * 256, number * 256 + 256)
                late[2:3, at] = jnp.concatenate([row[:, 0:128], row[:, 384:512]], axis=1)
                late[3:4, at] = jnp.concatenate([row[:, 256:384], row[:, 640:768]], axis=1)
                after("qkv_grads" + str(number))

            pl.when(group == number)(weight_grads)
        return carry

    lax.fori_loop(0, 3, backward_group, 0)

    for n in range(3):
        at = slice(n * TILE, n * TILE + TILE)
        grad_norm[:, at] = dot_nt(wide[...], wq[at])
        after("tokens" + str(n))

    def back_one(rows, carry):
        xhat, scale = standardized(tokens[rows].astype(F32))
        grad = grad_norm[rows]
        middle[rows] += back_through_norm(grad, xhat, scale, gain_one)
        return carry[0] + column_sum(grad * xhat), carry[1] + column_sum(grad)

    late[0:1], late[1:2] = strips(back_one, (zero, zero))
    tokens_copy = pltpu.make_async_copy(middle, grad_tokens, local_sems.at[1])
    tokens_copy.start()
    after("half")
    up = up_target[...]
    up_out[...] = jnp.concatenate(
        [
            up[:, WIDTH * j + ROWS * d : WIDTH * j + ROWS * d + ROWS]
            for d in range(DEVICES)
            for j in range(HIDDEN_PARTS)
        ],
        axis=1,
    )
    after("last")
    back = lax.rem(DEVICES - place.number, DEVICES) * ROWS
    small_out[0:8] = pltpu.roll(early[...], back, 1)[:, 0:128]
    small_out[8:12] = pltpu.roll(late[...], back, 1)[:, 0:128]
    small_out[12:16] = jnp.zeros((4, 128), F32)
    for unit in leaving:
        unit.finish()
    tokens_copy.wait()


def layer(tokens, documents, cotangent, shards, packed):
    vmem = pl.BlockSpec(memory_space=pltpu.VMEM)
    anywhere = pl.BlockSpec(memory_space=pl.ANY)
    out_shape = [jax.ShapeDtypeStruct((TOKENS, WIDTH), BF16), jax.ShapeDtypeStruct((TOKENS, WIDTH), F32)]
    out_shape += [jax.ShapeDtypeStruct(SHARDS[n], F32) for n in NAMES]
    out_shape.append(jax.ShapeDtypeStruct((16, 128), F32))
    scratch = [
        pltpu.VMEM((WIDTH, QKV), BF16),
        pltpu.VMEM((WIDTH, WIDTH), BF16),
        pltpu.VMEM((WIDTH, HIDDEN), BF16),
        pltpu.VMEM((HIDDEN, WIDTH), BF16),
        pltpu.VMEM((TOKENS, WIDTH), BF16),
        pltpu.VMEM((TOKENS, WIDTH), BF16),
        pltpu.VMEM((TOKENS, QKV), BF16),
        pltpu.VMEM((TOKENS, WIDTH), BF16),
        pltpu.VMEM((WIDTH + 16, TOKENS), BF16),
        pltpu.VMEM((TOKENS, WIDTH), BF16),
        pltpu.VMEM((TOKENS, WIDTH), BF16),
        pltpu.VMEM((TOKENS, WIDTH), BF16),
        pltpu.VMEM((WIDTH, TOKENS), BF16),
        pltpu.VMEM((TOKENS, WIDTH), BF16),
        pltpu.VMEM((TOKENS, WIDTH), F32),
        pltpu.VMEM((TOKENS, WIDTH), F32),
        pltpu.VMEM((TOKENS, WIDTH), F32),
        pltpu.VMEM((HEADS, 1, TOKENS), F32),
        pltpu.VMEM((TOKENS, 128), BF16),
        pltpu.VMEM((TOKENS, 128), BF16),
        pltpu.VMEM((QUERY_ROWS, QUERY_ROWS), F32),
        pltpu.VMEM((16, WIDTH), F32),
        pltpu.VMEM((1, QKV), F32),
        pltpu.VMEM((1, QKV), F32),
        pltpu.VMEM((8, WIDTH), F32),
        pltpu.VMEM((4, WIDTH), F32),
        pltpu.VMEM(SHARDS["up"], BF16),
        pltpu.VMEM(SHARDS["up"], F32),
        pltpu.VMEM((WIDTH + 16, TOKENS), BF16),
    ]
    for unit in GATHER_UNITS:
        scratch += [pltpu.VMEM((32, unit[3]), BF16)] * 2
    for unit in SCATTER_UNITS:
        scratch += ScatterUnit.scratch(unit[3])
    scratch += [pltpu.SemaphoreType.DMA((len(GATHER_UNITS), GatherUnit.SEMS))] * 2
    scratch += [pltpu.SemaphoreType.DMA((len(SCATTER_UNITS), ScatterUnit.SEMS))] * 2
    for shape, dtype in (((16, WIDTH), BF16), ((8, WIDTH), F32), ((4, WIDTH), F32)):
        scratch += SmallSum.scratch(shape, dtype)
    scratch.append(pltpu.SemaphoreType.DMA((4,)))
    return pl.pallas_call(
        layer_kernel,
        name="layer",
        out_shape=out_shape,
        in_specs=[anywhere, vmem, anywhere] + [vmem] * 5,
        out_specs=[anywhere] * 2 + [vmem] * 5,
        scratch_shapes=scratch,
        compiler_params=pltpu.CompilerParams(collective_id=0, has_side_effects=True, vmem_limit_bytes=VMEM_LIMIT),
        cost_estimate=pl.CostEstimate(flops=50 * 10**9, bytes_accessed=30 * 10**6, transcendentals=20 * 10**6),
    )(tokens, documents, cotangent, *[shards[n] for n in NAMES], packed)


def results_kernel(*refs):
    sources, parts, targets, vectors = refs[:6], refs[6], refs[7:13], refs[13:22]
    held, (sems_in, sems_out) = refs[22:28], refs[28:]
    copies_in = [pltpu.make_async_copy(a, b, sems_in.at[i]) for i, (a, b) in enumerate(zip(sources, held))]
    copies_out = [pltpu.make_async_copy(a, b, sems_out.at[i]) for i, (a, b) in enumerate(zip(held, targets))]
    for copy in copies_in:
        copy.start()
    for target, row in zip(vectors, (8, 9, 10, 11, 0, 1, 2, 3)):
        target[...] = parts[row, 0:ROWS]
    vectors[8][...] = jnp.concatenate([parts[4 + j : 5 + j, 0:ROWS] for j in range(HIDDEN_PARTS)], axis=1)[0]
    for copy_in, copy_out in zip(copies_in, copies_out):
        copy_in.wait()
        copy_out.start()
    for copy in copies_out:
        copy.wait()


def results(arrays, parts):
    vmem = pl.BlockSpec(memory_space=pltpu.VMEM)
    anywhere = pl.BlockSpec(memory_space=pl.ANY)
    out_shape = [jax.ShapeDtypeStruct(a.shape, a.dtype) for a in arrays]
    out_shape += [jax.ShapeDtypeStruct((ROWS,), F32)] * 8 + [jax.ShapeDtypeStruct((ROWS * HIDDEN_PARTS,), F32)]
    scratch = [pltpu.VMEM(a.shape, a.dtype) for a in arrays]
    return pl.pallas_call(
        results_kernel,
        name="results",
        out_shape=out_shape,
        in_specs=[anywhere] * 6 + [vmem],
        out_specs=[anywhere] * 6 + [vmem] * 9,
        scratch_shapes=scratch + [pltpu.SemaphoreType.DMA((6,))] * 2,
        compiler_params=pltpu.CompilerParams(vmem_limit_bytes=VMEM_LIMIT),
    )(*arrays, parts)


def fused_device(
    tokens,
    doc_ids,
    cotangent,
    first_gain,
    first_offset,
    qkv_weight,
    query_bias,
    value_bias,
    out_weight,
    out_bias,
    second_gain,
    second_offset,
    up_weight,
    up_bias,
    down_weight,
    down_bias,
):
    shards = {"qkv": qkv_weight, "out": out_weight, "up": up_weight, "down": down_weight}
    vectors = (
        first_gain,
        first_offset,
        query_bias,
        value_bias,
        out_bias,
        second_gain,
        second_offset,
        down_bias,
        up_bias,
        jnp.zeros((96,), BF16),
    )
    packed = jnp.concatenate(vectors).astype(F32)[None]
    *arrays, parts = layer(tokens, doc_ids, cotangent, shards, packed)
    layer_out, grad_tokens, grad_qkv, grad_out, grad_up, grad_down, *small = results(arrays, parts)
    return (
        layer_out,
        grad_tokens,
        small[0],
        small[1],
        grad_qkv,
        small[2],
        small[3],
        grad_out,
        small[4],
        small[5],
        small[6],
        grad_up,
        small[8],
        grad_down,
        small[7],
    )


def solution(mesh):
    placed = (
        P(("dp", "fsdp"), None),
        P(("dp", "fsdp"), None),
        P(("dp", "fsdp"), None),
        P(("dp", "fsdp")),
        P(("dp", "fsdp")),
        P(("dp", "fsdp"), None),
        P(("dp", "fsdp")),
        P(("dp", "fsdp")),
        P(("dp", "fsdp"), None),
        P(("dp", "fsdp")),
        P(("dp", "fsdp")),
        P(("dp", "fsdp")),
        P(("dp", "fsdp"), None),
        P(("dp", "fsdp")),
        P(("dp", "fsdp"), None),
        P(("dp", "fsdp")),
    )
    return jax.shard_map(
        fused_device if fits(mesh) else plain_device,
        mesh=mesh,
        in_specs=placed,
        out_specs=(
            P(("dp", "fsdp"), None),
            P(("dp", "fsdp"), None),
            P(("dp", "fsdp")),
            P(("dp", "fsdp")),
            P(("dp", "fsdp"), None),
            P(("dp", "fsdp")),
            P(("dp", "fsdp")),
            P(("dp", "fsdp"), None),
            P(("dp", "fsdp")),
            P(("dp", "fsdp")),
            P(("dp", "fsdp")),
            P(("dp", "fsdp"), None),
            P(("dp", "fsdp")),
            P(("dp", "fsdp"), None),
            P(("dp", "fsdp")),
        ),
        check_vma=False,
    )
```

```python
import jax
import jax.numpy as jnp
from jax import lax
from jax.experimental import pallas as pl
from jax.experimental.pallas import tpu as pltpu
from jax.sharding import PartitionSpec as P

HEADS = 12
HEAD_DIM = 64


norm_eps = 1e-05
branch_scale = 48.0 ** (-0.5)


def layer_norm(values, gains, offsets):
    average = jnp.mean(values, axis=-1, keepdims=True)
    centred = values - average
    variance = jnp.mean(centred * centred, axis=-1, keepdims=True)
    return centred * lax.rsqrt(variance + norm_eps) * gains + offsets


def scaled_norm(values, gains):
    return layer_norm(values, gains, 0.0)


def dense(former, latter):
    return jnp.dot(former, latter, preferred_element_type=jnp.float32)


def contract_rows(former, latter):
    return lax.dot_general(
        former, latter, (((0,), (0,)), ((), ())), preferred_element_type=jnp.float32
    )


def contract_cols(former, latter):
    return lax.dot_general(
        former, latter, (((1,), (1,)), ((), ())), preferred_element_type=jnp.float32
    )


def block_scores(queries, keys, documents, row_start, row_stop):
    score_scale = queries.shape[2] ** (-0.5)
    scores = (
        jnp.einsum(
            "qhd,khd->hqk",
            queries[row_start:row_stop],
            keys[:row_stop],
            preferred_element_type=jnp.float32,
        )
        * score_scale
    )
    positions = jnp.arange(row_stop)
    allowed = (documents[row_start:row_stop, None] == documents[None, :row_stop]) & (
        positions[None, :] <= positions[row_start:row_stop, None]
    )
    return jnp.where(allowed[None], scores, -1e30)


def attend_row(queries, keys, values, documents):
    seq_len = queries.shape[0]
    block_rows = min(512, seq_len)
    outputs = []
    logsums = []
    for row_start in range(0, seq_len, block_rows):
        row_stop = row_start + block_rows
        scores = block_scores(queries, keys, documents, row_start, row_stop)
        highest = jnp.max(scores, axis=-1, keepdims=True)
        raised = jnp.exp(scores - highest)
        summed = jnp.sum(raised, axis=-1, keepdims=True)
        weights = (raised / summed).astype(jnp.bfloat16)
        outputs.append(
            jnp.einsum(
                "hqk,khd->qhd", weights, values[:row_stop], preferred_element_type=jnp.float32
            )
        )
        logsums.append((highest + jnp.log(summed))[..., 0])
    return (jnp.concatenate(outputs, axis=0).astype(jnp.bfloat16), jnp.concatenate(logsums, axis=1))


def attend_row_back(queries, keys, values, documents, logsums, grad_out):
    seq_len = queries.shape[0]
    block_rows = min(512, seq_len)
    score_scale = queries.shape[2] ** (-0.5)
    query_parts = []
    grad_keys = jnp.zeros(keys.shape, jnp.float32)
    grad_values = jnp.zeros(values.shape, jnp.float32)
    for row_start in range(0, seq_len, block_rows):
        row_stop = row_start + block_rows
        scores = block_scores(queries, keys, documents, row_start, row_stop)
        probs = jnp.exp(scores - logsums[:, row_start:row_stop, None])
        incoming = grad_out[row_start:row_stop]
        grad_probs = jnp.einsum(
            "qhd,khd->hqk", incoming, values[:row_stop], preferred_element_type=jnp.float32
        )
        inner_sum = jnp.sum(probs * grad_probs, axis=-1, keepdims=True)
        grad_scores = (probs * (grad_probs - inner_sum)).astype(jnp.bfloat16)
        query_parts.append(
            jnp.einsum(
                "hqk,khd->qhd", grad_scores, keys[:row_stop], preferred_element_type=jnp.float32
            )
            * score_scale
        )
        key_term = (
            jnp.einsum(
                "hqk,qhd->khd",
                grad_scores,
                queries[row_start:row_stop],
                preferred_element_type=jnp.float32,
            )
            * score_scale
        )
        value_term = jnp.einsum(
            "hqk,qhd->khd", probs.astype(jnp.bfloat16), incoming, preferred_element_type=jnp.float32
        )
        padding = ((0, seq_len - row_stop), (0, 0), (0, 0))
        grad_keys = grad_keys + jnp.pad(key_term, padding)
        grad_values = grad_values + jnp.pad(value_term, padding)
    return (jnp.concatenate(query_parts, axis=0), grad_keys, grad_values)


def plain_device(
    tokens,
    doc_ids,
    cotangent,
    first_gain,
    first_offset,
    qkv_weight,
    query_bias,
    value_bias,
    out_weight,
    out_bias,
    second_gain,
    second_offset,
    up_weight,
    up_bias,
    down_weight,
    down_bias,
):
    attn_full = (
        lax.all_gather(first_gain, ("dp", "fsdp"), axis=0, tiled=True),
        lax.all_gather(first_offset, ("dp", "fsdp"), axis=0, tiled=True),
        lax.all_gather(qkv_weight, ("dp", "fsdp"), axis=0, tiled=True),
        lax.all_gather(query_bias, ("dp", "fsdp"), axis=0, tiled=True),
        lax.all_gather(value_bias, ("dp", "fsdp"), axis=0, tiled=True),
        lax.all_gather(out_weight, ("dp", "fsdp"), axis=0, tiled=True),
        lax.all_gather(out_bias, ("dp", "fsdp"), axis=0, tiled=True),
    )
    model_width = tokens.shape[1]
    rows_here = doc_ids.shape[0]
    seq_len = doc_ids.shape[1]
    inputs = tokens.astype(jnp.float32)
    gain_one = attn_full[0].astype(jnp.float32)
    normed_one = layer_norm(inputs, gain_one, attn_full[1].astype(jnp.float32)).astype(jnp.bfloat16)
    projected = dense(normed_one, attn_full[2])
    queries = (projected[:, :model_width] + attn_full[3].astype(jnp.float32)).astype(jnp.bfloat16)
    keys = projected[:, model_width : 2 * model_width].astype(jnp.bfloat16)
    values = (projected[:, 2 * model_width :] + attn_full[4].astype(jnp.float32)).astype(
        jnp.bfloat16
    )
    row_shape = (rows_here, seq_len, HEADS, HEAD_DIM)
    queries = queries.reshape(row_shape)
    keys = keys.reshape(row_shape)
    values = values.reshape(row_shape)
    attended, logsums = lax.map(
        lambda row_item: attend_row(*row_item), (queries, keys, values, doc_ids)
    )
    attended = attended.reshape(-1, model_width)
    branch = dense(attended, attn_full[5]) + attn_full[6].astype(jnp.float32)
    middle = inputs + branch_scale * branch
    mlp_full = (
        lax.all_gather(second_gain, ("dp", "fsdp"), axis=0, tiled=True),
        lax.all_gather(second_offset, ("dp", "fsdp"), axis=0, tiled=True),
        lax.all_gather(up_weight, ("dp", "fsdp"), axis=0, tiled=True),
        lax.all_gather(up_bias, ("dp", "fsdp"), axis=0, tiled=True),
        lax.all_gather(down_weight, ("dp", "fsdp"), axis=0, tiled=True),
        lax.all_gather(down_bias, ("dp", "fsdp"), axis=0, tiled=True),
    )
    gain_two = mlp_full[0].astype(jnp.float32)
    normed_two = layer_norm(middle, gain_two, mlp_full[1].astype(jnp.float32)).astype(jnp.bfloat16)
    hidden = dense(normed_two, mlp_full[2]) + mlp_full[3].astype(jnp.float32)
    active, gelu_back = jax.vjp(lambda pre_act: jax.nn.gelu(pre_act, approximate=True), hidden)
    active = active.astype(jnp.bfloat16)
    outer = dense(active, mlp_full[4]) + mlp_full[5].astype(jnp.float32)
    layer_out = (middle + branch_scale * outer).astype(jnp.bfloat16)
    mlp_back = (
        lax.all_gather(second_gain, ("dp", "fsdp"), axis=0, tiled=True),
        lax.all_gather(up_weight, ("dp", "fsdp"), axis=0, tiled=True),
        lax.all_gather(down_weight, ("dp", "fsdp"), axis=0, tiled=True),
    )
    seed = cotangent.astype(jnp.float32)
    grad_outer = (branch_scale * seed).astype(jnp.bfloat16)
    grad_down_bias = jnp.sum(grad_outer.astype(jnp.float32), axis=0)
    grad_down_weight = contract_rows(active, grad_outer)
    grad_active = contract_cols(grad_outer, mlp_back[2])
    grad_hidden = gelu_back(grad_active)[0].astype(jnp.bfloat16)
    grad_up_bias = jnp.sum(grad_hidden.astype(jnp.float32), axis=0)
    grad_up_weight = contract_rows(normed_two, grad_hidden)
    grad_normed_two = contract_cols(grad_hidden, mlp_back[1])
    _, norm_two_back = jax.vjp(scaled_norm, middle, mlp_back[0].astype(jnp.float32))
    grad_middle_part, grad_second_gain = norm_two_back(grad_normed_two)
    grad_second_offset = jnp.sum(grad_normed_two, axis=0)
    grad_middle = seed + grad_middle_part
    mlp_shares = (
        grad_second_gain,
        grad_second_offset,
        grad_up_weight,
        grad_up_bias,
        grad_down_weight,
        grad_down_bias,
    )
    attn_back = (
        lax.all_gather(first_gain, ("dp", "fsdp"), axis=0, tiled=True),
        lax.all_gather(qkv_weight, ("dp", "fsdp"), axis=0, tiled=True),
        lax.all_gather(out_weight, ("dp", "fsdp"), axis=0, tiled=True),
    )
    grad_branch = (branch_scale * grad_middle).astype(jnp.bfloat16)
    grad_out_bias = jnp.sum(grad_branch.astype(jnp.float32), axis=0)
    grad_out_weight = contract_rows(attended, grad_branch)
    grad_attended = contract_cols(grad_branch, attn_back[2]).astype(jnp.bfloat16).reshape(row_shape)
    grad_queries, grad_keys, grad_values = lax.map(
        lambda row_item: attend_row_back(*row_item),
        (queries, keys, values, doc_ids, logsums, grad_attended),
    )
    grad_projected = jnp.concatenate(
        [
            grad_queries.reshape(-1, model_width),
            grad_keys.reshape(-1, model_width),
            grad_values.reshape(-1, model_width),
        ],
        axis=1,
    ).astype(jnp.bfloat16)
    grad_wide = grad_projected.astype(jnp.float32)
    grad_query_bias = jnp.sum(grad_wide[:, :model_width], axis=0)
    grad_value_bias = jnp.sum(grad_wide[:, 2 * model_width :], axis=0)
    grad_qkv_weight = contract_rows(normed_one, grad_projected)
    grad_normed_one = contract_cols(grad_projected, attn_back[1])
    _, norm_one_back = jax.vjp(scaled_norm, inputs, attn_back[0].astype(jnp.float32))
    grad_input_part, grad_first_gain = norm_one_back(grad_normed_one)
    grad_first_offset = jnp.sum(grad_normed_one, axis=0)
    grad_tokens = grad_middle + grad_input_part
    every_share = (
        lax.psum_scatter(grad_second_gain, ("dp", "fsdp"), scatter_dimension=0, tiled=True),
        lax.psum_scatter(grad_second_offset, ("dp", "fsdp"), scatter_dimension=0, tiled=True),
        lax.psum_scatter(grad_up_weight, ("dp", "fsdp"), scatter_dimension=0, tiled=True),
        lax.psum_scatter(grad_up_bias, ("dp", "fsdp"), scatter_dimension=0, tiled=True),
        lax.psum_scatter(grad_down_weight, ("dp", "fsdp"), scatter_dimension=0, tiled=True),
        lax.psum_scatter(grad_down_bias, ("dp", "fsdp"), scatter_dimension=0, tiled=True),
        lax.psum_scatter(grad_first_gain, ("dp", "fsdp"), scatter_dimension=0, tiled=True),
        lax.psum_scatter(grad_first_offset, ("dp", "fsdp"), scatter_dimension=0, tiled=True),
        lax.psum_scatter(grad_qkv_weight, ("dp", "fsdp"), scatter_dimension=0, tiled=True),
        lax.psum_scatter(grad_query_bias, ("dp", "fsdp"), scatter_dimension=0, tiled=True),
        lax.psum_scatter(grad_value_bias, ("dp", "fsdp"), scatter_dimension=0, tiled=True),
        lax.psum_scatter(grad_out_weight, ("dp", "fsdp"), scatter_dimension=0, tiled=True),
        lax.psum_scatter(grad_out_bias, ("dp", "fsdp"), scatter_dimension=0, tiled=True),
    )
    mlp_shares = every_share[:6]
    attn_shares = every_share[6:]
    return (
        layer_out,
        grad_tokens,
        attn_shares[0],
        attn_shares[1],
        attn_shares[2],
        attn_shares[3],
        attn_shares[4],
        attn_shares[5],
        attn_shares[6],
        mlp_shares[0],
        mlp_shares[1],
        mlp_shares[2],
        mlp_shares[3],
        mlp_shares[4],
        mlp_shares[5],
    )


MESH = pl.DeviceIdType.MESH
F32 = jnp.float32
BF16 = jnp.bfloat16
WIDTH = 768
HIDDEN = 3072
TOKENS = 1024
QKV = 3 * WIDTH
PAIRS = 6
QUERY_ROWS = 256
KEY_WINDOWS = ((0, 256), (0, 512), (0, 768), (256, 1024))
DOCUMENTS = 6
FAR_BELOW = 2.0**100
STRIP = 256
TILE = 256
VMEM_LIMIT = 63 * 2**20
GELU_A = 0.7978845608028654
GELU_B = 0.044715

GATHER_UNITS = tuple(("qkv", 0, first, 128) for first in (0, 128, 256))
GATHER_UNITS += (("qkv", 1, 0, 384), ("qkv", 2, 0, 384), ("out", 0, 0, 384))
GATHER_UNITS += tuple((name, part, 0, 384) for part in range(4) for name in ("up", "down"))
SCATTER_UNITS = GATHER_UNITS[6:] + (("out", 0, 0, 384), ("qkv", 0, 0, 384), ("qkv", 1, 0, 384))
SCATTER_UNITS += tuple(("qkv", 2, first, 128) for first in (0, 128, 256))
ROWS = 24
HALF = 384
SHARDS = {"qkv": (24, 2304), "out": (24, 768), "up": (24, 3072), "down": (96, 768)}
NAMES = ("qkv", "out", "up", "down")
DEVICES = 32
HIDDEN_PARTS = 4


def fits(mesh):
    return mesh.shape["dp"] == 4 and mesh.shape["fsdp"] == 8


def aligned(value, step):
    return pl.multiple_of(value, step)


def dot_nt(a, b):
    return lax.dot_general(a, b, (((1,), (1,)), ((), ())), preferred_element_type=F32)


def dot_nn(a, b):
    return lax.dot_general(a, b, (((1,), (0,)), ((), ())), preferred_element_type=F32)


def dot_tn(a, b):
    return lax.dot_general(a, b, (((0,), (0,)), ((), ())), preferred_element_type=F32)


class Place:
    def __init__(self):
        self.dp = lax.axis_index("dp")
        self.fsdp = lax.axis_index("fsdp")
        self.core = lax.rem(self.fsdp, 2)
        self.z = lax.div(self.fsdp, 2)
        x = lax.rem(self.dp, 2)
        y = lax.div(self.dp, 2)
        self.dp_x = y * 2 + (1 - x)
        self.dp_y = (1 - y) * 2 + x
        self.dp_far = 3 - self.dp
        core = self.core
        self.near = self.dp_x * (1 - core) + self.dp_y * core
        self.next = self.dp_y * (1 - core) + self.dp_x * core
        self.chip = self.dp * 4 + self.z
        self.number = self.dp * 8 + self.fsdp
        self.partner = (self.dp, self.z * 2 + (1 - core))
        self.at_near = (self.near, self.fsdp)
        self.at_next = (self.next, self.fsdp)

    def along_z(self, step):
        z = lax.rem(self.z + step, 4)
        return (self.dp, z * 2 + self.core)

    def greet(self):
        barrier = pltpu.get_barrier_semaphore()
        others = [self.partner, (self.dp_x, self.fsdp), (self.dp_y, self.fsdp), (self.dp_far, self.fsdp)]
        others += [self.along_z(step) for step in (1, 2, 3)]
        for other in others:
            pl.semaphore_signal(barrier, inc=1, device_id=other, device_id_type=MESH)
        pl.semaphore_wait(barrier, len(others))


def remote(source, target, sems, index, device):
    return pltpu.make_async_remote_copy(
        src_ref=source,
        dst_ref=target,
        send_sem=sems[0].at[index],
        recv_sem=sems[1].at[index],
        device_id=device,
        device_id_type=MESH,
    )


class SmallSum:
    def __init__(self, place, source, target, buffers, landed, send_sems, recv_sems):
        self.place, self.source, self.target = place, source, target
        self.buffers, self.landed, self.sems = buffers, landed, (send_sems, recv_sems)

    @staticmethod
    def scratch(shape, dtype):
        return [
            pltpu.VMEM((3, *shape), dtype),
            pltpu.VMEM((7, *shape), dtype),
            pltpu.SemaphoreType.DMA((7,)),
            pltpu.SemaphoreType.DMA((7,)),
        ]

    def copies(self, stage):
        p = self.place
        if stage == 0:
            devices = [p.partner]
        elif stage == 1:
            devices = [(dp, p.fsdp) for dp in (p.dp_x, p.dp_y, p.dp_far)]
        else:
            devices = [p.along_z(step) for step in (1, 2, 3)]
        first = (0, 1, 4)[stage]
        return [
            remote(self.buffers.at[stage], self.landed.at[first + i], self.sems, first + i, device)
            for i, device in enumerate(devices)
        ]

    def begin(self):
        self.buffers[0] = self.source[...].astype(self.buffers.dtype)
        for copy in self.copies(0):
            copy.start()

    def middle(self):
        for copy in self.copies(0):
            copy.wait()
        self.buffers[1] = self.buffers[0] + self.landed[0]
        for copy in self.copies(1):
            copy.start()

    def later(self):
        for copy in self.copies(1):
            copy.wait()
        self.buffers[2] = (self.buffers[1] + self.landed[1]) + (self.landed[2] + self.landed[3])
        for copy in self.copies(2):
            copy.start()

    def end(self):
        for copy in self.copies(2):
            copy.wait()
        total = (self.buffers[2] + self.landed[4]) + (self.landed[5] + self.landed[6])
        self.target[...] = total.astype(self.target.dtype)


class GatherUnit:
    SEMS = 11

    def __init__(self, place, unit, shard, full, pair_out, pair_in, send_sems, recv_sems):
        self.place = place
        self.name, self.part, self.first, self.width = unit
        self.shard, self.full = shard, full
        self.pair_out, self.pair_in = pair_out, pair_in
        self.sems = (send_sems, recv_sems)

    def columns_of(self, core):
        if self.name == "qkv":
            start = 2 * self.part * 128 + 128 * core
            chosen = range(self.first // 128, (self.first + self.width) // 128)
            parts = [self.shard[:, pl.ds(aligned(start + WIDTH * i, 128), 128)] for i in chosen]
            return jnp.concatenate(parts, axis=1).astype(F32)
        start = WIDTH * self.part if self.name == "up" else 0
        columns = self.shard[:, pl.ds(aligned(start + HALF * core + self.first, 128), self.width)].astype(F32)
        return columns[ROWS * self.part : ROWS * self.part + ROWS] if self.name == "down" else columns

    def rows_at(self, first, count):
        columns = pl.ds(aligned(HALF * self.place.core + self.first, 128), self.width)
        return self.full.at[pl.ds(aligned(first, 16), count), columns]

    def group(self, dp):
        return self.rows_at(dp * (8 * ROWS), 8 * ROWS)

    def block(self, dp=None):
        chip = self.place.chip if dp is None else dp * 4 + self.place.z
        return self.rows_at(chip * (2 * ROWS), 2 * ROWS)

    def copy(self, index):
        p = self.place
        if index == 0:
            return remote(self.pair_out, self.pair_in, self.sems, 0, p.partner)
        if index < 4:
            return remote(self.block(), self.block(), self.sems, index, p.along_z(index))
        dp = (p.dp, p.dp, p.near, p.dp, p.near, p.next, p.dp_far)[index - 4]
        device = p.at_near if index == 4 else p.at_next if index < 7 else p.partner
        return remote(self.group(dp), self.group(dp), self.sems, index, device)

    def start(self, *indices):
        for index in indices:
            self.copy(index).start()

    def landed(self, *indices):
        for index in indices:
            self.copy(index).wait_recv()

    def pair(self):
        self.pair_out[0:ROWS] = self.columns_of(1 - self.place.core).astype(BF16)
        self.pair_out[ROWS:] = jnp.zeros((32 - ROWS, self.width), BF16)
        self.start(0)

    def assemble(self):
        self.landed(0)
        own = self.columns_of(self.place.core)
        came = self.pair_in[0:ROWS].astype(F32)
        first = self.place.core == 0
        block = jnp.concatenate([jnp.where(first, own, came), jnp.where(first, came, own)], axis=0)
        self.block()[...] = block.astype(BF16)

    def along_z(self):
        self.assemble()
        self.start(1, 2, 3)

    def to_near(self):
        self.landed(1, 2, 3)
        self.start(4, 7)

    def to_next(self):
        self.landed(4)
        self.start(5, 6, 8)

    def to_core(self):
        self.landed(5)
        self.start(9)
        self.landed(6)
        self.start(10)

    def arrived(self):
        self.landed(7, 8, 9, 10)

    def finish(self, last=0):
        for index in range(self.SEMS - last):
            self.copy(index).wait_send()


class ScatterUnit:
    SEMS = 8

    def __init__(self, place, unit, partial, target, halves, from_next, from_near, from_z, pair, send_sems, recv_sems):
        self.place = place
        self.name, self.part, self.first, self.width = unit
        self.partial, self.target = partial, target
        self.halves, self.from_next, self.from_near = halves, from_next, from_near
        self.from_z, self.pair_buffer = from_z, pair
        self.sems = (send_sems, recv_sems)

    @staticmethod
    def scratch(width):
        return [
            pltpu.VMEM((WIDTH, width), BF16),
            pltpu.VMEM((2, 8 * ROWS, width), BF16),
            pltpu.VMEM((8 * ROWS, width), BF16),
            pltpu.VMEM((3, 2 * ROWS, width), BF16),
            pltpu.VMEM((3, ROWS, width), F32),
        ]

    def columns(self, core):
        return pl.ds(aligned(HALF * core + self.first, 128), self.width)

    def group(self, dp):
        return self.halves.at[pl.ds(aligned(dp * (8 * ROWS), 16), 8 * ROWS)]

    def z_block(self, step, dp=None):
        chip = (self.place.dp if dp is None else dp) * 4 + lax.rem(self.place.z + step, 4)
        return self.halves.at[pl.ds(aligned(chip * (2 * ROWS), 16), 2 * ROWS)]

    def copy(self, index):
        p = self.place
        if index == 0:
            source = self.partial.at[pl.ds(0, WIDTH), self.columns(1 - p.core)]
            return remote(source, self.halves, self.sems, 0, p.partner)
        if index < 3:
            dp = (p.next, p.dp_far)[index - 1]
            return remote(self.group(dp), self.from_next.at[index - 1], self.sems, index, p.at_next)
        if index == 3:
            return remote(self.group(p.near), self.from_near, self.sems, 3, p.at_near)
        if index < 7:
            step = index - 3
            return remote(self.z_block(step), self.from_z.at[step - 1], self.sems, index, p.along_z(step))
        return remote(self.pair_buffer.at[0], self.pair_buffer.at[2], self.sems, 7, p.partner)

    def start(self, *indices):
        for index in indices:
            self.copy(index).start()

    def landed(self, *indices):
        for index in indices:
            self.copy(index).wait_recv()

    def add(self, former, latter, rows):
        step = 192

        def body(index, carry):
            at = pl.ds(aligned(index * step, 16), step)
            former[at] = former[at] + latter(at)
            return carry

        lax.fori_loop(0, rows // step, body, 0)

    def to_partner(self):
        self.start(0)

    def to_next(self):
        self.landed(0)
        mine = self.columns(self.place.core)
        self.add(self.halves, lambda at: self.partial[at, mine], WIDTH)
        self.start(1, 2)

    def to_near(self):
        p = self.place
        self.landed(1, 2)
        self.add(self.group(p.near), lambda at: self.from_next[1, at], 8 * ROWS)
        self.start(3)
        self.add(self.group(p.dp), lambda at: self.from_next[0, at], 8 * ROWS)

    def along_z(self):
        self.landed(3)
        self.add(self.group(self.place.dp), lambda at: self.from_near[at], 8 * ROWS)
        self.start(4, 5, 6)

    def to_pair(self):
        self.landed(4, 5, 6)
        came = [self.from_z[i].astype(F32) for i in range(3)]
        self.halve((self.z_block(0)[...].astype(F32) + came[0]) + (came[1] + came[2]))
        self.start(7)

    def halve(self, block):
        first = self.place.core == 0
        self.pair_buffer[0] = jnp.where(first, block[ROWS:], block[:ROWS])
        self.pair_buffer[1] = jnp.where(first, block[:ROWS], block[ROWS:])

    def store(self):
        self.landed(7)
        self.put()

    def put(self):
        for source, core in ((1, self.place.core), (2, 1 - self.place.core)):
            if self.name == "qkv":
                start = 2 * self.part * 128 + 128 * core
                for number in range(self.width // 128):
                    columns = pl.ds(aligned(start + WIDTH * (self.first // 128 + number), 128), 128)
                    self.target[:, columns] = self.pair_buffer[source, :, 128 * number : 128 * number + 128]
            elif self.name == "down":
                self.target[ROWS * self.part : ROWS * self.part + ROWS, self.columns(core)] = self.pair_buffer[source]
            else:
                start = WIDTH * self.part + HALF * core + self.first
                self.target[:, pl.ds(aligned(start, 128), self.width)] = self.pair_buffer[source]

    def finish(self, last=0):
        for index in range(self.SEMS - last):
            self.copy(index).wait_send()


class Stage:
    def __init__(self, kind, method):
        self.kind, self.method = kind, method

    def __getitem__(self, unit):
        return self.kind, self.method, unit


p, z, n = Stage(0, "pair"), Stage(0, "along_z"), Stage(0, "to_near")
x, c, r = Stage(0, "to_next"), Stage(0, "to_core"), Stage(0, "arrived")
G, A, B = Stage(1, "to_partner"), Stage(1, "to_next"), Stage(1, "to_near")
Z, D, S = Stage(1, "along_z"), Stage(1, "to_pair"), Stage(1, "store")
b, m, l, e = Stage(2, "begin"), Stage(2, "middle"), Stage(2, "later"), Stage(2, "end")


def strips(body, carry=0):
    def run(index, carry):
        return body(pl.ds(aligned(index * STRIP, STRIP), STRIP), carry)

    return lax.fori_loop(0, TOKENS // STRIP, run, carry)


def standardized(values):
    average = jnp.mean(values, axis=-1, keepdims=True)
    centred = values - average
    variance = jnp.mean(centred * centred, axis=-1, keepdims=True)
    scale = lax.rsqrt(variance + norm_eps)
    return centred * scale, scale


def back_through_norm(grad, xhat, scale, gains):
    lifted = grad * gains
    return scale * (
        lifted
        - jnp.mean(lifted, axis=-1, keepdims=True)
        - xhat * jnp.mean(lifted * xhat, axis=-1, keepdims=True)
    )


def column_sum(values):
    return jnp.sum(values, axis=0, keepdims=True)


def gelu_and_slope(h):
    square = h * h
    bent = GELU_A + GELU_A * GELU_B * square
    gate = 0.5 + 0.5 * jnp.tanh(h * bent)
    active = h * gate
    slope = gate + active * (1.0 - gate) * (6.0 * bent - 4.0 * GELU_A)
    return active, slope


def document_lanes(documents, query_side, key_side):
    lane = lax.rem(lax.broadcasted_iota(jnp.int32, (TOKENS, 128), 1), 64)
    own = jnp.broadcast_to(documents.astype(F32), (128, TOKENS)).T == lane.astype(F32)
    query_side[...] = jnp.where(own, 1.0, 0.0).astype(BF16)
    key_side[...] = jnp.where(own | (lane >= DOCUMENTS), 0.0, -FAR_BELOW).astype(BF16)


def causal_corner(causal):
    key = lax.broadcasted_iota(jnp.int32, (QUERY_ROWS, QUERY_ROWS), 0)
    query = lax.broadcasted_iota(jnp.int32, (QUERY_ROWS, QUERY_ROWS), 1)
    causal[...] = jnp.where(key <= query, 0.0, -FAR_BELOW)


class Pair:
    def __init__(self, wide, pair, block, query_side, key_side):
        start, stop = KEY_WINDOWS[block]
        self.keys = pl.ds(start, stop - start)
        self.rows = pl.ds(block * QUERY_ROWS, QUERY_ROWS)
        first = pair * 384
        self.at = [pl.ds(aligned(first + 128 * i, 128), 128) for i in range(3)]
        self.q = wide[self.rows, self.at[0]]
        self.k = wide[self.keys, self.at[1]]
        self.v = wide[self.keys, self.at[2]]
        self.query_side, self.key_side = query_side[self.rows], key_side[self.keys]
        self.start, self.stop = start, stop

    def choose(self, head, inside, outside):
        low = lax.broadcasted_iota(jnp.int32, inside.shape, 1) < 64
        return jnp.where(low, inside, outside) if head == 0 else jnp.where(low, outside, inside)

    def only(self, head, values):
        return self.choose(head, values, jnp.zeros_like(values))

    def scores(self, head, causal):
        scores = dot_nt(self.choose(head, self.k, self.key_side), self.choose(head, self.q, self.query_side))
        wide = self.stop - self.start - QUERY_ROWS
        corner = scores[wide:] + causal[...]
        return jnp.concatenate([scores[:wide], corner], axis=0) if wide else corner


def attend(wide, pair, block, query_side, key_side, causal, attended, logsums):
    p = Pair(wide, pair, block, query_side, key_side)
    weights, sums = [], []
    for head in range(2):
        scores = p.scores(head, causal)
        highest = jnp.max(scores, axis=0, keepdims=True)
        raised = jnp.exp(scores - highest)
        summed = column_sum(raised)
        weights.append(raised.astype(BF16))
        sums.append(jnp.broadcast_to(summed, (HEAD_DIM, QUERY_ROWS)))
        logsums[2 * pair + head, :, p.rows] = highest + jnp.log(summed)
    values = jnp.concatenate([p.only(head, p.v) for head in range(2)], axis=0)
    out = dot_tn(values, jnp.concatenate(weights, axis=0)) / jnp.concatenate(sums, axis=0)
    attended[p.rows, pl.ds(aligned(pair * 128, 128), 128)] = out.T.astype(BF16)


def attend_back(
    wide, pair, block, query_side, key_side, causal, attended, grad_attended, logsums, query_grad, key_sum, value_sum
):
    p = Pair(wide, pair, block, query_side, key_side)
    features = pl.ds(aligned(pair * 128, 128), 128)
    incoming = grad_attended[p.rows, features]
    inner = (incoming.astype(F32) * attended[p.rows, features].astype(F32)).T
    probs, slopes = [], []
    for head in range(2):
        delta = column_sum(inner[64 * head : 64 * head + 64])
        prob = jnp.exp(p.scores(head, causal) - logsums[2 * pair + head, :, p.rows])
        grad_prob = dot_nt(p.v, p.only(head, incoming))
        probs.append(prob.astype(BF16))
        slopes.append((prob * (grad_prob - delta)).astype(BF16))
    both = lambda values: jnp.concatenate([p.only(head, values) for head in range(2)], axis=0)
    value_part = dot_nn(jnp.concatenate(probs, axis=1), both(incoming))
    key_part = dot_nn(jnp.concatenate(slopes, axis=1), both(p.q))
    query_part = dot_tn(both(p.k), jnp.concatenate(slopes, axis=0))
    query_grad[:, p.rows] = (query_part * HEAD_DIM**-0.5).astype(BF16)
    inside = p.stop - p.start - QUERY_ROWS
    if inside:
        earlier = pl.ds(p.start, inside)
        key_sum[earlier] += key_part[:inside]
        value_sum[earlier] += value_part[:inside]
    newest = pl.ds(p.stop - QUERY_ROWS, QUERY_ROWS)
    key_sum[newest] = key_part[inside:]
    value_sum[newest] = value_part[inside:]


PLAN = dict(
        greet=(p[1], p[4],),
        packed=(p[8], p[5], p[2], p[12], z[1], p[10], p[0], p[6], b[0], z[2], m[0], p[7], p[3], p[11], z[0],
        z[3],),
        documents=(n[1], p[13], n[2], n[0], z[4], z[5], l[0], z[6], p[9], x[1],),
        vectors=(z[7], z[8], x[2], n[3], z[9], c[1], x[0], n[4], x[3], c[0], z[13], x[4], n[5], r[1], c[2],
        e[0],),
        one=(r[0], c[3],),
        seed=(n[6], r[2],),
        qkv0=(x[5],),
        pair0=(n[7], c[4],),
        pair1=(z[11],),
        group1=(n[8], z[10], r[3],),
        qkv1=(x[6], r[4], n[9], z[12],),
        pair2=(x[7],),
        qkv2=(x[9], c[5],),
        pair5=(x[8], n[10],),
        joined=(c[6], r[5],),
        branch=(c[7],),
        norm=(r[6],),
        step0=(r[7], n[12], n[11], c[9], n[13],),
        hidden0=(x[10], r[9],),
        outer0=(c[8],),
        step1=(G[0], x[11], r[8], G[1],),
        hidden1=(A[0], c[10], x[12],),
        outer1=(c[11], r[10],),
        grads1=(x[13], G[3], r[11],),
        step2=(A[1],),
        hidden2=(c[12],),
        outer2=(G[2], A[3], c[13],),
        grads2=(A[2],),
        step3=(B[1], r[12], G[5], r[13],),
        hidden3=(B[0], G[4],),
        outer3=(A[4], A[5],),
        grads3=(G[6], B[2],),
        back=(B[3], Z[0],),
        attended=(Z[1], A[6], b[1],),
        first=(G[7], B[4],),
        pair_back0=(m[1], A[7], Z[2],),
        pair_back1=(Z[4],),
        qkv_grads0=(l[1], B[5], G[8], Z[3], G[9], B[6],),
        pair_back2=(A[9],),
        pair_back3=(B[7],),
        qkv_grads1=(Z[5], A[8], Z[6], G[10],),
        pair_back4=(A[10], Z[7], B[9],),
        qkv_grads2=(G[12], D[1], G[13], B[8],),
        tokens0=(Z[9], G[11], D[2], D[0], A[12], D[4], B[10],),
        tokens1=(A[13], Z[8], A[11],),
        half=(Z[10], B[13], b[2], D[3], B[12], m[2], D[5], D[6], B[11], S[5], e[1], D[9], Z[13], S[3], Z[12],
        Z[11], S[6], S[0], S[2], S[4],),
        last=(D[7], D[8], l[2], D[13], S[1], D[10], S[7], S[8], S[9], S[13], D[12], D[11], S[12], S[10], e[2],
        S[11],),
)


def layer_kernel(*refs):
    refs = list(refs)

    def take(count):
        taken = refs[:count]
        del refs[:count]
        return taken

    tokens_in, documents, cotangent_in = take(3)
    shards = dict(zip(NAMES, take(4)))
    (packed,) = take(1)
    layer_out, grad_tokens = take(2)
    targets = dict(zip(NAMES, take(4)))
    (small_out,) = take(1)
    wq, wo, wu, wd = take(4)
    tokens, cotangent, wide, norm, norm_t, attended, seed, act, act_t, slope = take(10)
    middle, outer, grad_norm = take(3)
    logsums, query_side, key_side, causal, vectors, qkv_bias, qkv_scale, early = take(8)
    late, up_shard, up_target, first_t = take(4)
    pair_buffers = take(2 * len(GATHER_UNITS))
    scatter_buffers = take(5 * len(SCATTER_UNITS))
    gather_sems, scatter_sems = take(2), take(2)
    small_refs = [take(4) for _ in range(3)]
    (local_sems,) = take(1)

    place = Place()
    up_natural, shards["up"] = shards["up"], up_shard
    up_out, targets["up"] = targets["up"], up_target

    def part(index):
        return slice(WIDTH * index, WIDTH * index + WIDTH)

    def whole(name, index):
        if name == "out":
            return wo
        return wd.at[part(index)] if name == "down" else {"qkv": wq, "up": wu}[name].at[:, part(index)]

    coming = [
        GatherUnit(
            place,
            unit,
            shards[unit[0]],
            whole(*unit[:2]),
            *pair_buffers[2 * i : 2 * i + 2],
            gather_sems[0].at[i],
            gather_sems[1].at[i],
        )
        for i, unit in enumerate(GATHER_UNITS)
    ]
    qkv_partials = (slope.at[0:WIDTH], act_t.at[:, 0:WIDTH], norm.at[0:WIDTH])
    leaving = [
        ScatterUnit(
            place,
            unit,
            qkv_partials[unit[1]] if unit[0] == "qkv" else whole(*unit[:2]),
            targets[unit[0]],
            *scatter_buffers[5 * i : 5 * i + 5],
            scatter_sems[0].at[i],
            scatter_sems[1].at[i],
        )
        for i, unit in enumerate(SCATTER_UNITS)
    ]

    vector_sums = [
        SmallSum(place, source, target, *refs)
        for source, target, refs in zip((vectors, early, late), (vectors, early, late), small_refs)
    ]

    def run(steps):
        for kind, method, unit in steps:
            getattr((coming, leaving, vector_sums)[kind][unit], method)()

    def after(name, index=None, count=0):
        if index is None:
            run(PLAN.get(name, ()))
            return
        for number in range(count):
            steps = PLAN.get(name + str(number), ())
            if steps:
                pl.when(index == number)(lambda steps=steps: run(steps))

    loads = [
        pltpu.make_async_copy(source, target, local_sems.at[2 + i])
        for i, (source, target) in enumerate(((tokens_in, tokens), (cotangent_in, cotangent)))
    ]
    for load in loads:
        load.start()
    vectors[...] = jnp.zeros_like(vectors)
    for row in range(12):
        vectors[row : row + 1, 0:ROWS] = packed[:, ROWS * row : ROWS * row + ROWS]
    vectors[...] = pltpu.roll(vectors[...], place.number * ROWS, 1)
    place.greet()
    after("greet")
    up = up_natural[...].astype(F32)
    step = ROWS * HIDDEN_PARTS
    up_shard[...] = jnp.concatenate(
        [up[:, step * d + ROWS * j : step * d + ROWS * j + ROWS] for j in range(HIDDEN_PARTS) for d in range(DEVICES)],
        axis=1,
    ).astype(BF16)
    after("packed")
    document_lanes(documents[...], query_side, key_side)
    causal_corner(causal)
    after("documents")
    for load in loads:
        load.wait()
    after("vectors")
    gain_one, offset_one = vectors[0:1], vectors[1:2]
    for pair in range(PAIRS):
        at = slice(128 * pair, 128 * pair + 128)
        first = 384 * pair
        qkv_bias[:, first : first + 128] = vectors[2:3, at]
        qkv_bias[:, first + 128 : first + 256] = jnp.zeros((1, 128), F32)
        qkv_bias[:, first + 256 : first + 384] = vectors[3:4, at]
        qkv_scale[:, first : first + 128] = jnp.full((1, 128), HEAD_DIM**-0.5, F32)
        qkv_scale[:, first + 128 : first + 384] = jnp.ones((1, 256), F32)

    def norm_one(rows, carry):
        xhat, _ = standardized(tokens[rows].astype(F32))
        norm[rows] = (xhat * gain_one + offset_one).astype(BF16)
        return carry

    strips(norm_one)
    after("one")
    first_t[0:WIDTH] = norm[...].T
    first_t[WIDTH:] = jnp.ones((16, TOKENS), BF16)

    def seed_one(rows, down_bias):
        scaled = (branch_scale * cotangent[rows].astype(F32)).astype(BF16)
        seed[rows] = scaled
        outer[rows] = jnp.zeros((STRIP, WIDTH), F32)
        grad_norm[rows] = jnp.zeros((STRIP, WIDTH), F32)
        return down_bias + column_sum(scaled.astype(F32))

    early[3:4] = strips(seed_one, jnp.zeros((1, WIDTH), F32))
    after("seed")

    def forward_group(group, carry):
        after("group", group, 3)
        for n in range(3):
            columns = pl.ds(aligned(group * WIDTH + n * TILE, 128), TILE)
            projected = dot_nn(norm[...], wq[:, columns]) + qkv_bias[:, columns]
            wide[:, columns] = (projected * qkv_scale[:, columns]).astype(BF16)
        after("qkv", group, 3)

        def forward_pair(half, carry):
            pair = 2 * group + half
            for block in range(4):
                attend(wide, pair, block, query_side, key_side, causal, attended, logsums)
            after("pair", pair, PAIRS)
            return carry

        return lax.fori_loop(0, 2, forward_pair, carry)

    lax.fori_loop(0, 3, forward_group, 0)

    after("joined")
    for n in range(3):
        at = slice(n * TILE, n * TILE + TILE)
        branch = dot_nn(attended[...], wo[:, at]) + vectors[4:5, at]
        middle[:, at] = tokens[:, at].astype(F32) + branch_scale * branch
    after("branch")
    gain_two, offset_two = vectors[5:6], vectors[6:7]

    def norm_two(rows, carry):
        xhat, _ = standardized(middle[rows])
        norm[rows] = (xhat * gain_two + offset_two).astype(BF16)
        return carry

    strips(norm_two)
    norm_t[0:WIDTH] = norm[...].T
    norm_t[WIDTH:] = jnp.ones((16, TOKENS), BF16)
    after("norm")

    def feed_forward(step, carry):
        here = pl.ds(aligned(step * WIDTH, 128), WIDTH)
        after("step", step, 4)
        for n in range(3):
            at = slice(n * TILE, n * TILE + TILE)
            columns = pl.ds(aligned(step * WIDTH + n * TILE, 128), TILE)
            bias = vectors[pl.ds(8 + step, 1), at]
            hidden = dot_nn(norm[...], wu[:, columns]) + bias
            grad_active = dot_nt(seed[...], wd[columns])
            active, bent = gelu_and_slope(hidden)
            act[:, at] = active.astype(BF16)
            slope[:, at] = (grad_active * bent).astype(BF16)
        after("hidden", step, 4)
        for n in range(3):
            at = slice(n * TILE, n * TILE + TILE)
            outer[:, at] += dot_nn(act[...], wd[here, at])
            grad_norm[:, at] += dot_nt(slope[...], wu[at, here])
        after("outer", step, 4)
        for number in range(4):
            def sent(number=number):
                for unit in coming[6 + 2 * number : 8 + 2 * number]:
                    unit.finish()

            pl.when(step == number)(sent)
        act_t[...] = act[...].T
        for n in range(3):
            at = slice(n * TILE, n * TILE + TILE)
            columns = pl.ds(aligned(step * WIDTH + n * TILE, 128), TILE)
            grad = dot_nn(norm_t[...], slope[:, at])
            wu[:, columns] = grad[:WIDTH].astype(BF16)
            early[pl.ds(4 + step, 1), at] = grad[WIDTH : WIDTH + 1]
            wd[here, at] = dot_nn(act_t[...], seed[:, at]).astype(BF16)
        after("grads", step, 4)
        return carry

    lax.fori_loop(0, 4, feed_forward, 0)

    def back_two(rows, carry):
        mid = middle[rows]
        slope[rows] = (mid + branch_scale * (outer[rows] + vectors[7:8])).astype(BF16)
        xhat, scale = standardized(mid)
        grad = grad_norm[rows]
        grad_middle = cotangent[rows].astype(F32) + back_through_norm(grad, xhat, scale, gain_two)
        middle[rows] = grad_middle
        grad_branch = (branch_scale * grad_middle).astype(BF16)
        seed[rows] = grad_branch
        parts = (column_sum(grad_branch.astype(F32)), column_sum(grad * xhat), column_sum(grad))
        return tuple(former + part for former, part in zip(carry, parts))

    zero = jnp.zeros((1, WIDTH), F32)
    early[0:1], early[1:2], early[2:3] = strips(back_two, (zero, zero, zero))
    out_copy = pltpu.make_async_copy(slope, layer_out, local_sems.at[0])
    out_copy.start()
    after("back")

    for n in range(3):
        at = slice(n * TILE, n * TILE + TILE)
        act[:, at] = dot_nt(seed[...], wo[at]).astype(BF16)
    after("attended")
    coming[5].finish()
    act_t[...] = attended[...].T
    for n in range(3):
        at = slice(n * TILE, n * TILE + TILE)
        wo[:, at] = dot_nn(act_t[...], seed[:, at]).astype(BF16)
    after("out")
    out_copy.wait()
    after("first")

    query_grad = norm_t.at[0:128]
    key_sum, value_sum = outer.at[:, 0:128], outer.at[:, 128:256]

    def backward_group(group, carry):
        def backward_pair(half, carry):
            pair = 2 * group + half
            for block in range(4):
                attend_back(
                    wide,
                    pair,
                    block,
                    query_side,
                    key_side,
                    causal,
                    attended,
                    act,
                    logsums,
                    query_grad,
                    key_sum,
                    value_sum,
                )
            first = pair * 384
            wide[:, pl.ds(aligned(first, 128), 128)] = query_grad[...].T
            wide[:, pl.ds(aligned(first + 128, 128), 128)] = key_sum[...].astype(BF16)
            wide[:, pl.ds(aligned(first + 256, 128), 128)] = value_sum[...].astype(BF16)
            after("pair_back", pair, PAIRS)
            return carry

        lax.fori_loop(0, 2, backward_pair, carry)
        for number in range(3):
            def weight_grads(number=number):
                rows = []
                for n in range(3):
                    at = slice(n * TILE, n * TILE + TILE)
                    columns = slice(number * WIDTH + n * TILE, number * WIDTH + n * TILE + TILE)
                    grad = dot_nn(first_t[...], wide[:, columns])
                    qkv_partials[number][:, at] = grad[:WIDTH].astype(BF16)
                    rows.append(grad[WIDTH : WIDTH + 1])
                row = jnp.concatenate(rows, axis=1)
                at = slice(number * 256, number * 256 + 256)
                late[2:3, at] = jnp.concatenate([row[:, 0:128], row[:, 384:512]], axis=1)
                late[3:4, at] = jnp.concatenate([row[:, 256:384], row[:, 640:768]], axis=1)
                after("qkv_grads" + str(number))

            pl.when(group == number)(weight_grads)
        return carry

    lax.fori_loop(0, 3, backward_group, 0)

    for n in range(3):
        at = slice(n * TILE, n * TILE + TILE)
        grad_norm[:, at] = dot_nt(wide[...], wq[at])
        after("tokens" + str(n))

    def back_one(rows, carry):
        xhat, scale = standardized(tokens[rows].astype(F32))
        grad = grad_norm[rows]
        middle[rows] += back_through_norm(grad, xhat, scale, gain_one)
        return carry[0] + column_sum(grad * xhat), carry[1] + column_sum(grad)

    late[0:1], late[1:2] = strips(back_one, (zero, zero))
    tokens_copy = pltpu.make_async_copy(middle, grad_tokens, local_sems.at[1])
    tokens_copy.start()
    after("half")
    up = up_target[...]
    up_out[...] = jnp.concatenate(
        [
            up[:, WIDTH * j + ROWS * d : WIDTH * j + ROWS * d + ROWS]
            for d in range(DEVICES)
            for j in range(HIDDEN_PARTS)
        ],
        axis=1,
    )
    back = lax.rem(DEVICES - place.number, DEVICES) * ROWS
    small_out[0:8] = pltpu.roll(early[...], back, 1)[:, 0:128]
    for unit in coming[:5] + leaving[:9]:
        unit.finish(1)
    after("last")
    small_out[8:12] = pltpu.roll(late[...], back, 1)[:, 0:128]
    small_out[12:16] = jnp.zeros((4, 128), F32)
    for unit in coming[:5] + leaving[:9]:
        unit.copy(unit.SEMS - 1).wait_send()
    for unit in leaving[9:]:
        unit.finish()
    tokens_copy.wait()


def layer(tokens, documents, cotangent, shards, packed):
    vmem = pl.BlockSpec(memory_space=pltpu.VMEM)
    anywhere = pl.BlockSpec(memory_space=pl.ANY)
    out_shape = [jax.ShapeDtypeStruct((TOKENS, WIDTH), BF16), jax.ShapeDtypeStruct((TOKENS, WIDTH), F32)]
    out_shape += [jax.ShapeDtypeStruct(SHARDS[n], F32) for n in NAMES]
    out_shape.append(jax.ShapeDtypeStruct((16, 128), F32))
    scratch = [
        pltpu.VMEM((WIDTH, QKV), BF16),
        pltpu.VMEM((WIDTH, WIDTH), BF16),
        pltpu.VMEM((WIDTH, HIDDEN), BF16),
        pltpu.VMEM((HIDDEN, WIDTH), BF16),
        pltpu.VMEM((TOKENS, WIDTH), BF16),
        pltpu.VMEM((TOKENS, WIDTH), BF16),
        pltpu.VMEM((TOKENS, QKV), BF16),
        pltpu.VMEM((TOKENS, WIDTH), BF16),
        pltpu.VMEM((WIDTH + 16, TOKENS), BF16),
        pltpu.VMEM((TOKENS, WIDTH), BF16),
        pltpu.VMEM((TOKENS, WIDTH), BF16),
        pltpu.VMEM((TOKENS, WIDTH), BF16),
        pltpu.VMEM((WIDTH, TOKENS), BF16),
        pltpu.VMEM((TOKENS, WIDTH), BF16),
        pltpu.VMEM((TOKENS, WIDTH), F32),
        pltpu.VMEM((TOKENS, WIDTH), F32),
        pltpu.VMEM((TOKENS, WIDTH), F32),
        pltpu.VMEM((HEADS, 1, TOKENS), F32),
        pltpu.VMEM((TOKENS, 128), BF16),
        pltpu.VMEM((TOKENS, 128), BF16),
        pltpu.VMEM((QUERY_ROWS, QUERY_ROWS), F32),
        pltpu.VMEM((16, WIDTH), F32),
        pltpu.VMEM((1, QKV), F32),
        pltpu.VMEM((1, QKV), F32),
        pltpu.VMEM((8, WIDTH), F32),
        pltpu.VMEM((4, WIDTH), F32),
        pltpu.VMEM(SHARDS["up"], BF16),
        pltpu.VMEM(SHARDS["up"], F32),
        pltpu.VMEM((WIDTH + 16, TOKENS), BF16),
    ]
    for unit in GATHER_UNITS:
        scratch += [pltpu.VMEM((32, unit[3]), BF16)] * 2
    for unit in SCATTER_UNITS:
        scratch += ScatterUnit.scratch(unit[3])
    scratch += [pltpu.SemaphoreType.DMA((len(GATHER_UNITS), GatherUnit.SEMS))] * 2
    scratch += [pltpu.SemaphoreType.DMA((len(SCATTER_UNITS), ScatterUnit.SEMS))] * 2
    for shape, dtype in (((16, WIDTH), BF16), ((8, WIDTH), F32), ((4, WIDTH), F32)):
        scratch += SmallSum.scratch(shape, dtype)
    scratch.append(pltpu.SemaphoreType.DMA((4,)))
    return pl.pallas_call(
        layer_kernel,
        name="layer",
        out_shape=out_shape,
        in_specs=[anywhere, vmem, anywhere] + [vmem] * 5,
        out_specs=[anywhere] * 2 + [vmem] * 5,
        scratch_shapes=scratch,
        compiler_params=pltpu.CompilerParams(collective_id=0, has_side_effects=True, vmem_limit_bytes=VMEM_LIMIT),
        cost_estimate=pl.CostEstimate(flops=50 * 10**9, bytes_accessed=30 * 10**6, transcendentals=20 * 10**6),
    )(tokens, documents, cotangent, *[shards[n] for n in NAMES], packed)


def results_kernel(*refs):
    sources, parts, targets, vectors = refs[:6], refs[6], refs[7:13], refs[13:22]
    held, (sems_in, sems_out) = refs[22:28], refs[28:]
    copies_in = [pltpu.make_async_copy(a, b, sems_in.at[i]) for i, (a, b) in enumerate(zip(sources, held))]
    copies_out = [pltpu.make_async_copy(a, b, sems_out.at[i]) for i, (a, b) in enumerate(zip(held, targets))]
    for copy in copies_in:
        copy.start()
    for target, row in zip(vectors, (8, 9, 10, 11, 0, 1, 2, 3)):
        target[...] = parts[row, 0:ROWS]
    vectors[8][...] = jnp.concatenate([parts[4 + j : 5 + j, 0:ROWS] for j in range(HIDDEN_PARTS)], axis=1)[0]
    for copy_in, copy_out in zip(copies_in, copies_out):
        copy_in.wait()
        copy_out.start()
    for copy in copies_out:
        copy.wait()


def results(arrays, parts):
    vmem = pl.BlockSpec(memory_space=pltpu.VMEM)
    anywhere = pl.BlockSpec(memory_space=pl.ANY)
    out_shape = [jax.ShapeDtypeStruct(a.shape, a.dtype) for a in arrays]
    out_shape += [jax.ShapeDtypeStruct((ROWS,), F32)] * 8 + [jax.ShapeDtypeStruct((ROWS * HIDDEN_PARTS,), F32)]
    scratch = [pltpu.VMEM(a.shape, a.dtype) for a in arrays]
    return pl.pallas_call(
        results_kernel,
        name="results",
        out_shape=out_shape,
        in_specs=[anywhere] * 6 + [vmem],
        out_specs=[anywhere] * 6 + [vmem] * 9,
        scratch_shapes=scratch + [pltpu.SemaphoreType.DMA((6,))] * 2,
        compiler_params=pltpu.CompilerParams(vmem_limit_bytes=VMEM_LIMIT),
    )(*arrays, parts)


def fused_device(
    tokens,
    doc_ids,
    cotangent,
    first_gain,
    first_offset,
    qkv_weight,
    query_bias,
    value_bias,
    out_weight,
    out_bias,
    second_gain,
    second_offset,
    up_weight,
    up_bias,
    down_weight,
    down_bias,
):
    shards = {"qkv": qkv_weight, "out": out_weight, "up": up_weight, "down": down_weight}
    vectors = (
        first_gain,
        first_offset,
        query_bias,
        value_bias,
        out_bias,
        second_gain,
        second_offset,
        down_bias,
        up_bias,
        jnp.zeros((96,), BF16),
    )
    packed = jnp.concatenate(vectors).astype(F32)[None]
    *arrays, parts = layer(tokens, doc_ids, cotangent, shards, packed)
    layer_out, grad_tokens, grad_qkv, grad_out, grad_up, grad_down, *small = results(arrays, parts)
    return (
        layer_out,
        grad_tokens,
        small[0],
        small[1],
        grad_qkv,
        small[2],
        small[3],
        grad_out,
        small[4],
        small[5],
        small[6],
        grad_up,
        small[8],
        grad_down,
        small[7],
    )


def solution(mesh):
    placed = (
        P(("dp", "fsdp"), None),
        P(("dp", "fsdp"), None),
        P(("dp", "fsdp"), None),
        P(("dp", "fsdp")),
        P(("dp", "fsdp")),
        P(("dp", "fsdp"), None),
        P(("dp", "fsdp")),
        P(("dp", "fsdp")),
        P(("dp", "fsdp"), None),
        P(("dp", "fsdp")),
        P(("dp", "fsdp")),
        P(("dp", "fsdp")),
        P(("dp", "fsdp"), None),
        P(("dp", "fsdp")),
        P(("dp", "fsdp"), None),
        P(("dp", "fsdp")),
    )
    return jax.shard_map(
        fused_device if fits(mesh) else plain_device,
        mesh=mesh,
        in_specs=placed,
        out_specs=(
            P(("dp", "fsdp"), None),
            P(("dp", "fsdp"), None),
            P(("dp", "fsdp")),
            P(("dp", "fsdp")),
            P(("dp", "fsdp"), None),
            P(("dp", "fsdp")),
            P(("dp", "fsdp")),
            P(("dp", "fsdp"), None),
            P(("dp", "fsdp")),
            P(("dp", "fsdp")),
            P(("dp", "fsdp")),
            P(("dp", "fsdp"), None),
            P(("dp", "fsdp")),
            P(("dp", "fsdp"), None),
            P(("dp", "fsdp")),
        ),
        check_vma=False,
    )
```
